32 devices in a mesh: energy: 8 (over y, x, core), mom: 4 (over z).
Axes of the slice: x: 2, y: 2, z: 4, core: 2. Of those that a mesh axis runs over, the one named last changes fastest.
Arguments:
- green: bfloat16 [4, 8, 4, 2, 256, 256], P('mom', 'energy'), may hold values from -6 to 6
- coupling: bfloat16 [2, 256, 256], replicated, may hold values from -0.375 to 0.375
- phonon: bfloat16 [3, 1024, 256], replicated, may hold values from -4 to 4
- shift: int32 [3, 2], replicated, may hold values from 0 to 1
Outputs:
- sigma: bfloat16 [4, 8, 4, 2, 256, 256], P('mom', 'energy')
The draws below stay inside these ranges and needn't reach their ends.
All inputs are finite; a program needn't handle non-finite values.
Results may differ from the reference program's by a relative error of at most 0.0049.
Values may be sent and summed in bfloat16 or wider, within the bound.
No kernel may reach another device: no remote copies, remote signals or barrier semaphores. Data moves between devices by JAX's collectives and lax.ppermute only.
A program may use at most 64 MiB of HBM per device.

```python
import jax
import jax.numpy as jnp
from jax import lax

NO = 256
MODES = 2
QR = 1
SMAX = 1
E_OUT = 4
NOFF = 3
NK = 4
NG = 8


def draw_shift(key, part):
    first_key, second_key = jax.random.split(jax.random.fold_in(key, 11))
    values_flat = jax.random.randint(first_key, (NOFF * MODES,), 0, SMAX + 1, dtype=jnp.int32)
    placing = jax.random.permutation(second_key, NOFF * MODES)
    values_flat = values_flat.at[placing[0]].set(SMAX).at[placing[1]].set(0)
    return values_flat.reshape(NOFF, MODES)


def steps_of(own_key, shape, shards, low, high):
    level, own = 1.0, jax.random.fold_in(own_key, 6)
    for dim, blocks in shards:
        steps = jnp.exp(jax.random.uniform(jax.random.fold_in(own, dim), (blocks,), jnp.float32, low / len(shards), high / len(shards)))
        level = level * jnp.repeat(steps, shape[dim] // blocks).reshape([-1 if axis == dim else 1 for axis in range(len(shape))])
    return level


def normal_values(rng, shape, deviation, limit, shards=(), kind=jnp.bfloat16):
    drawn = jax.random.normal(rng, shape, jnp.float32) * deviation
    if len(shards) > 0:
        drawn = steps_of(rng, shape, shards, -0.22, 0.18) * drawn
    return jnp.clip(drawn, min=-limit, max=limit).astype(kind)


def setup_inputs(seed: int = 0) -> dict:
    streams_of = jax.random.split(jax.random.key(seed), 5)
    green = normal_values(streams_of[0], (NK, NG, E_OUT, 2, NO, NO), 1.0, 6.0, ((0, 4), (1, 8)))
    coupling = normal_values(streams_of[1], (MODES, NO, NO), NO ** -0.5, 0.375)
    phonon = normal_values(streams_of[2], (NOFF, MODES * 2 * NO, NO), 0.5, 4.0)
    shift = draw_shift(jax.random.fold_in(streams_of[4], 71), 0)
    return dict(green=green, coupling=coupling, phonon=phonon, shift=shift)


def reference(green, coupling, phonon, shift):
    points = green.shape[0]
    groups = green.shape[1]
    couple = coupling.astype(jnp.float32)

    def one_point(momentum):
        accumulated = jnp.zeros((groups, E_OUT, 2, NO, NO), jnp.float32)
        for offset in range(2 * QR + 1):
            source = ((momentum - (offset - QR)) % points).astype(jnp.int32)
            blocks = lax.dynamic_index_in_dim(green, source, 0, keepdims=False)
            flat = blocks.reshape(groups * E_OUT, 2, NO, NO)
            padded = jnp.concatenate([jnp.zeros((SMAX, 2, NO, NO), flat.dtype), flat], axis=0)
            weights = phonon[offset].astype(jnp.float32).reshape(MODES, 2, NO, NO)
            for mode_index in range(MODES):
                first_slot = (SMAX - shift[offset, mode_index]).astype(jnp.int32)
                window = lax.dynamic_slice_in_dim(padded, first_slot, groups * E_OUT, 0)
                window = window.reshape(groups, E_OUT, 2, NO, NO).astype(jnp.float32)
                left_product = jnp.einsum('xy,gecyz->gecxz', couple[mode_index], window).astype(jnp.bfloat16)
                left_product = lax.optimization_barrier(left_product).astype(jnp.float32)
                product = jnp.einsum('gecxy,yz->gecxz', left_product, couple[mode_index])
                real_part = product[:, :, 0] * weights[mode_index, 0] - product[:, :, 1] * weights[mode_index, 1]
                imag_part = product[:, :, 0] * weights[mode_index, 1] + product[:, :, 1] * weights[mode_index, 0]
                accumulated = accumulated + jnp.stack([real_part, imag_part], axis=2)
        return accumulated.astype(jnp.bfloat16)

    return lax.map(one_point, jnp.arange(points, dtype=jnp.int32))
```

```python
import jax
import jax.numpy as jnp
from jax import lax
from jax.experimental import pallas as pl
from jax.experimental.pallas import tpu as pltpu
from jax.sharding import PartitionSpec as P

SMAX = 1


def passed_along(x, axis, by):
    length = lax.axis_size(axis)
    pairs = [(i, i + by) for i in range(length) if 0 <= i + by < length]
    return lax.ppermute(x, axis, pairs)


def passed_round(x, axis, by):
    length = lax.axis_size(axis)
    return lax.ppermute(x, axis, [(i, (i + by) % length) for i in range(length)])


def product(block, coupling):
    left = [
        jnp.dot(coupling, block[c], preferred_element_type=jnp.float32).astype(jnp.bfloat16)
        for c in range(2)
    ]
    return [jnp.dot(l, coupling, preferred_element_type=jnp.float32) for l in left]


def add_term(total, slot, parts, real, imag):
    total[slot, 0] += parts[0] * real - parts[1] * imag
    total[slot, 1] += parts[0] * imag + parts[1] * real


def weights_of(phonon, mode, size):
    rows = pl.ds(2 * mode * size, size)
    more = pl.ds((2 * mode + 1) * size, size)
    return phonon[rows, :].astype(jnp.float32), phonon[more, :].astype(jnp.float32)


def terms(shift, coupling, phonon, offset, inner, first, edge, total):
    modes, size, _ = coupling.shape
    top = total.shape[0] - 1
    for mode in range(modes):
        step = shift[offset, mode]
        real, imag = weights_of(phonon, mode, size)
        if edge is not None:
            own, below = edge
            blocks = [jnp.where(step > 0, below[0, c], own[c]) for c in range(2)]
            add_term(total, jnp.where(step > 0, 0, top), product(blocks, coupling[mode]), real, imag)
        if inner is not None:
            for l in range(inner.shape[0]):
                blocks = [inner[l, c] for c in range(2)]
                add_term(total, first + l + step, product(blocks, coupling[mode]), real, imag)


def own_kernel(offset, shift, coupling, phonon, own, below, total):
    total[...] = jnp.zeros_like(total)
    top = own.shape[0] - 1
    terms(shift, coupling, phonon, offset, own.at[pl.ds(0, top)], 0, (own.at[top], below), total)


def more_kernel(plan, *refs):
    shift, coupling, phonons = refs[0], refs[1], refs[2]
    refs = refs[3:]
    total_in, total = refs[-2], refs[-1]
    total[...] = total_in[...]
    at = 0
    for offset, first, has_edge in plan:
        if has_edge:
            terms(shift, coupling, phonons.at[offset], offset, None, 0, (refs[at].at[0], refs[at + 1]), total)
            at += 2
        else:
            terms(shift, coupling, phonons.at[offset], offset, refs[at], first, None, total)
            at += 1


def last_kernel(offset, shift, coupling, phonons, block, total_in, out, total):
    total[...] = total_in[...]
    terms(shift, coupling, phonons.at[offset], offset, block, 0, None, total)
    out[...] = total[...].astype(out.dtype)


def call(kernel, out_shape, args, products, scratch=(), aliases=None):
    size = args[1].shape[-1]
    return pl.pallas_call(
        kernel,
        out_shape=out_shape,
        in_specs=[pl.BlockSpec(memory_space=pltpu.SMEM)]
        + [pl.BlockSpec(memory_space=pltpu.VMEM)] * (len(args) - 1),
        out_specs=pl.BlockSpec(memory_space=pltpu.VMEM),
        scratch_shapes=list(scratch),
        input_output_aliases=aliases or {},
        compiler_params=pltpu.CompilerParams(vmem_limit_bytes=32 * 1024 * 1024),
        cost_estimate=pl.CostEstimate(
            flops=products * 4 * size**3, bytes_accessed=1 << 20, transcendentals=0
        ),
    )(*args)


def body(green, coupling, phonon, shift):
    own = green[0, 0]
    energies, _, size, _ = own.shape
    modes = coupling.shape[0]
    offsets = phonon.shape[0]
    radius = (offsets - 1) // 2
    top = own[energies - SMAX :]
    rest = own[: energies - SMAX]
    mid = own[1 : energies - SMAX]
    low = own[:1]
    f32_total = jax.ShapeDtypeStruct(own.shape, jnp.float32)

    ups = [q for q in range(1, radius + 1)]
    downs = [-q for q in ups]
    moved = ups + downs
    tops = {q: passed_round(top, "mom", q) for q in moved}
    below = passed_along(top, "energy", 1)
    rests = {}
    for q in moved[:-1]:
        rests[q] = passed_round(rest, "mom", q)
    last = moved[-1]
    last_mid = passed_round(mid, "mom", last)
    last_low = passed_round(low, "mom", last)
    belows = {q: passed_along(tops[q], "energy", 1) for q in moved}

    def own_part(shift_ref, coupling_ref, phonon_ref, own_ref, below_ref, total_ref):
        own_kernel(radius, shift_ref, coupling_ref, phonon_ref.at[radius], own_ref, below_ref, total_ref)

    total = call(own_part, f32_total, (shift, coupling, phonon, own, below), 2 * modes * energies)

    def more(plan, blocks, total, products):
        args = (shift, coupling, phonon, *blocks, total)

        def kernel(*refs):
            more_kernel(plan, *refs)

        return call(kernel, f32_total, args, products, aliases={len(args) - 1: 0})

    plan, blocks = [], []
    for q in moved:
        plan.append((q + radius, 0, True))
        blocks += [tops[q], belows[q]]
    total = more(plan, blocks, total, 2 * modes * len(moved))
    for q in moved[:-1]:
        total = more([(q + radius, 0, False)], [rests[q]], total, 2 * modes * rest.shape[0])
    total = more([(last + radius, 1, False)], [last_mid], total, 2 * modes * mid.shape[0])

    def finish(*refs):
        last_kernel(last + radius, *refs)

    out = call(
        finish,
        jax.ShapeDtypeStruct(own.shape, jnp.bfloat16),
        (shift, coupling, phonon, last_low, total),
        2 * modes,
        scratch=[pltpu.VMEM(own.shape, jnp.float32)],
    )
    return out[None, None]


def solution(mesh):
    placed = (P("mom", "energy", None, None, None, None), P(), P(), P())
    return jax.shard_map(
        body,
        mesh=mesh,
        in_specs=placed,
        out_specs=P("mom", "energy", None, None, None, None),
        check_vma=False,
    )
```

```python
import jax
import jax.numpy as jnp
from jax import lax
from jax.experimental import pallas as pl
from jax.experimental.pallas import tpu as pltpu
from jax.sharding import PartitionSpec as P

SMAX = 1
VMEM = pl.BlockSpec(memory_space=pltpu.VMEM)
SMEM = pl.BlockSpec(memory_space=pltpu.SMEM)


def passed_along(x, axis, by):
    length = lax.axis_size(axis)
    pairs = [(i, i + by) for i in range(length) if 0 <= i + by < length]
    return lax.ppermute(x, axis, pairs)


def passed_round(x, axis, by):
    length = lax.axis_size(axis)
    return lax.ppermute(x, axis, [(i, (i + by) % length) for i in range(length)])


def after(args, result):
    shift, coupling, phonon, own = args
    own, _ = lax.optimization_barrier((own, result))
    return (shift, coupling, phonon, own)


def products(blocks, coupling):
    lefts = [
        jnp.dot(coupling, block, preferred_element_type=jnp.float32).astype(jnp.bfloat16)
        for block in blocks
    ]
    return [jnp.dot(left, coupling, preferred_element_type=jnp.float32) for left in lefts]


def one_energy(energy, offset, shift, coupling, phonon, own, below):
    modes, size, _ = coupling.shape
    real_sum, imag_sum = None, None
    for mode in range(modes):
        step = shift[offset, mode]
        if energy == 0:
            blocks = [jnp.where(step > 0, below[0, c], own[0, c]) for c in range(2)]
        else:
            blocks = [own[energy - step, c] for c in range(2)]
        first, second = products(blocks, coupling[mode])
        real = phonon[offset, pl.ds(2 * mode * size, size), :].astype(jnp.float32)
        imag = phonon[offset, pl.ds((2 * mode + 1) * size, size), :].astype(jnp.float32)
        real_term = first * real - second * imag
        imag_term = first * imag + second * real
        real_sum = real_term if real_sum is None else real_sum + real_term
        imag_sum = imag_term if imag_sum is None else imag_sum + imag_term
    return real_sum, imag_sum


def partial_kernel(offset, energies, with_top, shift, coupling, phonon, own, *rest):
    rest = list(rest)
    below = rest.pop(0) if energies[0] == 0 else None
    out = rest.pop(0)
    for at, energy in enumerate(energies):
        real, imag = one_energy(energy, offset, shift, coupling, phonon, own, below)
        out[at, 0] = real.astype(out.dtype)
        out[at, 1] = imag.astype(out.dtype)
    if with_top:
        rest[0][0] = own[own.shape[0] - 1]


def partial_call(offset, energies, args, dtype, with_top=False):
    _, parts, size, _ = args[3].shape
    shapes = [jax.ShapeDtypeStruct((len(energies), parts, size, size), dtype)]
    if with_top:
        shapes.append(jax.ShapeDtypeStruct((1, parts, size, size), args[3].dtype))

    def kernel(*refs):
        partial_kernel(offset, energies, with_top, *refs)

    flops = len(energies) * args[1].shape[0] * 8 * size**3
    return pl.pallas_call(
        kernel,
        out_shape=shapes,
        in_specs=[SMEM] + [VMEM] * (len(args) - 1),
        out_specs=[VMEM] * len(shapes),
        compiler_params=pltpu.CompilerParams(vmem_limit_bytes=32 * 1024 * 1024),
        cost_estimate=pl.CostEstimate(flops=flops * 16, bytes_accessed=1 << 24, transcendentals=0),
    )(*args)


def finish_call(first, whole, own_sum, pieces, out=None):
    count, parts, size, _ = own_sum.shape

    def kernel(own_ref, *refs):
        at = pl.program_id(0)
        total = own_ref[at]
        for piece in refs[: len(pieces)]:
            total = total + piece[at].astype(jnp.float32)
        refs[-1][0] = total.astype(jnp.bfloat16)

    args = [own_sum, *pieces]
    specs = [VMEM] * len(args)
    aliases = {}
    if out is not None:
        aliases = {len(args): 0}
        args.append(out)
        specs.append(pl.BlockSpec(memory_space=pl.ANY))
    return pl.pallas_call(
        kernel,
        grid=(count,),
        out_shape=jax.ShapeDtypeStruct(whole, jnp.bfloat16),
        in_specs=specs,
        out_specs=pl.BlockSpec((1, parts, size, size), lambda i: (i + first, 0, 0, 0)),
        input_output_aliases=aliases,
        compiler_params=pltpu.CompilerParams(vmem_limit_bytes=32 * 1024 * 1024),
        cost_estimate=pl.CostEstimate(flops=1 << 20, bytes_accessed=1 << 20, transcendentals=0),
    )(*args)


def body(green, coupling, phonon, shift):
    own = green[0, 0]
    energies = own.shape[0]
    offsets = phonon.shape[0]
    radius = (offsets - 1) // 2
    moved = [q for r in range(1, radius + 1) for q in (r, -r)]
    args = (shift, coupling, phonon, own)
    top, middle = (energies - 1,), tuple(range(SMAX, energies - 1))
    bottom = tuple(range(SMAX))

    arrived = {}
    own_top = None
    for q in moved:
        results = partial_call(q + radius, top, args, jnp.bfloat16, with_top=own_top is None)
        if own_top is None:
            own_top = results[1]
        args = after(args, results[0])
        arrived[q, top] = passed_round(results[0], "mom", q)
    below = passed_along(own_top, "energy", 1)
    for q in moved:
        part = partial_call(q + radius, middle, args, jnp.bfloat16)[0]
        args = after(args, part)
        arrived[q, middle] = passed_round(part, "mom", q)
    for q in moved:
        part = partial_call(q + radius, bottom, args + (below,), jnp.bfloat16)[0]
        args = after(args, part)
        arrived[q, bottom] = passed_round(part, "mom", q)
    own_sums = {
        group: partial_call(
            radius, group, args + ((below,) if group == bottom else ()), jnp.float32
        )[0]
        for group in (top, middle, bottom)
    }
    out = None
    for group in (top, middle, bottom):
        out = finish_call(group[0], own.shape, own_sums[group], [arrived[q, group] for q in moved], out)
    return out[None, None]


def solution(mesh):
    placed = (P("mom", "energy", None, None, None, None), P(), P(), P())
    return jax.shard_map(
        body,
        mesh=mesh,
        in_specs=placed,
        out_specs=P("mom", "energy", None, None, None, None),
        check_vma=False,
    )
```

```python
import jax
import jax.numpy as jnp
from jax import lax
from jax.experimental import pallas as pl
from jax.experimental.pallas import tpu as pltpu
from jax.sharding import PartitionSpec as P

SMAX = 1
HBM = pl.BlockSpec(memory_space=pltpu.HBM)
VMEM = pl.BlockSpec(memory_space=pltpu.VMEM)
SMEM = pl.BlockSpec(memory_space=pltpu.SMEM)


def passed_along(x, axis, by):
    length = lax.axis_size(axis)
    pairs = [(i, i + by) for i in range(length) if 0 <= i + by < length]
    return lax.ppermute(x, axis, pairs)


def passed_round(x, axis, by):
    length = lax.axis_size(axis)
    return lax.ppermute(x, axis, [(i, (i + by) % length) for i in range(length)])


def after(args, result):
    shift, coupling, phonon, own = args
    own, _ = lax.optimization_barrier((own, result))
    return (shift, coupling, phonon, own)


def products(blocks, coupling):
    lefts = [
        jnp.dot(coupling, block, preferred_element_type=jnp.float32).astype(jnp.bfloat16)
        for block in blocks
    ]
    return [jnp.dot(left, coupling, preferred_element_type=jnp.float32) for left in lefts]


def one_energy(energy, offset, shift, coupling, phonon, own, below, row=None):
    row = offset if row is None else row
    modes, size, _ = coupling.shape
    real_sum, imag_sum = None, None
    for mode in range(modes):
        step = shift[mode, offset]
        if energy == 0:
            blocks = [jnp.where(step > 0, below[0, c], own[0, c]) for c in range(2)]
        else:
            blocks = [own[energy - step, c] for c in range(2)]
        first, second = products(blocks, coupling[mode])
        real = phonon[row, pl.ds(2 * mode * size, size), :].astype(jnp.float32)
        imag = phonon[row, pl.ds((2 * mode + 1) * size, size), :].astype(jnp.float32)
        real_term = first * real - second * imag
        imag_term = first * imag + second * real
        real_sum = real_term if real_sum is None else real_sum + real_term
        imag_sum = imag_term if imag_sum is None else imag_sum + imag_term
    return real_sum, imag_sum


def partial_kernel(offset, energies, with_top, shift, coupling, phonon, own, *rest):
    rest = list(rest)
    below = rest.pop(0) if energies[0] == 0 else None
    out = rest.pop(0)
    for at, energy in enumerate(energies):
        real, imag = one_energy(energy, offset, shift, coupling, phonon, own, below)
        out[at, 0] = real.astype(out.dtype)
        out[at, 1] = imag.astype(out.dtype)
    if with_top:
        rest[0][0] = own[own.shape[0] - 1]


def early_kernel(offset, with_top, shift, coupling_hbm, phonon_hbm, own_hbm, *rest):
    coupling, phonon, own, sems = rest[-4:]
    out = rest[0]
    used = pl.ds(own_hbm.shape[0] - 1 - SMAX, 1 + SMAX)
    pairs = [(coupling_hbm, coupling), (own_hbm.at[used], own)]
    pairs += [(phonon_hbm.at[pl.ds(offset, 1)], phonon)]
    copies = [pltpu.make_async_copy(*pair, sems.at[n]) for n, pair in enumerate(pairs)]
    for copy in copies:
        copy.start()
    for copy in copies:
        copy.wait()
    real, imag = one_energy(SMAX, offset, shift, coupling, phonon, own, None, 0)
    out[0, 0] = real.astype(out.dtype)
    out[0, 1] = imag.astype(out.dtype)
    if with_top:
        rest[1][0] = own[SMAX]


def early_call(offset, args, with_top=False):
    shift, coupling, phonon, own = args
    _, parts, size, _ = own.shape

    def kernel(*refs):
        early_kernel(offset, with_top, *refs)

    shapes = [jax.ShapeDtypeStruct((1, parts, size, size), jnp.bfloat16)] * (2 if with_top else 1)
    return pl.pallas_call(
        kernel,
        out_shape=shapes,
        in_specs=[SMEM, HBM, HBM, HBM],
        out_specs=[VMEM] * len(shapes),
        scratch_shapes=[
            pltpu.VMEM(coupling.shape, coupling.dtype),
            pltpu.VMEM((1,) + phonon.shape[1:], phonon.dtype),
            pltpu.VMEM((1 + SMAX,) + own.shape[1:], own.dtype),
            pltpu.SemaphoreType.DMA((3,)),
        ],
        compiler_params=pltpu.CompilerParams(vmem_limit_bytes=60 * 1024 * 1024),
        cost_estimate=estimate(coupling, 1),
    )(*args)


def estimate(coupling, energies):
    modes, size, _ = coupling.shape
    flops = 128 * energies * modes * size**3
    return pl.CostEstimate(flops=flops, bytes_accessed=1 << 24, transcendentals=0)


def partial_call(offset, energies, args, dtype, with_top=False):
    _, parts, size, _ = args[3].shape
    shapes = [jax.ShapeDtypeStruct((len(energies), parts, size, size), dtype)]
    if with_top:
        shapes.append(jax.ShapeDtypeStruct((1, parts, size, size), args[3].dtype))

    def kernel(*refs):
        partial_kernel(offset, energies, with_top, *refs)

    return pl.pallas_call(
        kernel,
        out_shape=shapes,
        in_specs=[SMEM] + [VMEM] * (len(args) - 1),
        out_specs=[VMEM] * len(shapes),
        compiler_params=pltpu.CompilerParams(vmem_limit_bytes=32 * 1024 * 1024),
        cost_estimate=estimate(args[1], len(energies)),
    )(*args)


def finish_call(first, whole, own_sum, pieces, out=None):
    count, parts, size, _ = own_sum.shape

    def kernel(own_ref, *refs):
        at = pl.program_id(0)
        total = own_ref[at]
        for piece in refs[: len(pieces)]:
            total = total + piece[at].astype(jnp.float32)
        refs[-1][0] = total.astype(jnp.bfloat16)

    args = [own_sum, *pieces]
    specs = [VMEM] * len(args)
    aliases = {}
    if out is not None:
        aliases = {len(args): 0}
        args.append(out)
        specs.append(pl.BlockSpec(memory_space=pl.ANY))
    return pl.pallas_call(
        kernel,
        grid=(count,),
        out_shape=jax.ShapeDtypeStruct(whole, jnp.bfloat16),
        in_specs=specs,
        out_specs=pl.BlockSpec((1, parts, size, size), lambda i: (i + first, 0, 0, 0)),
        input_output_aliases=aliases,
        compiler_params=pltpu.CompilerParams(vmem_limit_bytes=32 * 1024 * 1024),
        cost_estimate=pl.CostEstimate(flops=1 << 20, bytes_accessed=1 << 20, transcendentals=0),
    )(*args)


def body(green, coupling, phonon, shift):
    own = green[0, 0]
    energies = own.shape[0]
    offsets = phonon.shape[0]
    radius = (offsets - 1) // 2
    moved = [q for r in range(1, radius + 1) for q in (r, -r)]
    args = (shift.T, coupling, phonon, own)
    top, middle = (energies - 1,), tuple(range(SMAX, energies - 1))
    bottom = tuple(range(SMAX))

    arrived = {}
    for q in moved:
        results = early_call(q + radius, args, with_top=q == moved[1])
        if q == moved[1]:
            own_top = results[1]
        args = after(args, results[0])
        arrived[q, top] = passed_round(results[0], "mom", q)
    below = passed_along(own_top, "energy", 1)
    for q in moved:
        part = partial_call(q + radius, middle, args, jnp.bfloat16)[0]
        args = after(args, part)
        arrived[q, middle] = passed_round(part, "mom", q)
    for q in moved:
        part = partial_call(q + radius, bottom, args + (below,), jnp.bfloat16)[0]
        args = after(args, part)
        arrived[q, bottom] = passed_round(part, "mom", q)
    own_sums = {
        group: partial_call(
            radius, group, args + ((below,) if group == bottom else ()), jnp.float32
        )[0]
        for group in (top, middle, bottom)
    }
    out = None
    for group in (top, middle, bottom):
        out = finish_call(group[0], own.shape, own_sums[group], [arrived[q, group] for q in moved], out)
    return out[None, None]


def solution(mesh):
    placed = (P("mom", "energy", None, None, None, None), P(), P(), P())
    return jax.shard_map(
        body,
        mesh=mesh,
        in_specs=placed,
        out_specs=P("mom", "energy", None, None, None, None),
        check_vma=False,
    )
```

```python
import jax
import jax.numpy as jnp
from jax import lax
from jax.experimental import pallas as pl
from jax.experimental.pallas import tpu as pltpu
from jax.sharding import PartitionSpec as P

SMAX = 1
HBM = pl.BlockSpec(memory_space=pltpu.HBM)
VMEM = pl.BlockSpec(memory_space=pltpu.VMEM)
SMEM = pl.BlockSpec(memory_space=pltpu.SMEM)


def passed_along(x, axis, by):
    length = lax.axis_size(axis)
    pairs = [(i, i + by) for i in range(length) if 0 <= i + by < length]
    return lax.ppermute(x, axis, pairs)


def passed_round(x, axis, by):
    length = lax.axis_size(axis)
    return lax.ppermute(x, axis, [(i, (i + by) % length) for i in range(length)])


def after(args, result):
    shift, coupling, phonon, own = args
    own, _ = lax.optimization_barrier((own, result))
    return (shift, coupling, phonon, own)


def products(blocks, coupling):
    lefts = [
        jnp.dot(coupling, block, preferred_element_type=jnp.float32).astype(jnp.bfloat16)
        for block in blocks
    ]
    return [jnp.dot(left, coupling, preferred_element_type=jnp.float32) for left in lefts]


def energy_products(energy, offset, shift, coupling, own, below):
    found = []
    for mode in range(coupling.shape[0]):
        step = shift[mode, offset]
        if energy == 0:
            blocks = [jnp.where(step > 0, below[0, c], own[0, c]) for c in range(2)]
        else:
            blocks = [own[energy - step, c] for c in range(2)]
        found.append(products(blocks, coupling[mode]))
    return found


def weighted(found, row, phonon):
    real_sum, imag_sum = None, None
    for mode, (first, second) in enumerate(found):
        size = first.shape[0]
        real = phonon[row, pl.ds(2 * mode * size, size), :].astype(jnp.float32)
        imag = phonon[row, pl.ds((2 * mode + 1) * size, size), :].astype(jnp.float32)
        real_term = first * real - second * imag
        imag_term = first * imag + second * real
        real_sum = real_term if real_sum is None else real_sum + real_term
        imag_sum = imag_term if imag_sum is None else imag_sum + imag_term
    return real_sum, imag_sum


def partial_kernel(offset, energies, with_top, shift, coupling, phonon, own, *rest):
    rest = list(rest)
    below = rest.pop(0) if energies[0] == 0 else None
    out = rest.pop(0)
    for at, energy in enumerate(energies):
        found = energy_products(energy, offset, shift, coupling, own, below)
        real, imag = weighted(found, offset, phonon)
        out[at, 0] = real.astype(out.dtype)
        out[at, 1] = imag.astype(out.dtype)
    if with_top:
        rest[0][0] = own[own.shape[0] - 1]


def early_kernel(offset, shift_hbm, coupling_hbm, phonon_hbm, own_hbm, out, *scratch):
    shift, coupling, phonon, own, sems = scratch
    used = pl.ds(own_hbm.shape[0] - 1 - SMAX, 1 + SMAX)
    pairs = [(shift_hbm, shift), (coupling_hbm, coupling), (own_hbm.at[used], own)]
    pairs += [(phonon_hbm.at[pl.ds(offset, 1)], phonon)]
    copies = [pltpu.make_async_copy(*pair, sems.at[n]) for n, pair in enumerate(pairs)]
    for copy in copies:
        copy.start()
    for copy in copies[:3]:
        copy.wait()
    found = energy_products(SMAX, offset, shift, coupling, own, None)
    copies[3].wait()
    real, imag = weighted(found, 0, phonon)
    out[0, 0] = real.astype(out.dtype)
    out[0, 1] = imag.astype(out.dtype)


def early_call(offset, args):
    shift, coupling, phonon, own = args
    _, parts, size, _ = own.shape

    def kernel(*refs):
        early_kernel(offset, *refs)

    return pl.pallas_call(
        kernel,
        out_shape=jax.ShapeDtypeStruct((1, parts, size, size), jnp.bfloat16),
        in_specs=[HBM] * 4,
        out_specs=VMEM,
        scratch_shapes=[
            pltpu.SMEM(shift.shape, shift.dtype),
            pltpu.VMEM(coupling.shape, coupling.dtype),
            pltpu.VMEM((1,) + phonon.shape[1:], phonon.dtype),
            pltpu.VMEM((1 + SMAX,) + own.shape[1:], own.dtype),
            pltpu.SemaphoreType.DMA((4,)),
        ],
        compiler_params=pltpu.CompilerParams(vmem_limit_bytes=60 * 1024 * 1024),
        cost_estimate=estimate(coupling, 1),
    )(*args)


def estimate(coupling, energies):
    modes, size, _ = coupling.shape
    flops = 128 * energies * modes * size**3
    return pl.CostEstimate(flops=flops, bytes_accessed=1 << 24, transcendentals=0)


def partial_call(offset, energies, args, dtype, with_top=False):
    _, parts, size, _ = args[3].shape
    shapes = [jax.ShapeDtypeStruct((len(energies), parts, size, size), dtype)]
    if with_top:
        shapes.append(jax.ShapeDtypeStruct((1, parts, size, size), args[3].dtype))

    def kernel(*refs):
        partial_kernel(offset, energies, with_top, *refs)

    return pl.pallas_call(
        kernel,
        out_shape=shapes,
        in_specs=[SMEM] + [VMEM] * (len(args) - 1),
        out_specs=[VMEM] * len(shapes),
        compiler_params=pltpu.CompilerParams(vmem_limit_bytes=32 * 1024 * 1024),
        cost_estimate=estimate(args[1], len(energies)),
    )(*args)


def finish_call(first, whole, own_sum, pieces, out=None):
    count, parts, size, _ = own_sum.shape

    def kernel(own_ref, *refs):
        at = pl.program_id(0)
        total = own_ref[at]
        for piece in refs[: len(pieces)]:
            total = total + piece[at].astype(jnp.float32)
        refs[-1][0] = total.astype(jnp.bfloat16)

    args = [own_sum, *pieces]
    specs = [VMEM] * len(args)
    aliases = {}
    if out is not None:
        aliases = {len(args): 0}
        args.append(out)
        specs.append(pl.BlockSpec(memory_space=pl.ANY))
    return pl.pallas_call(
        kernel,
        grid=(count,),
        out_shape=jax.ShapeDtypeStruct(whole, jnp.bfloat16),
        in_specs=specs,
        out_specs=pl.BlockSpec((1, parts, size, size), lambda i: (i + first, 0, 0, 0)),
        input_output_aliases=aliases,
        compiler_params=pltpu.CompilerParams(vmem_limit_bytes=32 * 1024 * 1024),
        cost_estimate=pl.CostEstimate(flops=1 << 20, bytes_accessed=1 << 20, transcendentals=0),
    )(*args)


def body(green, coupling, phonon, shift):
    own = green[0, 0]
    energies = own.shape[0]
    offsets = phonon.shape[0]
    radius = (offsets - 1) // 2
    moved = [q for r in range(1, radius + 1) for q in (r, -r)]
    args = (shift.T, coupling, phonon, own)
    top, middle = (energies - 1,), tuple(range(SMAX, energies - 1))
    bottom = tuple(range(SMAX))

    arrived = {}
    for q in moved:
        part = early_call(q + radius, args)
        args = after(args, part)
        arrived[q, top] = passed_round(part, "mom", q)
    for q in moved:
        results = partial_call(q + radius, middle, args, jnp.bfloat16, with_top=q == moved[-1])
        if q == moved[-1]:
            below = passed_along(results[1], "energy", 1)
        args = after(args, results[0])
        arrived[q, middle] = passed_round(results[0], "mom", q)
    for q in moved:
        part = partial_call(q + radius, bottom, args + (below,), jnp.bfloat16)[0]
        args = after(args, part)
        arrived[q, bottom] = passed_round(part, "mom", q)
    own_sums = {
        group: partial_call(
            radius, group, args + ((below,) if group == bottom else ()), jnp.float32
        )[0]
        for group in (top, middle, bottom)
    }
    out = None
    for group in (top, middle, bottom):
        out = finish_call(group[0], own.shape, own_sums[group], [arrived[q, group] for q in moved], out)
    return out[None, None]


def solution(mesh):
    placed = (P("mom", "energy", None, None, None, None), P(), P(), P())
    return jax.shard_map(
        body,
        mesh=mesh,
        in_specs=placed,
        out_specs=P("mom", "energy", None, None, None, None),
        check_vma=False,
    )
```

```python
import jax
import jax.numpy as jnp
from jax import lax
from jax.experimental import pallas as pl
from jax.experimental.pallas import tpu as pltpu
from jax.sharding import PartitionSpec as P

SMAX = 1
HBM = pl.BlockSpec(memory_space=pltpu.HBM)
VMEM = pl.BlockSpec(memory_space=pltpu.VMEM)
SMEM = pl.BlockSpec(memory_space=pltpu.SMEM)


def passed_along(x, axis, by):
    length = lax.axis_size(axis)
    pairs = [(i, i + by) for i in range(length) if 0 <= i + by < length]
    return lax.ppermute(x, axis, pairs)


def passed_round(x, axis, by):
    length = lax.axis_size(axis)
    return lax.ppermute(x, axis, [(i, (i + by) % length) for i in range(length)])


def after(args, result):
    shift, coupling, phonon, own, *below = args
    own, _ = lax.optimization_barrier((own, result))
    return (shift, coupling, phonon, own, *below)


def products(blocks, coupling):
    lefts = [
        jnp.dot(coupling, block, preferred_element_type=jnp.float32).astype(jnp.bfloat16)
        for block in blocks
    ]
    return [jnp.dot(left, coupling, preferred_element_type=jnp.float32) for left in lefts]


def energy_products(energy, offset, shift, coupling, own, below):
    found = []
    for mode in range(coupling.shape[0]):
        step = shift[mode, offset]
        if energy == 0:
            blocks = [jnp.where(step > 0, below[0, c], own[0, c]) for c in range(2)]
        else:
            blocks = [own[energy - step, c] for c in range(2)]
        found.append(products(blocks, coupling[mode]))
    return found


def weighted(found, row, phonon):
    real_sum, imag_sum = None, None
    for mode, (first, second) in enumerate(found):
        size = first.shape[0]
        real = phonon[row, pl.ds(2 * mode * size, size), :].astype(jnp.float32)
        imag = phonon[row, pl.ds((2 * mode + 1) * size, size), :].astype(jnp.float32)
        real_term = first * real - second * imag
        imag_term = first * imag + second * real
        real_sum = real_term if real_sum is None else real_sum + real_term
        imag_sum = imag_term if imag_sum is None else imag_sum + imag_term
    return real_sum, imag_sum


def partial_kernel(offset, energies, shift, coupling, phonon, own, *rest):
    below = rest[0] if energies[0] == 0 else None
    out = rest[-1]
    for at, energy in enumerate(energies):
        found = energy_products(energy, offset, shift, coupling, own, below)
        real, imag = weighted(found, offset, phonon)
        out[at, 0] = real.astype(out.dtype)
        out[at, 1] = imag.astype(out.dtype)


def early_kernel(offset, shift_hbm, coupling_hbm, phonon_hbm, own_hbm, out, *rest):
    shift, coupling, phonon, own, sems = rest[-5:]
    used = pl.ds(own_hbm.shape[0] - 1 - SMAX, 1 + SMAX)
    pairs = [(shift_hbm, shift), (coupling_hbm, coupling), (own_hbm.at[used], own)]
    pairs += [(phonon_hbm.at[pl.ds(offset, 1)], phonon)]
    copies = [pltpu.make_async_copy(*pair, sems.at[n]) for n, pair in enumerate(pairs)]
    for copy in copies:
        copy.start()
    for copy in copies[:3]:
        copy.wait()
    found = energy_products(SMAX, offset, shift, coupling, own, None)
    copies[3].wait()
    real, imag = weighted(found, 0, phonon)
    out[0, 0] = real.astype(out.dtype)
    out[0, 1] = imag.astype(out.dtype)
    if len(rest) > 5:
        rest[0][0] = own[SMAX]


def early_call(offset, args, with_top=False):
    shift, coupling, phonon, own = args
    _, parts, size, _ = own.shape

    def kernel(*refs):
        early_kernel(offset, *refs)

    shape = jax.ShapeDtypeStruct((1, parts, size, size), jnp.bfloat16)
    return pl.pallas_call(
        kernel,
        out_shape=[shape] * (2 if with_top else 1),
        in_specs=[HBM] * 4,
        out_specs=[VMEM] * (2 if with_top else 1),
        scratch_shapes=[
            pltpu.SMEM(shift.shape, shift.dtype),
            pltpu.VMEM(coupling.shape, coupling.dtype),
            pltpu.VMEM((1,) + phonon.shape[1:], phonon.dtype),
            pltpu.VMEM((1 + SMAX,) + own.shape[1:], own.dtype),
            pltpu.SemaphoreType.DMA((4,)),
        ],
        compiler_params=pltpu.CompilerParams(vmem_limit_bytes=60 * 1024 * 1024),
        cost_estimate=estimate(coupling, 1),
    )(*args)


def estimate(coupling, energies):
    modes, size, _ = coupling.shape
    flops = 128 * energies * modes * size**3
    return pl.CostEstimate(flops=flops, bytes_accessed=1 << 24, transcendentals=0)


def partial_call(offset, energies, args, dtype):
    _, parts, size, _ = args[3].shape

    def kernel(*refs):
        partial_kernel(offset, energies, *refs)

    return pl.pallas_call(
        kernel,
        out_shape=jax.ShapeDtypeStruct((len(energies), parts, size, size), dtype),
        in_specs=[SMEM] + [VMEM] * (len(args) - 1),
        out_specs=VMEM,
        compiler_params=pltpu.CompilerParams(vmem_limit_bytes=32 * 1024 * 1024),
        cost_estimate=estimate(args[1], len(energies)),
    )(*args)


def finish_call(first, whole, own_sum, pieces, out=None):
    count, parts, size, _ = own_sum.shape

    def kernel(own_ref, *refs):
        at = pl.program_id(0)
        total = own_ref[at]
        for piece in refs[: len(pieces)]:
            total = total + piece[at].astype(jnp.float32)
        refs[-1][0] = total.astype(jnp.bfloat16)

    args = [own_sum, *pieces]
    specs = [VMEM] * len(args)
    aliases = {}
    if out is not None:
        aliases = {len(args): 0}
        args.append(out)
        specs.append(pl.BlockSpec(memory_space=pl.ANY))
    return pl.pallas_call(
        kernel,
        grid=(count,),
        out_shape=jax.ShapeDtypeStruct(whole, jnp.bfloat16),
        in_specs=specs,
        out_specs=pl.BlockSpec((1, parts, size, size), lambda i: (i + first, 0, 0, 0)),
        input_output_aliases=aliases,
        compiler_params=pltpu.CompilerParams(vmem_limit_bytes=32 * 1024 * 1024),
        cost_estimate=pl.CostEstimate(flops=1 << 33, bytes_accessed=1 << 24, transcendentals=0),
    )(*args)


def body(green, coupling, phonon, shift):
    own = green[0, 0]
    energies = own.shape[0]
    offsets = phonon.shape[0]
    radius = (offsets - 1) // 2
    moved = [q for r in range(1, radius + 1) for q in (r, -r)]
    args = (shift.T, coupling, phonon, own)
    top, middle = (energies - 1,), tuple(range(SMAX, energies - 1))
    bottom = tuple(range(SMAX))

    arrived = {}
    for q in moved:
        results = early_call(q + radius, args, with_top=q == moved[-1])
        args = after(args, results[0])
        arrived[q, top] = passed_round(results[0], "mom", q)
    below = passed_along(results[1], "energy", 1)

    def send(group, args):
        for q in moved:
            part = partial_call(q + radius, group, args, jnp.bfloat16)
            args = after(args, part)
            arrived[q, group] = passed_round(part, "mom", q)
        return args

    def finish(group, args, out):
        own_sum = partial_call(radius, group, args, jnp.float32)
        return finish_call(group[0], own.shape, own_sum, [arrived[q, group] for q in moved], out)

    args = send(middle, args)
    out = finish(top, args, None)
    shift, coupling, phonon, own = args
    own, below, out = lax.optimization_barrier((own, below, out))
    args = (shift, coupling, phonon, own)
    send(bottom, args + (below,))
    out = finish(middle, args, out)
    out = finish(bottom, args + (below,), out)
    return out[None, None]


def solution(mesh):
    placed = (P("mom", "energy", None, None, None, None), P(), P(), P())
    return jax.shard_map(
        body,
        mesh=mesh,
        in_specs=placed,
        out_specs=P("mom", "energy", None, None, None, None),
        check_vma=False,
    )
```

```python
import jax
import jax.numpy as jnp
from jax import lax
from jax.experimental import pallas as pl
from jax.experimental.pallas import tpu as pltpu
from jax.sharding import PartitionSpec as P

SMAX = 1
HBM = pl.BlockSpec(memory_space=pltpu.HBM)
VMEM = pl.BlockSpec(memory_space=pltpu.VMEM)
SMEM = pl.BlockSpec(memory_space=pltpu.SMEM)


def passed_along(x, axis, by):
    length = lax.axis_size(axis)
    pairs = [(i, i + by) for i in range(length) if 0 <= i + by < length]
    return lax.ppermute(x, axis, pairs)


def passed_round(x, by):
    groups, points = lax.axis_size("energy"), lax.axis_size("mom")
    pairs = []
    for group in range(groups):
        way = by if group % 2 == 0 else -by
        for point in range(points):
            pairs.append((group * points + point, group * points + (point + way) % points))
    return lax.ppermute(x, ("energy", "mom"), pairs)


def sent_offset(by, radius):
    return radius + by * (1 - 2 * lax.rem(lax.axis_index("energy"), 2))


def after(args, result):
    shift, coupling, phonon, own, *below = args
    own, _ = lax.optimization_barrier((own, result))
    return (shift, coupling, phonon, own, *below)


def products(blocks, coupling):
    lefts = [
        jnp.dot(coupling, block, preferred_element_type=jnp.float32).astype(jnp.bfloat16)
        for block in blocks
    ]
    return [jnp.dot(left, coupling, preferred_element_type=jnp.float32) for left in lefts]


def energy_products(energy, offset, shift, coupling, own, below):
    found = []
    for mode in range(coupling.shape[0]):
        step = shift[mode, offset]
        if energy == 0:
            blocks = [jnp.where(step > 0, below[0, c], own[0, c]) for c in range(2)]
        else:
            blocks = [own[energy - step, c] for c in range(2)]
        found.append(products(blocks, coupling[mode]))
    return found


def weighted(found, row, phonon):
    real_sum, imag_sum = None, None
    for mode, (first, second) in enumerate(found):
        size = first.shape[0]
        real = phonon[row, pl.ds(2 * mode * size, size), :].astype(jnp.float32)
        imag = phonon[row, pl.ds((2 * mode + 1) * size, size), :].astype(jnp.float32)
        real_term = first * real - second * imag
        imag_term = first * imag + second * real
        real_sum = real_term if real_sum is None else real_sum + real_term
        imag_sum = imag_term if imag_sum is None else imag_sum + imag_term
    return real_sum, imag_sum


def partial_kernel(by, radius, energies, shift, coupling, phonon, own, *rest):
    below = rest[0] if energies[0] == 0 else None
    out = rest[-1]
    offset = sent_offset(by, radius)
    for at, energy in enumerate(energies):
        found = energy_products(energy, offset, shift, coupling, own, below)
        real, imag = weighted(found, offset, phonon)
        out[at, 0] = real.astype(out.dtype)
        out[at, 1] = imag.astype(out.dtype)


def early_kernel(by, radius, shift_hbm, coupling_hbm, phonon_hbm, own_hbm, out, *rest):
    shift, coupling, phonon, own, sems = rest[-5:]
    offset = sent_offset(by, radius)
    used = pl.ds(own_hbm.shape[0] - 1 - SMAX, 1 + SMAX)
    pairs = [(shift_hbm, shift), (coupling_hbm, coupling), (own_hbm.at[used], own)]
    pairs += [(phonon_hbm.at[pl.ds(offset, 1)], phonon)]
    copies = [pltpu.make_async_copy(*pair, sems.at[n]) for n, pair in enumerate(pairs)]
    for copy in copies:
        copy.start()
    for copy in copies[:3]:
        copy.wait()
    found = energy_products(SMAX, offset, shift, coupling, own, None)
    copies[3].wait()
    real, imag = weighted(found, 0, phonon)
    out[0, 0] = real.astype(out.dtype)
    out[0, 1] = imag.astype(out.dtype)
    if len(rest) > 5:
        rest[0][0] = own[SMAX]


def early_call(by, radius, args, with_top=False):
    shift, coupling, phonon, own = args
    _, parts, size, _ = own.shape

    def kernel(*refs):
        early_kernel(by, radius, *refs)

    shape = jax.ShapeDtypeStruct((1, parts, size, size), jnp.bfloat16)
    return pl.pallas_call(
        kernel,
        out_shape=[shape] * (2 if with_top else 1),
        in_specs=[HBM] * 4,
        out_specs=[VMEM] * (2 if with_top else 1),
        scratch_shapes=[
            pltpu.SMEM(shift.shape, shift.dtype),
            pltpu.VMEM(coupling.shape, coupling.dtype),
            pltpu.VMEM((1,) + phonon.shape[1:], phonon.dtype),
            pltpu.VMEM((1 + SMAX,) + own.shape[1:], own.dtype),
            pltpu.SemaphoreType.DMA((4,)),
        ],
        compiler_params=pltpu.CompilerParams(vmem_limit_bytes=60 * 1024 * 1024),
        cost_estimate=estimate(coupling, 1),
    )(*args)


def estimate(coupling, energies):
    modes, size, _ = coupling.shape
    flops = 128 * energies * modes * size**3
    return pl.CostEstimate(flops=flops, bytes_accessed=1 << 24, transcendentals=0)


def partial_call(by, radius, energies, args, dtype):
    _, parts, size, _ = args[3].shape

    def kernel(*refs):
        partial_kernel(by, radius, energies, *refs)

    return pl.pallas_call(
        kernel,
        out_shape=jax.ShapeDtypeStruct((len(energies), parts, size, size), dtype),
        in_specs=[SMEM] + [VMEM] * (len(args) - 1),
        out_specs=VMEM,
        compiler_params=pltpu.CompilerParams(vmem_limit_bytes=32 * 1024 * 1024),
        cost_estimate=estimate(args[1], len(energies)),
    )(*args)


def finish_call(first, whole, own_sum, pieces, out=None):
    count, parts, size, _ = own_sum.shape

    def kernel(own_ref, *refs):
        at = pl.program_id(0)
        total = own_ref[at]
        for piece in refs[: len(pieces)]:
            total = total + piece[at].astype(jnp.float32)
        refs[-1][0] = total.astype(jnp.bfloat16)

    args = [own_sum, *pieces]
    specs = [VMEM] * len(args)
    aliases = {}
    if out is not None:
        aliases = {len(args): 0}
        args.append(out)
        specs.append(pl.BlockSpec(memory_space=pl.ANY))
    return pl.pallas_call(
        kernel,
        grid=(count,),
        out_shape=jax.ShapeDtypeStruct(whole, jnp.bfloat16),
        in_specs=specs,
        out_specs=pl.BlockSpec((1, parts, size, size), lambda i: (i + first, 0, 0, 0)),
        input_output_aliases=aliases,
        compiler_params=pltpu.CompilerParams(vmem_limit_bytes=32 * 1024 * 1024),
        cost_estimate=pl.CostEstimate(flops=1 << 33, bytes_accessed=1 << 24, transcendentals=0),
    )(*args)


def body(green, coupling, phonon, shift):
    own = green[0, 0]
    energies = own.shape[0]
    offsets = phonon.shape[0]
    radius = (offsets - 1) // 2
    moved = [q for r in range(1, radius + 1) for q in (r, -r)]
    args = (shift.T, coupling, phonon, own)
    top, middle = (energies - 1,), tuple(range(SMAX, energies - 1))
    bottom = tuple(range(SMAX))

    arrived = {}
    for q in moved:
        results = early_call(q, radius, args, with_top=q == moved[-1])
        args = after(args, results[0])
        arrived[q, top] = passed_round(results[0], q)
    below = passed_along(results[1], "energy", 1)

    def send(group, args):
        for q in moved:
            part = partial_call(q, radius, group, args, jnp.bfloat16)
            args = after(args, part)
            arrived[q, group] = passed_round(part, q)
        return args

    def finish(group, args, out):
        own_sum = partial_call(0, radius, group, args, jnp.float32)
        return finish_call(group[0], own.shape, own_sum, [arrived[q, group] for q in moved], out)

    args = send(middle, args)
    out = finish(top, args, None)
    shift, coupling, phonon, own = args
    own, below, out = lax.optimization_barrier((own, below, out))
    args = (shift, coupling, phonon, own)
    send(bottom, args + (below,))
    out = finish(middle, args, out)
    out = finish(bottom, args + (below,), out)
    return out[None, None]


def solution(mesh):
    placed = (P("mom", "energy", None, None, None, None), P(), P(), P())
    return jax.shard_map(
        body,
        mesh=mesh,
        in_specs=placed,
        out_specs=P("mom", "energy", None, None, None, None),
        check_vma=False,
    )
```

```python
import jax
import jax.numpy as jnp
from jax import lax
from jax.experimental import pallas as pl
from jax.experimental.pallas import tpu as pltpu
from jax.sharding import PartitionSpec as P

SMAX = 1
HBM = pl.BlockSpec(memory_space=pltpu.HBM)
VMEM = pl.BlockSpec(memory_space=pltpu.VMEM)
SMEM = pl.BlockSpec(memory_space=pltpu.SMEM)


def passed_along(x, axis, by):
    length = lax.axis_size(axis)
    pairs = [(i, i + by) for i in range(length) if 0 <= i + by < length]
    return lax.ppermute(x, axis, pairs)


def passed_round(x, by):
    groups, points = lax.axis_size("energy"), lax.axis_size("mom")
    pairs = []
    for group in range(groups):
        way = by if group % 2 == 0 else -by
        for point in range(points):
            pairs.append((group * points + point, group * points + (point + way) % points))
    return lax.ppermute(x, ("energy", "mom"), pairs)


def sent_offset(by, radius):
    return radius + by * (1 - 2 * lax.rem(lax.axis_index("energy"), 2))


def after(args, result):
    shift, coupling, phonon, own, *below = args
    own, _ = lax.optimization_barrier((own, result))
    return (shift, coupling, phonon, own, *below)


def products(blocks, coupling):
    lefts = [
        jnp.dot(coupling, block, preferred_element_type=jnp.float32).astype(jnp.bfloat16)
        for block in blocks
    ]
    return [jnp.dot(left, coupling, preferred_element_type=jnp.float32) for left in lefts]


def energy_products(energy, offset, shift, coupling, own, below):
    found = []
    for mode in range(coupling.shape[0]):
        step = shift[mode, offset]
        if energy == 0:
            blocks = [jnp.where(step > 0, below[0, c], own[0, c]) for c in range(2)]
        else:
            blocks = [own[energy - step, c] for c in range(2)]
        found.append(products(blocks, coupling[mode]))
    return found


def weighted(found, row, phonon):
    real_sum, imag_sum = None, None
    for mode, (first, second) in enumerate(found):
        size = first.shape[0]
        real = phonon[row, pl.ds(2 * mode * size, size), :].astype(jnp.float32)
        imag = phonon[row, pl.ds((2 * mode + 1) * size, size), :].astype(jnp.float32)
        real_term = first * real - second * imag
        imag_term = first * imag + second * real
        real_sum = real_term if real_sum is None else real_sum + real_term
        imag_sum = imag_term if imag_sum is None else imag_sum + imag_term
    return real_sum, imag_sum


def partial_kernel(by, radius, energies, shift, coupling, phonon, own, *rest):
    below = rest[0] if energies[0] == 0 else None
    out = rest[-1]
    offset = sent_offset(by, radius)
    for at, energy in enumerate(energies):
        found = energy_products(energy, offset, shift, coupling, own, below)
        real, imag = weighted(found, offset, phonon)
        out[at, 0] = real.astype(out.dtype)
        out[at, 1] = imag.astype(out.dtype)


def early_kernel(by, radius, shift_hbm, coupling_hbm, phonon_hbm, own_hbm, out, *rest):
    shift, coupling, phonon, own, sems = rest[-5:]
    offset = sent_offset(by, radius)
    used = pl.ds(own_hbm.shape[0] - 1 - SMAX, 1 + SMAX)
    pairs = [(shift_hbm, shift), (coupling_hbm, coupling), (own_hbm.at[used], own)]
    pairs += [(phonon_hbm.at[pl.ds(offset, 1)], phonon)]
    copies = [pltpu.make_async_copy(*pair, sems.at[n]) for n, pair in enumerate(pairs)]
    for copy in copies:
        copy.start()
    for copy in copies[:3]:
        copy.wait()
    found = energy_products(SMAX, offset, shift, coupling, own, None)
    copies[3].wait()
    real, imag = weighted(found, 0, phonon)
    out[0, 0] = real.astype(out.dtype)
    out[0, 1] = imag.astype(out.dtype)
    if len(rest) > 5:
        rest[0][0] = own[SMAX]


def early_call(by, radius, args, with_top=False):
    shift, coupling, phonon, own = args
    _, parts, size, _ = own.shape

    def kernel(*refs):
        early_kernel(by, radius, *refs)

    shape = jax.ShapeDtypeStruct((1, parts, size, size), jnp.bfloat16)
    return pl.pallas_call(
        kernel,
        out_shape=[shape] * (2 if with_top else 1),
        in_specs=[HBM] * 4,
        out_specs=[VMEM] * (2 if with_top else 1),
        scratch_shapes=[
            pltpu.SMEM(shift.shape, shift.dtype),
            pltpu.VMEM(coupling.shape, coupling.dtype),
            pltpu.VMEM((1,) + phonon.shape[1:], phonon.dtype),
            pltpu.VMEM((1 + SMAX,) + own.shape[1:], own.dtype),
            pltpu.SemaphoreType.DMA((4,)),
        ],
        compiler_params=pltpu.CompilerParams(vmem_limit_bytes=60 * 1024 * 1024),
        cost_estimate=estimate(coupling, 1),
    )(*args)


def estimate(coupling, energies):
    modes, size, _ = coupling.shape
    flops = 128 * energies * modes * size**3
    return pl.CostEstimate(flops=flops, bytes_accessed=1 << 24, transcendentals=0)


def partial_call(by, radius, energies, args, dtype):
    _, parts, size, _ = args[3].shape

    def kernel(*refs):
        partial_kernel(by, radius, energies, *refs)

    return pl.pallas_call(
        kernel,
        out_shape=jax.ShapeDtypeStruct((len(energies), parts, size, size), dtype),
        in_specs=[SMEM] + [VMEM] * (len(args) - 1),
        out_specs=VMEM,
        compiler_params=pltpu.CompilerParams(vmem_limit_bytes=32 * 1024 * 1024),
        cost_estimate=estimate(args[1], len(energies)),
    )(*args)


def finish_call(first, whole, own_sum, pieces, out=None):
    count, parts, size, _ = own_sum.shape

    def kernel(own_ref, *refs):
        at = pl.program_id(0)
        total = own_ref[at]
        for piece in refs[: len(pieces)]:
            total = total + piece[at].astype(jnp.float32)
        refs[-1][0] = total.astype(jnp.bfloat16)

    args = [own_sum, *pieces]
    specs = [VMEM] * len(args)
    aliases = {}
    if out is not None:
        aliases = {len(args): 0}
        args.append(out)
        specs.append(pl.BlockSpec(memory_space=pl.ANY))
    return pl.pallas_call(
        kernel,
        grid=(count,),
        out_shape=jax.ShapeDtypeStruct(whole, jnp.bfloat16),
        in_specs=specs,
        out_specs=pl.BlockSpec((1, parts, size, size), lambda i: (i + first, 0, 0, 0)),
        input_output_aliases=aliases,
        compiler_params=pltpu.CompilerParams(vmem_limit_bytes=32 * 1024 * 1024),
        cost_estimate=pl.CostEstimate(flops=1 << 33, bytes_accessed=1 << 24, transcendentals=0),
    )(*args)


def body(green, coupling, phonon, shift):
    own = green[0, 0]
    energies = own.shape[0]
    offsets = phonon.shape[0]
    radius = (offsets - 1) // 2
    moved = [q for r in range(1, radius + 1) for q in (r, -r)]
    args = (shift.T, coupling, phonon, own)
    groups = [(energy,) for energy in reversed(range(energies))]
    arrived = {}
    for q in moved:
        results = early_call(q, radius, args, with_top=q == moved[-1])
        args = after(args, results[0])
        arrived[q, groups[0]] = passed_round(results[0], q)
    below = passed_along(results[1], "energy", 1)

    def needs(group):
        return args + ((below,) if group[0] == 0 else ())

    def finish(group, out):
        own_sum = partial_call(0, radius, group, needs(group), jnp.float32)
        return finish_call(group[0], own.shape, own_sum, [arrived[q, group] for q in moved], out)

    out = None
    for n, group in enumerate(groups[1:], 1):
        if n > 1:
            out = finish(groups[n - 2], out)
            shift, coupling, phonon, kept = args
            kept, below, out = lax.optimization_barrier((kept, below, out))
            args = (shift, coupling, phonon, kept)
        for q in moved:
            part = partial_call(q, radius, group, needs(group), jnp.bfloat16)
            args = after(args, part)
            arrived[q, group] = passed_round(part, q)
    for group in groups[-2:]:
        out = finish(group, out)
    return out[None, None]


def solution(mesh):
    placed = (P("mom", "energy", None, None, None, None), P(), P(), P())
    return jax.shard_map(
        body,
        mesh=mesh,
        in_specs=placed,
        out_specs=P("mom", "energy", None, None, None, None),
        check_vma=False,
    )
```

```python
import jax
import jax.numpy as jnp
from jax import lax
from jax.experimental import pallas as pl
from jax.experimental.pallas import tpu as pltpu
from jax.sharding import PartitionSpec as P

SMAX = 1
MIB = 1024 * 1024
HBM = pl.BlockSpec(memory_space=pltpu.HBM)
VMEM = pl.BlockSpec(memory_space=pltpu.VMEM)
SMEM = pl.BlockSpec(memory_space=pltpu.SMEM)


def passed_along(x, axis, by):
    length = lax.axis_size(axis)
    pairs = [(i, i + by) for i in range(length) if 0 <= i + by < length]
    return lax.ppermute(x, axis, pairs)


def passed_round(x, axis, by):
    length = lax.axis_size(axis)
    return lax.ppermute(x, axis, [(i, (i + by) % length) for i in range(length)])


def after(x, *results):
    return lax.optimization_barrier((x, *results))[0]


def estimate(coupling, energies):
    modes, size, _ = coupling.shape
    flops = 128 * energies * modes * size**3
    return pl.CostEstimate(flops=flops, bytes_accessed=1 << 24, transcendentals=0)


def params(limit=32):
    return pltpu.CompilerParams(vmem_limit_bytes=limit * MIB)


def products(blocks, coupling):
    lefts = [
        jnp.dot(coupling, block, preferred_element_type=jnp.float32).astype(jnp.bfloat16)
        for block in blocks
    ]
    return [jnp.dot(left, coupling, preferred_element_type=jnp.float32) for left in lefts]


class Slots:
    def __init__(self, rest, top=None, below=None):
        self.rest, self.top, self.below = rest, top, below

    def take(self, energy, step, part, last):
        if energy == last and self.top is not None:
            return jnp.where(step > 0, self.rest[last - 1, part], self.top[0, part])
        if energy == 0:
            return jnp.where(step > 0, self.below[0, part], self.rest[0, part])
        return self.rest[energy - step, part]


def terms(energy, last, offset, shift, coupling, phonon, slots):
    modes, size, _ = coupling.shape
    real_sum, imag_sum = None, None
    for mode in range(modes):
        step = shift[mode, offset]
        blocks = [slots.take(energy, step, part, last) for part in range(2)]
        first, second = products(blocks, coupling[mode])
        real = phonon[offset, pl.ds(2 * mode * size, size), :].astype(jnp.float32)
        imag = phonon[offset, pl.ds((2 * mode + 1) * size, size), :].astype(jnp.float32)
        real_term = first * real - second * imag
        imag_term = first * imag + second * real
        real_sum = real_term if real_sum is None else real_sum + real_term
        imag_sum = imag_term if imag_sum is None else imag_sum + imag_term
    return real_sum, imag_sum


def sums_call(energies, sources, args, whole, dtype):
    count, parts, size, _ = whole
    arrays, layout = [], []
    for offset, slots in sources:
        places = []
        for array in (slots.rest, slots.top, slots.below):
            if array is None:
                places.append(None)
            else:
                places.append(len(arrays))
                arrays.append(array)
        layout.append((offset, places))

    def kernel(shift, coupling, phonon, *refs):
        out = refs[-1]
        for at, energy in enumerate(energies):
            for n, (offset, places) in enumerate(layout):
                slots = Slots(*[None if p is None else refs[p] for p in places])
                real, imag = terms(energy, count - 1, offset, shift, coupling, phonon, slots)
                if n > 0:
                    real, imag = real + out[at, 0], imag + out[at, 1]
                out[at, 0] = real.astype(out.dtype)
                out[at, 1] = imag.astype(out.dtype)

    return pl.pallas_call(
        kernel,
        out_shape=jax.ShapeDtypeStruct((len(energies), parts, size, size), dtype),
        in_specs=[SMEM] + [VMEM] * (2 + len(arrays)),
        out_specs=VMEM,
        compiler_params=params(),
        cost_estimate=estimate(args[1], len(energies) * len(sources)),
    )(*args, *arrays)


def early_call(offset, args, own):
    shift, coupling, phonon = args
    energies, parts, size, _ = own.shape
    used = pl.ds(energies - 1 - SMAX, 1 + SMAX)

    def kernel(shift_hbm, coupling_hbm, phonon_hbm, own_hbm, out, *scratch):
        shift, coupling, phonon, own, sems = scratch
        pairs = [(shift_hbm, shift), (coupling_hbm, coupling), (own_hbm.at[used], own)]
        pairs += [(phonon_hbm.at[offset], phonon.at[offset])]
        copies = [pltpu.make_async_copy(*pair, sems.at[n]) for n, pair in enumerate(pairs)]
        for copy in copies:
            copy.start()
        for copy in copies:
            copy.wait()
        real, imag = terms(SMAX, SMAX + 1, offset, shift, coupling, phonon, Slots(own))
        out[0, 0] = real.astype(out.dtype)
        out[0, 1] = imag.astype(out.dtype)

    return pl.pallas_call(
        kernel,
        out_shape=jax.ShapeDtypeStruct((1, parts, size, size), own.dtype),
        in_specs=[HBM] * 4,
        out_specs=VMEM,
        scratch_shapes=[
            pltpu.SMEM(shift.shape, shift.dtype),
            pltpu.VMEM(coupling.shape, coupling.dtype),
            pltpu.VMEM(phonon.shape, phonon.dtype),
            pltpu.VMEM((1 + SMAX,) + own.shape[1:], own.dtype),
            pltpu.SemaphoreType.DMA((4,)),
        ],
        compiler_params=params(60),
        cost_estimate=estimate(coupling, 1),
    )(shift, coupling, phonon, own)


def top_call(own):
    energies = own.shape[0]

    def kernel(own_ref, out_ref, sem):
        copy = pltpu.make_async_copy(own_ref.at[pl.ds(energies - 1, 1)], out_ref, sem)
        copy.start()
        copy.wait()

    return pl.pallas_call(
        kernel,
        out_shape=jax.ShapeDtypeStruct((1,) + own.shape[1:], own.dtype),
        in_specs=[HBM],
        out_specs=HBM,
        scratch_shapes=[pltpu.SemaphoreType.DMA],
        compiler_params=params(60),
        cost_estimate=pl.CostEstimate(flops=0, bytes_accessed=1 << 20, transcendentals=0),
    )(own)


def finish_call(first, whole, total, place, pieces, out=None):
    count, parts, size, _ = pieces[0].shape

    def kernel(total_ref, *refs):
        at = pl.program_id(0)
        result = total_ref[place + at]
        for piece in refs[: len(pieces)]:
            result = result + piece[at].astype(jnp.float32)
        refs[-1][0] = result.astype(jnp.bfloat16)

    args = [total, *pieces]
    specs = [VMEM] * len(args)
    aliases = {}
    if out is not None:
        aliases = {len(args): 0}
        args.append(out)
        specs.append(pl.BlockSpec(memory_space=pl.ANY))
    return pl.pallas_call(
        kernel,
        grid=(count,),
        out_shape=jax.ShapeDtypeStruct(whole, jnp.bfloat16),
        in_specs=specs,
        out_specs=pl.BlockSpec((1, parts, size, size), lambda i: (i + first, 0, 0, 0)),
        input_output_aliases=aliases,
        compiler_params=params(),
        cost_estimate=pl.CostEstimate(flops=1 << 33, bytes_accessed=1 << 24, transcendentals=0),
    )(*args)


def body(green, coupling, phonon, shift):
    own = green[0, 0]
    whole = own.shape
    energies = whole[0]
    offsets = phonon.shape[0]
    radius = (offsets - 1) // 2
    ups = range(1, radius + 1)
    args = (shift.T, coupling, phonon)
    top, middle, bottom = (energies - 1,), tuple(range(1, energies - 1)), (0,)

    own_top = top_call(own)
    tops = {q: passed_round(own_top, "mom", q) for q in ups}
    own = after(own, own_top)
    arrived = {}
    for q in ups:
        part = early_call(radius - q, args, own)
        own = after(own, part)
        arrived[-q, top] = passed_round(part, "mom", -q)
    below = passed_along(after(own_top, part), "energy", 1)
    rest = own[: energies - 1]
    rests = {q: passed_round(rest, "mom", q) for q in ups}
    own = after(own, rest)
    for group in (middle, bottom):
        for q in ups:
            slots = Slots(own, None, below if group == bottom else None)
            part = sums_call(group, [(radius - q, slots)], args, whole, jnp.bfloat16)
            own = after(own, part)
            arrived[-q, group] = passed_round(part, "mom", -q)
    belows = {q: passed_along(after(tops[q], own), "energy", 1) for q in ups}

    out = None
    for group in (top, middle, bottom):
        at_bottom = group == bottom
        sources = [(radius, Slots(own, None, below if at_bottom else None))]
        for q in ups:
            slots = Slots(
                rests[q],
                tops[q] if group == top else None,
                belows[q] if at_bottom else None,
            )
            sources.append((radius + q, slots))
        total = sums_call(group, sources, args, whole, jnp.float32)
        pieces = [arrived[-q, group] for q in ups]
        out = finish_call(group[0], whole, total, 0, pieces, out)
    return out[None, None]


def solution(mesh):
    placed = (P("mom", "energy", None, None, None, None), P(), P(), P())
    return jax.shard_map(
        body,
        mesh=mesh,
        in_specs=placed,
        out_specs=P("mom", "energy", None, None, None, None),
        check_vma=False,
    )
```

```python
import jax
import jax.numpy as jnp
from jax import lax
from jax.experimental import pallas as pl
from jax.experimental.pallas import tpu as pltpu
from jax.sharding import PartitionSpec as P

SMAX = 1
MIB = 1024 * 1024
VMEM = pl.BlockSpec(memory_space=pltpu.VMEM)
SMEM = pl.BlockSpec(memory_space=pltpu.SMEM)


def passed_along(x, axis, by):
    length = lax.axis_size(axis)
    pairs = [(i, i + by) for i in range(length) if 0 <= i + by < length]
    return lax.ppermute(x, axis, pairs)


def passed_round(x, axis, by):
    length = lax.axis_size(axis)
    return lax.ppermute(x, axis, [(i, (i + by) % length) for i in range(length)])


def after(x, *results):
    return lax.optimization_barrier((x, *results))[0]


def estimate(coupling, energies):
    modes, size, _ = coupling.shape
    flops = 128 * energies * modes * size**3
    return pl.CostEstimate(flops=flops, bytes_accessed=1 << 24, transcendentals=0)


def params(limit=32):
    return pltpu.CompilerParams(vmem_limit_bytes=limit * MIB)


def products(blocks, coupling):
    lefts = [
        jnp.dot(coupling, block, preferred_element_type=jnp.float32).astype(jnp.bfloat16)
        for block in blocks
    ]
    return [jnp.dot(left, coupling, preferred_element_type=jnp.float32) for left in lefts]


class Slots:
    def __init__(self, places):
        self.places = places

    def take(self, energy, step, part):
        low, high = self.places[energy - SMAX], self.places[energy]
        if low[0] is high[0]:
            return high[0][high[1] - step, part]
        return jnp.where(step > 0, low[0][low[1], part], high[0][high[1], part])


def terms(energy, offset, shift, coupling, phonon, slots):
    modes, size, _ = coupling.shape
    real_sum, imag_sum = None, None
    for mode in range(modes):
        step = shift[mode, offset]
        blocks = [slots.take(energy, step, part) for part in range(2)]
        first, second = products(blocks, coupling[mode])
        real = phonon[offset, pl.ds(2 * mode * size, size), :].astype(jnp.float32)
        imag = phonon[offset, pl.ds((2 * mode + 1) * size, size), :].astype(jnp.float32)
        real_term = first * real - second * imag
        imag_term = first * imag + second * real
        real_sum = real_term if real_sum is None else real_sum + real_term
        imag_sum = imag_term if imag_sum is None else imag_sum + imag_term
    return real_sum, imag_sum


def sums_call(energies, sources, args, like, dtype):
    _, parts, size, _ = like.shape
    arrays = []

    def number(array):
        for n, other in enumerate(arrays):
            if other is array:
                return n
        arrays.append(array)
        return len(arrays) - 1

    used = {slot for energy in energies for slot in (energy - SMAX, energy)}
    layout = []
    for offset, slots in sources:
        places = {k: (number(v[0]), v[1]) for k, v in slots.places.items() if k in used}
        layout.append((offset, places))

    def kernel(shift, coupling, phonon, *refs):
        out = refs[-1]
        for at, energy in enumerate(energies):
            for n, (offset, places) in enumerate(layout):
                slots = Slots({k: (refs[v[0]], v[1]) for k, v in places.items()})
                real, imag = terms(energy, offset, shift, coupling, phonon, slots)
                if n > 0:
                    real, imag = real + out[at, 0], imag + out[at, 1]
                out[at, 0] = real.astype(out.dtype)
                out[at, 1] = imag.astype(out.dtype)

    return pl.pallas_call(
        kernel,
        out_shape=jax.ShapeDtypeStruct((len(energies), parts, size, size), dtype),
        in_specs=[SMEM] + [VMEM] * (2 + len(arrays)),
        out_specs=VMEM,
        compiler_params=params(),
        cost_estimate=estimate(args[1], len(energies) * len(sources)),
    )(*args, *arrays)


def finish_call(energy, whole, total, pieces, out=None):
    _, parts, size, _ = whole

    def kernel(total_ref, *refs):
        result = total_ref[0]
        for piece in refs[: len(pieces)]:
            result = result + piece[0].astype(jnp.float32)
        refs[-1][0] = result.astype(jnp.bfloat16)

    args = [total, *pieces]
    specs = [VMEM] * len(args)
    aliases = {}
    if out is not None:
        aliases = {len(args): 0}
        args.append(out)
        specs.append(pl.BlockSpec(memory_space=pl.ANY))
    return pl.pallas_call(
        kernel,
        grid=(1,),
        out_shape=jax.ShapeDtypeStruct(whole, jnp.bfloat16),
        in_specs=specs,
        out_specs=pl.BlockSpec((1, parts, size, size), lambda i: (energy, 0, 0, 0)),
        input_output_aliases=aliases,
        compiler_params=params(),
        cost_estimate=pl.CostEstimate(flops=1 << 33, bytes_accessed=1 << 24, transcendentals=0),
    )(*args)


def body(green, coupling, phonon, shift):
    own = green[0, 0]
    whole = own.shape
    energies = whole[0]
    last = energies - 1
    offsets = phonon.shape[0]
    radius = (offsets - 1) // 2
    ups = range(1, radius + 1)
    args = (shift.T, coupling, phonon)

    def raw(first, count, *results):
        return after(own, *results)[first : first + count]

    def send_raw(block):
        return {q: passed_round(block, "mom", q) for q in ups}

    def send_part(energy, slots):
        parts = []
        for q in ups:
            part = sums_call((energy,), [(radius - q, slots)], args, own, jnp.bfloat16)
            parts.append((part, passed_round(part, "mom", -q)))
        return [part for part, _ in parts], [piece for _, piece in parts]

    def slots_of(block, below=None):
        places = {energy: (block, energy) for energy in range(energies)}
        if below is not None:
            places[-1] = (below, 0)
        return Slots(places)

    own_top = raw(last, 1)
    tops = send_raw(own_top)
    pieces = {}
    made, pieces[last] = send_part(last, slots_of(after(own, own_top)))
    below = passed_along(after(own_top, *made), "energy", 1)
    mid = raw(1, last - 1, own_top)
    mids = send_raw(mid)
    made, pieces[last - 1] = send_part(last - 1, slots_of(after(own, mid)))
    low = raw(0, 1, *made, *tops.values(), *pieces[last])
    lows = send_raw(low)
    belows = {q: passed_along(after(tops[q], low), "energy", 1) for q in ups}
    paced = [low, *mids.values()]
    for energy in reversed(range(last - 1)):
        made, pieces[energy] = send_part(energy, slots_of(after(own, *paced), below))
        paced = made + pieces[energy + 1]

    out = None
    for energy in reversed(range(energies)):
        sources = [(radius, slots_of(own, below))]
        for q in ups:
            places = {slot: (mids[q], slot - 1) for slot in range(1, last)}
            places.update({last: (tops[q], 0), 0: (lows[q], 0), -1: (belows[q], 0)})
            sources.append((radius + q, Slots(places)))
        total = sums_call((energy,), sources, args, own, jnp.float32)
        out = finish_call(energy, whole, total, pieces[energy], out)
    return out[None, None]


def solution(mesh):
    placed = (P("mom", "energy", None, None, None, None), P(), P(), P())
    return jax.shard_map(
        body,
        mesh=mesh,
        in_specs=placed,
        out_specs=P("mom", "energy", None, None, None, None),
        check_vma=False,
    )
```

```python
import jax
import jax.numpy as jnp
from jax import lax
from jax.experimental import pallas as pl
from jax.experimental.pallas import tpu as pltpu
from jax.sharding import PartitionSpec as P

SMAX = 1
MIB = 1024 * 1024
VMEM = pl.BlockSpec(memory_space=pltpu.VMEM)
SMEM = pl.BlockSpec(memory_space=pltpu.SMEM)


def passed_along(x, axis, by):
    length = lax.axis_size(axis)
    pairs = [(i, i + by) for i in range(length) if 0 <= i + by < length]
    return lax.ppermute(x, axis, pairs)


def passed_round(x, axis, by):
    length = lax.axis_size(axis)
    return lax.ppermute(x, axis, [(i, (i + by) % length) for i in range(length)])


def after(x, *results):
    return lax.optimization_barrier((x, *results))[0]


def estimate(coupling, energies):
    modes, size, _ = coupling.shape
    flops = 128 * energies * modes * size**3
    return pl.CostEstimate(flops=flops, bytes_accessed=1 << 24, transcendentals=0)


def params(limit=32):
    return pltpu.CompilerParams(vmem_limit_bytes=limit * MIB)


def products(blocks, coupling):
    lefts = [
        jnp.dot(coupling, block, preferred_element_type=jnp.float32).astype(jnp.bfloat16)
        for block in blocks
    ]
    return [jnp.dot(left, coupling, preferred_element_type=jnp.float32) for left in lefts]


class Slots:
    def __init__(self, places):
        self.places = places

    def take(self, energy, step, part):
        low, high = self.places[energy - SMAX], self.places[energy]
        if low[0] is high[0]:
            return high[0][high[1] - step, part]
        return jnp.where(step > 0, low[0][low[1], part], high[0][high[1], part])


def terms(energy, offset, shift, coupling, phonon, slots):
    modes, size, _ = coupling.shape
    real_sum, imag_sum = None, None
    for mode in range(modes):
        step = shift[mode, offset]
        blocks = [slots.take(energy, step, part) for part in range(2)]
        first, second = products(blocks, coupling[mode])
        real = phonon[offset, pl.ds(2 * mode * size, size), :].astype(jnp.float32)
        imag = phonon[offset, pl.ds((2 * mode + 1) * size, size), :].astype(jnp.float32)
        real_term = first * real - second * imag
        imag_term = first * imag + second * real
        real_sum = real_term if real_sum is None else real_sum + real_term
        imag_sum = imag_term if imag_sum is None else imag_sum + imag_term
    return real_sum, imag_sum


def sums_call(energies, sources, args, like, dtype):
    _, parts, size, _ = like.shape
    arrays = []

    def number(array):
        for n, other in enumerate(arrays):
            if other is array:
                return n
        arrays.append(array)
        return len(arrays) - 1

    used = {slot for energy in energies for slot in (energy - SMAX, energy)}
    layout = []
    for offset, slots in sources:
        places = {k: (number(v[0]), v[1]) for k, v in slots.places.items() if k in used}
        layout.append((offset, places))

    def kernel(shift, coupling, phonon, *refs):
        out = refs[-1]
        for at, energy in enumerate(energies):
            for n, (offset, places) in enumerate(layout):
                slots = Slots({k: (refs[v[0]], v[1]) for k, v in places.items()})
                real, imag = terms(energy, offset, shift, coupling, phonon, slots)
                if n > 0:
                    real, imag = real + out[at, 0], imag + out[at, 1]
                out[at, 0] = real.astype(out.dtype)
                out[at, 1] = imag.astype(out.dtype)

    return pl.pallas_call(
        kernel,
        out_shape=jax.ShapeDtypeStruct((len(energies), parts, size, size), dtype),
        in_specs=[SMEM] + [VMEM] * (2 + len(arrays)),
        out_specs=VMEM,
        compiler_params=params(),
        cost_estimate=estimate(args[1], len(energies) * len(sources)),
    )(*args, *arrays)


def finish_call(energy, whole, total, pieces, out=None):
    _, parts, size, _ = whole

    def kernel(total_ref, *refs):
        result = total_ref[0]
        for piece in refs[: len(pieces)]:
            result = result + piece[0].astype(jnp.float32)
        refs[-1][0] = result.astype(jnp.bfloat16)

    args = [total, *pieces]
    specs = [VMEM] * len(args)
    aliases = {}
    if out is not None:
        aliases = {len(args): 0}
        args.append(out)
        specs.append(pl.BlockSpec(memory_space=pl.ANY))
    return pl.pallas_call(
        kernel,
        grid=(1,),
        out_shape=jax.ShapeDtypeStruct(whole, jnp.bfloat16),
        in_specs=specs,
        out_specs=pl.BlockSpec((1, parts, size, size), lambda i: (energy, 0, 0, 0)),
        input_output_aliases=aliases,
        compiler_params=params(),
        cost_estimate=pl.CostEstimate(flops=1 << 33, bytes_accessed=1 << 24, transcendentals=0),
    )(*args)


def body(green, coupling, phonon, shift):
    own = green[0, 0]
    whole = own.shape
    energies = whole[0]
    last = energies - 1
    offsets = phonon.shape[0]
    radius = (offsets - 1) // 2
    ups = range(1, radius + 1)
    args = (shift.T, coupling, phonon)

    def raw(first, count, *results):
        return after(own, *results)[first : first + count]

    def send_raw(block):
        return {q: passed_round(block, "mom", q) for q in ups}

    def send_part(energy, slots):
        parts = []
        for q in ups:
            part = sums_call((energy,), [(radius - q, slots)], args, own, jnp.bfloat16)
            parts.append((part, passed_round(part, "mom", -q)))
        return [part for part, _ in parts], [piece for _, piece in parts]

    def slots_of(block, below=None):
        places = {energy: (block, energy) for energy in range(energies)}
        if below is not None:
            places[-1] = (below, 0)
        return Slots(places)

    own_top = raw(last, 1)
    tops = send_raw(own_top)
    pieces = {}
    made, pieces[last] = send_part(last, slots_of(after(own, own_top)))
    below = passed_along(after(own_top, *made), "energy", 1)
    mid = raw(1, last - 1, own_top)
    mids = send_raw(mid)
    made, pieces[last - 1] = send_part(last - 1, slots_of(after(own, mid)))
    low = raw(0, 1, *made, *tops.values(), *pieces[last])
    lows = send_raw(low)
    belows = {q: passed_along(after(tops[q], low), "energy", 1) for q in ups}
    paced = [low, *mids.values()]
    for energy in reversed(range(last - 1)):
        made, pieces[energy] = send_part(energy, slots_of(after(own, *paced), below))
        paced = [*made, *lows.values()]

    out = None
    for energy in reversed(range(energies)):
        sources = [(radius, slots_of(own, below))]
        for q in ups:
            places = {slot: (mids[q], slot - 1) for slot in range(1, last)}
            places.update({last: (tops[q], 0), 0: (lows[q], 0), -1: (belows[q], 0)})
            sources.append((radius + q, Slots(places)))
        total = sums_call((energy,), sources, args, own, jnp.float32)
        out = finish_call(energy, whole, total, pieces[energy], out)
    return out[None, None]


def solution(mesh):
    placed = (P("mom", "energy", None, None, None, None), P(), P(), P())
    return jax.shard_map(
        body,
        mesh=mesh,
        in_specs=placed,
        out_specs=P("mom", "energy", None, None, None, None),
        check_vma=False,
    )
```

```python
import jax
import jax.numpy as jnp
from jax import lax
from jax.experimental import pallas as pl
from jax.experimental.pallas import tpu as pltpu
from jax.sharding import PartitionSpec as P

SMAX = 1
HBM = pl.BlockSpec(memory_space=pltpu.HBM)
VMEM = pl.BlockSpec(memory_space=pltpu.VMEM)
SMEM = pl.BlockSpec(memory_space=pltpu.SMEM)
LIMIT = 32 * 1024 * 1024


def passed_along(x, axis, by):
    length = lax.axis_size(axis)
    pairs = [(i, i + by) for i in range(length) if 0 <= i + by < length]
    return lax.ppermute(x, axis, pairs)


def passed_round(x, even_by, odd_by):
    groups, points = lax.axis_size("energy"), lax.axis_size("mom")
    pairs = []
    for group in range(groups):
        by = even_by if group % 2 == 0 else odd_by
        for point in range(points):
            pairs.append((group * points + point, group * points + (point + by) % points))
    return lax.ppermute(x, ("energy", "mom"), pairs)


def after(x, *results):
    return lax.optimization_barrier((x, *results))[0]


def even_group():
    return lax.rem(lax.axis_index("energy"), 2) == 0


def products(blocks, coupling):
    lefts = [
        jnp.dot(coupling, block, preferred_element_type=jnp.float32).astype(jnp.bfloat16)
        for block in blocks
    ]
    return [jnp.dot(left, coupling, preferred_element_type=jnp.float32) for left in lefts]


def load(place, even, part, back=0):
    first, second, at = place
    if first is second:
        return first[at - back, part]
    return jnp.where(even, first[at - back, part], second[at - back, part])


def terms(energy, offset, shift, coupling, phonon, slots, even):
    modes, size, _ = coupling.shape
    low, high = slots[energy - SMAX], slots[energy]
    real_sum, imag_sum = None, None
    for mode in range(modes):
        step = shift[mode, offset]
        if low[0] is high[0] and low[1] is high[1]:
            blocks = [load(high, even, part, step) for part in range(2)]
        else:
            blocks = [
                jnp.where(step > 0, load(low, even, part), load(high, even, part))
                for part in range(2)
            ]
        first, second = products(blocks, coupling[mode])
        real = phonon[offset, pl.ds(2 * mode * size, size), :].astype(jnp.float32)
        imag = phonon[offset, pl.ds((2 * mode + 1) * size, size), :].astype(jnp.float32)
        real_term = first * real - second * imag
        imag_term = first * imag + second * real
        real_sum = real_term if real_sum is None else real_sum + real_term
        imag_sum = imag_term if imag_sum is None else imag_sum + imag_term
    return real_sum, imag_sum


class Operands:
    def __init__(self):
        self.arrays = []

    def add(self, array):
        for n, other in enumerate(self.arrays):
            if other is array:
                return n
        self.arrays.append(array)
        return len(self.arrays) - 1

    def place(self, place):
        return (self.add(place[0]), self.add(place[1]), place[2])

    def slots(self, slots, energies):
        used = {slot for energy in energies for slot in (energy - SMAX, energy)}
        return {slot: self.place(slots[slot]) for slot in slots if slot in used}


def at_refs(refs, place):
    return (refs[place[0]], refs[place[1]], place[2])


def estimate(coupling, energies):
    modes, size, _ = coupling.shape
    flops = 128 * energies * modes * size**3
    return pl.CostEstimate(flops=flops, bytes_accessed=1 << 24, transcendentals=0)


def sums_call(energies, sources, args, like, dtype, raw=None, start=None):
    _, parts, size, _ = like.shape
    count = len(energies)
    operands = Operands()
    layout = [(offset, operands.slots(slots, energies)) for offset, slots in sources]
    source = operands.add(like) if raw is not None else None
    begin = operands.add(start) if start is not None else None

    def kernel(shift, coupling, phonon, *refs):
        out = refs[-1]
        even = even_group()

        def sums():
            for at, energy in enumerate(energies):
                for n, (offset, slots) in enumerate(layout):
                    slots = {slot: at_refs(refs, place) for slot, place in slots.items()}
                    real, imag = terms(energy, offset, shift, coupling, phonon, slots, even)
                    if n > 0:
                        real, imag = real + out[at, 0], imag + out[at, 1]
                    elif begin is not None:
                        real, imag = real + refs[begin][energy, 0], imag + refs[begin][energy, 1]
                    out[at, 0] = real.astype(out.dtype)
                    out[at, 1] = imag.astype(out.dtype)

        if raw is None:
            sums()
        else:
            first, on_even = raw
            sends_raw = even if on_even else jnp.logical_not(even)

            @pl.when(sends_raw)
            def _():
                out[...] = refs[source][first : first + count]

            @pl.when(jnp.logical_not(sends_raw))
            def _():
                sums()

    return pl.pallas_call(
        kernel,
        out_shape=jax.ShapeDtypeStruct((count, parts, size, size), dtype),
        in_specs=[SMEM] + [VMEM] * (2 + len(operands.arrays)),
        out_specs=VMEM,
        compiler_params=pltpu.CompilerParams(vmem_limit_bytes=LIMIT),
        cost_estimate=estimate(args[1], count * len(sources)),
    )(*args, *operands.arrays)


def early_call(energies, offset, args, like):
    shift, coupling, phonon = args
    _, parts, size, _ = like.shape
    count, first = len(energies), energies[0] - SMAX

    def kernel(shift_hbm, coupling_hbm, phonon_hbm, own_hbm, out, *scratch):
        shift, coupling, phonon, own, sems = scratch
        pairs = [(own_hbm.at[pl.ds(first, count + SMAX)], own), (shift_hbm, shift)]
        pairs += [(coupling_hbm, coupling), (phonon_hbm.at[offset], phonon.at[offset])]
        copies = [pltpu.make_async_copy(*pair, sems.at[n]) for n, pair in enumerate(pairs)]
        even = even_group()
        copies[0].start()

        @pl.when(even)
        def _():
            copies[0].wait()
            out[...] = own[:count]

        @pl.when(jnp.logical_not(even))
        def _():
            for copy in copies[1:]:
                copy.start()
            for copy in copies:
                copy.wait()
            slots = {first + n: (own, own, n) for n in range(count + SMAX)}
            for at, energy in enumerate(energies):
                real, imag = terms(energy, offset, shift, coupling, phonon, slots, even)
                out[at, 0] = real.astype(out.dtype)
                out[at, 1] = imag.astype(out.dtype)

    return pl.pallas_call(
        kernel,
        out_shape=jax.ShapeDtypeStruct((count, parts, size, size), like.dtype),
        in_specs=[HBM] * 4,
        out_specs=VMEM,
        scratch_shapes=[
            pltpu.SMEM(shift.shape, shift.dtype),
            pltpu.VMEM(coupling.shape, coupling.dtype),
            pltpu.VMEM(phonon.shape, phonon.dtype),
            pltpu.VMEM((count + SMAX, parts, size, size), like.dtype),
            pltpu.SemaphoreType.DMA((4,)),
        ],
        compiler_params=pltpu.CompilerParams(vmem_limit_bytes=60 * 1024 * 1024),
        cost_estimate=estimate(coupling, count),
    )(shift, coupling, phonon, like)


def finish_call(energies, whole, total, sources, pieces, args, out=None):
    _, parts, size, _ = whole
    operands = Operands()
    base = operands.add(total)
    layout = [(offset, operands.slots(slots, energies)) for offset, slots in sources]
    added = {energy: [operands.place(p) for p in pieces[energy]] for energy in energies}

    def kernel(*refs):
        shift, coupling, phonon = refs[: len(args)] if args else (None,) * 3
        refs = refs[len(args) :]
        even = even_group()
        for at, energy in enumerate(energies):

            @pl.when(pl.program_id(0) == at)
            def _():
                row = energy if total.shape[0] == whole[0] else at
                results = [refs[base][row, part] for part in range(2)]
                for offset, slots in layout:
                    slots = {slot: at_refs(refs, place) for slot, place in slots.items()}
                    found = terms(energy, offset, shift, coupling, phonon, slots, even)
                    results = [result + term for result, term in zip(results, found)]
                for part in range(2):
                    for place in added[energy]:
                        piece = load(at_refs(refs, place), even, part)
                        results[part] = results[part] + piece.astype(jnp.float32)
                    refs[-1][0, part] = results[part].astype(jnp.bfloat16)

    arrays = [*args, *operands.arrays]
    specs = [SMEM] * min(len(args), 1) + [VMEM] * (len(arrays) - min(len(args), 1))
    aliases = {}
    if out is not None:
        aliases = {len(arrays): 0}
        arrays.append(out)
        specs.append(pl.BlockSpec(memory_space=pl.ANY))
    first = energies[0]
    return pl.pallas_call(
        kernel,
        grid=(len(energies),),
        out_shape=jax.ShapeDtypeStruct(whole, jnp.bfloat16),
        in_specs=specs,
        out_specs=pl.BlockSpec((1, parts, size, size), lambda i: (i + first, 0, 0, 0)),
        input_output_aliases=aliases,
        compiler_params=pltpu.CompilerParams(vmem_limit_bytes=LIMIT),
        cost_estimate=pl.CostEstimate(flops=1 << 33, bytes_accessed=1 << 24, transcendentals=0),
    )(*arrays)


def body(green, coupling, phonon, shift):
    own = green[0, 0]
    whole = own.shape
    last = whole[0] - 1
    offsets = phonon.shape[0]
    radius = (offsets - 1) // 2
    ups = range(1, radius + 1)
    args = (shift.T, coupling, phonon)
    high = tuple(range(2, last + 1))

    def own_slots(block, below=None):
        slots = {energy: (block, block, energy) for energy in range(last + 1)}
        if below is not None:
            slots[-1] = (below, below, 0)
        return slots

    def send(energies, raw, *results, below=None, early=False):
        block = after(own, *results)
        made, arrived = {}, {}
        for q in ups:
            sources = [(radius - q, own_slots(block, below))]
            if early:
                made[q] = early_call(energies, radius - q, args, block)
            else:
                made[q] = sums_call(energies, sources, args, block, jnp.bfloat16, raw)
            ways = (-q, -q) if raw is None else (q, -q) if raw[1] else (-q, q)
            arrived[q] = passed_round(made[q], *ways)
        return list(made.values()), arrived

    own_top = own[last:]
    tops = {q: passed_round(own_top, q, q) for q in ups}
    made, high_1 = send(high, (1, True), own_top, early=True)
    below = passed_along(after(own_top, *made), "energy", 1)
    made, high_2 = send(high, (1, False), *made)
    own_total = sums_call(
        tuple(range(last + 1)),
        [(radius, own_slots(after(own, *made), below))],
        args,
        own,
        jnp.float32,
    )
    made, low_1 = send((1,), (0, True), *made, *tops.values())
    belows = {q: passed_along(after(tops[q], *made), "energy", 1) for q in ups}
    made, low_2 = send((1,), (0, False), *made, *high_1.values())
    made, lowest = send((0,), None, *made, *high_2.values(), below=below)

    sources = []
    pieces = {energy: [] for energy in range(last + 1)}
    for q in ups:
        slots = {slot: (high_1[q], high_2[q], slot - 1) for slot in range(1, last)}
        slots[last] = (tops[q], tops[q], 0)
        slots[0] = (low_1[q], low_2[q], 0)
        slots[-1] = (belows[q], belows[q], 0)
        sources.append((radius + q, slots))
        for energy in high:
            pieces[energy].append((high_2[q], high_1[q], energy - 2))
        pieces[1].append((low_2[q], low_1[q], 0))
        pieces[0].append((lowest[q], lowest[q], 0))
    out = finish_call(high, whole, own_total, sources, pieces, args)
    out = finish_call((1,), whole, own_total, sources, pieces, args, out)
    bottom = sums_call((0,), sources, args, own, jnp.float32, start=own_total)
    out = finish_call((0,), whole, bottom, [], pieces, (), out)
    return out[None, None]


def solution(mesh):
    placed = (P("mom", "energy", None, None, None, None), P(), P(), P())
    return jax.shard_map(
        body,
        mesh=mesh,
        in_specs=placed,
        out_specs=P("mom", "energy", None, None, None, None),
        check_vma=False,
    )
```

```python
import jax
import jax.numpy as jnp
from jax import lax
from jax.experimental import pallas as pl
from jax.experimental.pallas import tpu as pltpu
from jax.sharding import PartitionSpec as P

SMAX = 1
HBM = pl.BlockSpec(memory_space=pltpu.HBM)
VMEM = pl.BlockSpec(memory_space=pltpu.VMEM)
SMEM = pl.BlockSpec(memory_space=pltpu.SMEM)
LIMIT = 32 * 1024 * 1024


def passed_along(x, axis, by):
    length = lax.axis_size(axis)
    pairs = [(i, i + by) for i in range(length) if 0 <= i + by < length]
    return lax.ppermute(x, axis, pairs)


def passed_round(x, even_by, odd_by):
    groups, points = lax.axis_size("energy"), lax.axis_size("mom")
    pairs = []
    for group in range(groups):
        by = even_by if group % 2 == 0 else odd_by
        for point in range(points):
            pairs.append((group * points + point, group * points + (point + by) % points))
    return lax.ppermute(x, ("energy", "mom"), pairs)


def after(x, *results):
    return lax.optimization_barrier((x, *results))[0]


def even_group():
    return lax.rem(lax.axis_index("energy"), 2) == 0


def products(blocks, coupling):
    lefts = [
        jnp.dot(coupling, block, preferred_element_type=jnp.float32).astype(jnp.bfloat16)
        for block in blocks
    ]
    return [jnp.dot(left, coupling, preferred_element_type=jnp.float32) for left in lefts]


def load(place, even, part, back=0):
    first, second, at = place
    if first is second:
        return first[at - back, part]
    return jnp.where(even, first[at - back, part], second[at - back, part])


def terms(energy, offset, shift, coupling, phonon, slots, even):
    modes = coupling.shape[0]
    low, high = slots[energy - SMAX], slots[energy]
    sums = None
    for mode in range(modes):
        step = shift[mode, offset]
        if low[0] is high[0] and low[1] is high[1]:
            blocks = [load(high, even, part, step) for part in range(2)]
        else:
            blocks = [
                jnp.where(step > 0, load(low, even, part), load(high, even, part))
                for part in range(2)
            ]
        found = mode_terms(mode, offset, blocks, coupling, phonon)
        sums = found if sums is None else [x + y for x, y in zip(sums, found)]
    return sums


def mode_terms(mode, offset, blocks, coupling, phonon):
    size = coupling.shape[1]
    first, second = products(blocks, coupling[mode])
    real = phonon[offset, pl.ds(2 * mode * size, size), :].astype(jnp.float32)
    imag = phonon[offset, pl.ds((2 * mode + 1) * size, size), :].astype(jnp.float32)
    return [first * real - second * imag, first * imag + second * real]


def add_low(pair, sources, shift, coupling, phonon, even):
    for offset, place in sources:
        for mode in range(coupling.shape[0]):
            blocks = [load(place, even, part) for part in range(2)]
            found = mode_terms(mode, offset, blocks, coupling, phonon)
            step = shift[mode, offset]
            pair[step, 0] += found[0]
            pair[step, 1] += found[1]


def add_edges(pair, sources, shift, coupling, phonon, even):
    for offset, below, above in sources:
        for mode in range(coupling.shape[0]):
            step = shift[mode, offset]
            blocks = [
                jnp.where(step > 0, load(below, even, part), load(above, even, part))
                for part in range(2)
            ]
            found = mode_terms(mode, offset, blocks, coupling, phonon)
            pair[1 - step, 0] += found[0]
            pair[1 - step, 1] += found[1]


class Operands:
    def __init__(self):
        self.arrays = []

    def add(self, array):
        for n, other in enumerate(self.arrays):
            if other is array:
                return n
        self.arrays.append(array)
        return len(self.arrays) - 1

    def place(self, place):
        return (self.add(place[0]), self.add(place[1]), place[2])

    def slots(self, slots, energies):
        used = {slot for energy in energies for slot in (energy - SMAX, energy)}
        return {slot: self.place(slots[slot]) for slot in slots if slot in used}


def at_refs(refs, place):
    return (refs[place[0]], refs[place[1]], place[2])


def estimate(coupling, energies):
    modes, size, _ = coupling.shape
    flops = 128 * energies * modes * size**3
    return pl.CostEstimate(flops=flops, bytes_accessed=1 << 24, transcendentals=0)


def sums_call(energies, sources, args, like, dtype, raw=None):
    _, parts, size, _ = like.shape
    count = len(energies)
    operands = Operands()
    layout = [(offset, operands.slots(slots, energies)) for offset, slots in sources]
    source = operands.add(like) if raw is not None else None

    def kernel(shift, coupling, phonon, *refs):
        out = refs[-1]
        even = even_group()

        def sums():
            for at, energy in enumerate(energies):
                for n, (offset, slots) in enumerate(layout):
                    slots = {slot: at_refs(refs, place) for slot, place in slots.items()}
                    real, imag = terms(energy, offset, shift, coupling, phonon, slots, even)
                    if n > 0:
                        real, imag = real + out[at, 0], imag + out[at, 1]
                    out[at, 0] = real.astype(out.dtype)
                    out[at, 1] = imag.astype(out.dtype)

        if raw is None:
            sums()
        else:
            first, on_even = raw
            sends_raw = even if on_even else jnp.logical_not(even)

            @pl.when(sends_raw)
            def _():
                out[...] = refs[source][first : first + count]

            @pl.when(jnp.logical_not(sends_raw))
            def _():
                sums()

    return pl.pallas_call(
        kernel,
        out_shape=jax.ShapeDtypeStruct((count, parts, size, size), dtype),
        in_specs=[SMEM] + [VMEM] * (2 + len(operands.arrays)),
        out_specs=VMEM,
        compiler_params=pltpu.CompilerParams(vmem_limit_bytes=LIMIT),
        cost_estimate=estimate(args[1], count * len(sources)),
    )(*args, *operands.arrays)


def early_call(energies, offset, args, like):
    shift, coupling, phonon = args
    _, parts, size, _ = like.shape
    count, first = len(energies), energies[0] - SMAX

    def kernel(shift_hbm, coupling_hbm, phonon_hbm, own_hbm, out, *scratch):
        shift, coupling, phonon, own, sems = scratch
        pairs = [(own_hbm.at[pl.ds(first, count + SMAX)], own), (shift_hbm, shift)]
        pairs += [(coupling_hbm, coupling), (phonon_hbm.at[offset], phonon.at[offset])]
        copies = [pltpu.make_async_copy(*pair, sems.at[n]) for n, pair in enumerate(pairs)]
        even = even_group()
        copies[0].start()

        @pl.when(even)
        def _():
            copies[0].wait()
            out[...] = own[:count]

        @pl.when(jnp.logical_not(even))
        def _():
            for copy in copies[1:]:
                copy.start()
            for copy in copies:
                copy.wait()
            slots = {first + n: (own, own, n) for n in range(count + SMAX)}
            for at, energy in enumerate(energies):
                real, imag = terms(energy, offset, shift, coupling, phonon, slots, even)
                out[at, 0] = real.astype(out.dtype)
                out[at, 1] = imag.astype(out.dtype)

    return pl.pallas_call(
        kernel,
        out_shape=jax.ShapeDtypeStruct((count, parts, size, size), like.dtype),
        in_specs=[HBM] * 4,
        out_specs=VMEM,
        scratch_shapes=[
            pltpu.SMEM(shift.shape, shift.dtype),
            pltpu.VMEM(coupling.shape, coupling.dtype),
            pltpu.VMEM(phonon.shape, phonon.dtype),
            pltpu.VMEM((count + SMAX, parts, size, size), like.dtype),
            pltpu.SemaphoreType.DMA((4,)),
        ],
        compiler_params=pltpu.CompilerParams(vmem_limit_bytes=60 * 1024 * 1024),
        cost_estimate=estimate(coupling, count),
    )(shift, coupling, phonon, like)


def pair_call(pair, sources, args, on_even):
    operands = Operands()
    layout = [(offset, *[operands.place(place) for place in places]) for offset, *places in sources]

    def kernel(shift, coupling, phonon, pair_ref, *refs):
        out = refs[-1]
        even = even_group()
        out[...] = pair_ref[...]
        found = [(offset, *[at_refs(refs, p) for p in places]) for offset, *places in layout]
        if on_even:

            @pl.when(even)
            def _():
                add_low(out, found, shift, coupling, phonon, even)

        else:
            add_edges(out, found, shift, coupling, phonon, even)

    return pl.pallas_call(
        kernel,
        out_shape=jax.ShapeDtypeStruct(pair.shape, pair.dtype),
        in_specs=[SMEM] + [VMEM] * (len(args) + len(operands.arrays)),
        out_specs=VMEM,
        compiler_params=pltpu.CompilerParams(vmem_limit_bytes=LIMIT),
        cost_estimate=estimate(args[1], 1),
    )(*args, pair, *operands.arrays)


def second_call(pair, sources, pieces, args, out):
    _, parts, size, _ = out.shape
    operands = Operands()
    layout = [(offset, operands.place(place)) for offset, place in sources]
    added = [operands.place(place) for place in pieces]

    def kernel(shift, coupling, phonon, pair_ref, *refs):
        out_ref, bottom, sums = refs[-3:]
        even = even_group()
        sums[...] = pair_ref[...]

        @pl.when(jnp.logical_not(even))
        def _():
            found = [(offset, at_refs(refs, place)) for offset, place in layout]
            add_low(sums, found, shift, coupling, phonon, even)

        bottom[0] = sums[0]
        for part in range(2):
            result = sums[1, part]
            for place in added:
                result = result + load(at_refs(refs, place), even, part).astype(jnp.float32)
            out_ref[0, part] = result.astype(out_ref.dtype)

    arrays = [*args, pair, *operands.arrays, out]
    return pl.pallas_call(
        kernel,
        grid=(1,),
        out_shape=[
            jax.ShapeDtypeStruct(out.shape, out.dtype),
            jax.ShapeDtypeStruct((1, parts, size, size), pair.dtype),
        ],
        in_specs=[SMEM] + [VMEM] * (len(arrays) - 2) + [pl.BlockSpec(memory_space=pl.ANY)],
        out_specs=[pl.BlockSpec((1, parts, size, size), lambda i: (i + 1, 0, 0, 0)), VMEM],
        scratch_shapes=[pltpu.VMEM(pair.shape, pair.dtype)],
        input_output_aliases={len(arrays) - 1: 0},
        compiler_params=pltpu.CompilerParams(vmem_limit_bytes=LIMIT),
        cost_estimate=pl.CostEstimate(flops=1 << 33, bytes_accessed=1 << 24, transcendentals=0),
    )(*arrays)


def finish_call(energies, whole, total, sources, pieces, args, out=None):
    _, parts, size, _ = whole
    operands = Operands()
    base = operands.add(total)
    layout = [(offset, operands.slots(slots, energies)) for offset, slots in sources]
    added = {energy: [operands.place(p) for p in pieces[energy]] for energy in energies}

    def kernel(*refs):
        shift, coupling, phonon = refs[: len(args)] if args else (None,) * 3
        refs = refs[len(args) :]
        even = even_group()
        for at, energy in enumerate(energies):

            @pl.when(pl.program_id(0) == at)
            def _():
                results = [refs[base][at, part] for part in range(2)]
                for offset, slots in layout:
                    slots = {slot: at_refs(refs, place) for slot, place in slots.items()}
                    found = terms(energy, offset, shift, coupling, phonon, slots, even)
                    results = [result + term for result, term in zip(results, found)]
                for part in range(2):
                    for place in added[energy]:
                        piece = load(at_refs(refs, place), even, part)
                        results[part] = results[part] + piece.astype(jnp.float32)
                    refs[-1][0, part] = results[part].astype(jnp.bfloat16)

    arrays = [*args, *operands.arrays]
    specs = [SMEM] * min(len(args), 1) + [VMEM] * (len(arrays) - min(len(args), 1))
    aliases = {}
    if out is not None:
        aliases = {len(arrays): 0}
        arrays.append(out)
        specs.append(pl.BlockSpec(memory_space=pl.ANY))
    first = energies[0]
    return pl.pallas_call(
        kernel,
        grid=(len(energies),),
        out_shape=jax.ShapeDtypeStruct(whole, jnp.bfloat16),
        in_specs=specs,
        out_specs=pl.BlockSpec((1, parts, size, size), lambda i: (i + first, 0, 0, 0)),
        input_output_aliases=aliases,
        compiler_params=pltpu.CompilerParams(vmem_limit_bytes=LIMIT),
        cost_estimate=pl.CostEstimate(flops=1 << 33, bytes_accessed=1 << 24, transcendentals=0),
    )(*arrays)


def body(green, coupling, phonon, shift):
    own = green[0, 0]
    whole = own.shape
    last = whole[0] - 1
    offsets = phonon.shape[0]
    radius = (offsets - 1) // 2
    ups = range(1, radius + 1)
    args = (shift.T, coupling, phonon)
    high = tuple(range(2, last + 1))

    def own_slots(block, below=None):
        slots = {energy: (block, block, energy) for energy in range(last + 1)}
        if below is not None:
            slots[-1] = (below, below, 0)
        return slots

    def send(energies, raw, *results, below=None, early=False):
        block = after(own, *results)
        made, arrived = {}, {}
        for q in ups:
            sources = [(radius - q, own_slots(block, below))]
            if early:
                made[q] = early_call(energies, radius - q, args, block)
            else:
                made[q] = sums_call(energies, sources, args, block, jnp.bfloat16, raw)
            ways = (-q, -q) if raw is None else (q, -q) if raw[1] else (-q, q)
            arrived[q] = passed_round(made[q], *ways)
        return list(made.values()), arrived

    own_top = own[last:]
    tops = {q: passed_round(own_top, q, q) for q in ups}
    made, high_1 = send(high, (1, True), own_top, early=True)
    below = passed_along(after(own_top, *made), "energy", 1)
    made, high_2 = send(high, (1, False), *made)
    block = after(own, *made)
    own_high = sums_call(high, [(radius, own_slots(block))], args, own, jnp.float32)
    pair = sums_call((0, 1), [(radius, own_slots(block, below))], args, own, jnp.float32)
    made, low_1 = send((1,), (0, True), *made, *tops.values())
    belows = {q: passed_along(after(tops[q], *made), "energy", 1) for q in ups}
    made, low_2 = send((1,), (0, False), *made, *high_1.values())
    made, lowest = send((0,), None, *made, *high_2.values(), below=below)

    sources = []
    pieces = {energy: [] for energy in range(last + 1)}
    for q in ups:
        slots = {slot: (high_1[q], high_2[q], slot - 1) for slot in range(1, last)}
        slots[last] = (tops[q], tops[q], 0)
        slots[0] = (low_1[q], low_2[q], 0)
        slots[-1] = (belows[q], belows[q], 0)
        sources.append((radius + q, slots))
        for energy in high:
            pieces[energy].append((high_2[q], high_1[q], energy - 2))
        pieces[1].append((low_2[q], low_1[q], 0))
        pieces[0].append((lowest[q], lowest[q], 0))
    out = finish_call(high, whole, own_high, sources, pieces, args)
    edges = [(offset, slots[-1], slots[1]) for offset, slots in sources]
    lows = [(offset, (low_1[q], low_1[q], 0)) for q, (offset, _) in zip(ups, sources)]
    pair = pair_call(pair, edges, args, on_even=False)
    pair = pair_call(pair, lows, args, on_even=True)
    lows = [(offset, (low_2[q], low_2[q], 0)) for q, (offset, _) in zip(ups, sources)]
    out, bottom = second_call(pair, lows, pieces[1], args, out)
    out = finish_call((0,), whole, bottom, [], pieces, (), out)
    return out[None, None]


def solution(mesh):
    placed = (P("mom", "energy", None, None, None, None), P(), P(), P())
    return jax.shard_map(
        body,
        mesh=mesh,
        in_specs=placed,
        out_specs=P("mom", "energy", None, None, None, None),
        check_vma=False,
    )
```

```python
import jax
import jax.numpy as jnp
from jax import lax
from jax.experimental import pallas as pl
from jax.experimental.pallas import tpu as pltpu
from jax.sharding import PartitionSpec as P

SMAX = 1
HBM = pl.BlockSpec(memory_space=pltpu.HBM)
VMEM = pl.BlockSpec(memory_space=pltpu.VMEM)
SMEM = pl.BlockSpec(memory_space=pltpu.SMEM)
LIMIT = 32 * 1024 * 1024


def passed_along(x, axis, by):
    length = lax.axis_size(axis)
    pairs = [(i, i + by) for i in range(length) if 0 <= i + by < length]
    return lax.ppermute(x, axis, pairs)


def passed_round(x, even_by, odd_by):
    groups, points = lax.axis_size("energy"), lax.axis_size("mom")
    pairs = []
    for group in range(groups):
        by = even_by if group % 2 == 0 else odd_by
        for point in range(points):
            pairs.append((group * points + point, group * points + (point + by) % points))
    return lax.ppermute(x, ("energy", "mom"), pairs)


def after(x, *results):
    return lax.optimization_barrier((x, *results))[0]


def even_group():
    return lax.rem(lax.axis_index("energy"), 2) == 0


def products(blocks, coupling):
    lefts = [
        jnp.dot(coupling, block, preferred_element_type=jnp.float32).astype(jnp.bfloat16)
        for block in blocks
    ]
    return [jnp.dot(left, coupling, preferred_element_type=jnp.float32) for left in lefts]


def load(place, even, part, back=0):
    first, second, at = place
    if first is second:
        return first[at - back, part]
    return jnp.where(even, first[at - back, part], second[at - back, part])


def terms(energy, offset, shift, coupling, phonon, slots, even):
    modes = coupling.shape[0]
    low, high = slots[energy - SMAX], slots[energy]
    sums = None
    for mode in range(modes):
        step = shift[mode, offset]
        if low[0] is high[0] and low[1] is high[1]:
            blocks = [load(high, even, part, step) for part in range(2)]
        else:
            blocks = [
                jnp.where(step > 0, load(low, even, part), load(high, even, part))
                for part in range(2)
            ]
        found = mode_terms(mode, offset, blocks, coupling, phonon)
        sums = found if sums is None else [x + y for x, y in zip(sums, found)]
    return sums


def mode_terms(mode, offset, blocks, coupling, phonon):
    size = coupling.shape[1]
    first, second = products(blocks, coupling[mode])
    real = phonon[offset, pl.ds(2 * mode * size, size), :].astype(jnp.float32)
    imag = phonon[offset, pl.ds((2 * mode + 1) * size, size), :].astype(jnp.float32)
    return [first * real - second * imag, first * imag + second * real]


def add_low(pair, sources, shift, coupling, phonon, even):
    for offset, place in sources:
        for mode in range(coupling.shape[0]):
            blocks = [load(place, even, part) for part in range(2)]
            found = mode_terms(mode, offset, blocks, coupling, phonon)
            step = shift[mode, offset]
            pair[step, 0] += found[0]
            pair[step, 1] += found[1]


def add_edges(pair, sources, shift, coupling, phonon, even):
    for offset, below, above in sources:
        for mode in range(coupling.shape[0]):
            step = shift[mode, offset]
            blocks = [
                jnp.where(step > 0, load(below, even, part), load(above, even, part))
                for part in range(2)
            ]
            found = mode_terms(mode, offset, blocks, coupling, phonon)
            pair[1 - step, 0] += found[0]
            pair[1 - step, 1] += found[1]


class Operands:
    def __init__(self):
        self.arrays = []

    def add(self, array):
        for n, other in enumerate(self.arrays):
            if other is array:
                return n
        self.arrays.append(array)
        return len(self.arrays) - 1

    def place(self, place):
        return (self.add(place[0]), self.add(place[1]), place[2])

    def slots(self, slots, energies):
        used = {slot for energy in energies for slot in (energy - SMAX, energy)}
        return {slot: self.place(slots[slot]) for slot in slots if slot in used}


def at_refs(refs, place):
    return (refs[place[0]], refs[place[1]], place[2])


def estimate(coupling, energies):
    modes, size, _ = coupling.shape
    flops = 128 * energies * modes * size**3
    return pl.CostEstimate(flops=flops, bytes_accessed=1 << 24, transcendentals=0)


def sums_call(energies, sources, args, like, dtype, raw=None):
    _, parts, size, _ = like.shape
    count = len(energies)
    operands = Operands()
    layout = [(offset, operands.slots(slots, energies)) for offset, slots in sources]
    source = operands.add(like) if raw is not None else None

    def kernel(shift, coupling, phonon, *refs):
        out = refs[-1]
        even = even_group()

        def sums():
            for at, energy in enumerate(energies):
                for n, (offset, slots) in enumerate(layout):
                    slots = {slot: at_refs(refs, place) for slot, place in slots.items()}
                    real, imag = terms(energy, offset, shift, coupling, phonon, slots, even)
                    if n > 0:
                        real, imag = real + out[at, 0], imag + out[at, 1]
                    out[at, 0] = real.astype(out.dtype)
                    out[at, 1] = imag.astype(out.dtype)

        if raw is None:
            sums()
        else:
            first, on_even = raw
            sends_raw = even if on_even else jnp.logical_not(even)

            @pl.when(sends_raw)
            def _():
                out[...] = refs[source][first : first + count]

            @pl.when(jnp.logical_not(sends_raw))
            def _():
                sums()

    return pl.pallas_call(
        kernel,
        out_shape=jax.ShapeDtypeStruct((count, parts, size, size), dtype),
        in_specs=[SMEM] + [VMEM] * (2 + len(operands.arrays)),
        out_specs=VMEM,
        compiler_params=pltpu.CompilerParams(vmem_limit_bytes=LIMIT),
        cost_estimate=estimate(args[1], count * len(sources)),
    )(*args, *operands.arrays)


def early_call(energies, offset, args, like):
    shift, coupling, phonon = args
    _, parts, size, _ = like.shape
    count, first = len(energies), energies[0] - SMAX

    def kernel(shift_hbm, coupling_hbm, phonon_hbm, own_hbm, out, *scratch):
        shift, coupling, phonon, own, sems = scratch
        pairs = [(own_hbm.at[pl.ds(first, count + SMAX)], own), (shift_hbm, shift)]
        pairs += [(coupling_hbm, coupling), (phonon_hbm.at[offset], phonon.at[offset])]
        copies = [pltpu.make_async_copy(*pair, sems.at[n]) for n, pair in enumerate(pairs)]
        even = even_group()
        copies[0].start()

        @pl.when(even)
        def _():
            copies[0].wait()
            out[...] = own[:count]

        @pl.when(jnp.logical_not(even))
        def _():
            for copy in copies[1:]:
                copy.start()
            for copy in copies:
                copy.wait()
            slots = {first + n: (own, own, n) for n in range(count + SMAX)}
            for at, energy in enumerate(energies):
                real, imag = terms(energy, offset, shift, coupling, phonon, slots, even)
                out[at, 0] = real.astype(out.dtype)
                out[at, 1] = imag.astype(out.dtype)

    return pl.pallas_call(
        kernel,
        out_shape=jax.ShapeDtypeStruct((count, parts, size, size), like.dtype),
        in_specs=[HBM] * 4,
        out_specs=VMEM,
        scratch_shapes=[
            pltpu.SMEM(shift.shape, shift.dtype),
            pltpu.VMEM(coupling.shape, coupling.dtype),
            pltpu.VMEM(phonon.shape, phonon.dtype),
            pltpu.VMEM((count + SMAX, parts, size, size), like.dtype),
            pltpu.SemaphoreType.DMA((4,)),
        ],
        compiler_params=pltpu.CompilerParams(vmem_limit_bytes=60 * 1024 * 1024),
        cost_estimate=estimate(coupling, count),
    )(shift, coupling, phonon, like)


def pair_call(pair, sources, args, on_even):
    operands = Operands()
    layout = [(offset, *[operands.place(place) for place in places]) for offset, *places in sources]

    def kernel(shift, coupling, phonon, pair_ref, *refs):
        out = refs[-1]
        even = even_group()
        out[...] = pair_ref[...]
        found = [(offset, *[at_refs(refs, p) for p in places]) for offset, *places in layout]
        if on_even:

            @pl.when(even)
            def _():
                add_low(out, found, shift, coupling, phonon, even)

        else:
            add_edges(out, found, shift, coupling, phonon, even)

    return pl.pallas_call(
        kernel,
        out_shape=jax.ShapeDtypeStruct(pair.shape, pair.dtype),
        in_specs=[SMEM] + [VMEM] * (len(args) + len(operands.arrays)),
        out_specs=VMEM,
        compiler_params=pltpu.CompilerParams(vmem_limit_bytes=LIMIT),
        cost_estimate=estimate(args[1], 1),
    )(*args, pair, *operands.arrays)


def last_call(pair, sources, pieces, args, out):
    _, parts, size, _ = out.shape
    operands = Operands()
    layout = [(offset, operands.place(place)) for offset, place in sources]
    added = [[operands.place(place) for place in pieces[energy]] for energy in (0, 1)]

    def kernel(shift, coupling, phonon, pair_ref, *refs):
        out_ref, sums = refs[-2:]
        even = even_group()
        odd_start = jnp.logical_and(pl.program_id(0) == 0, jnp.logical_not(even))

        @pl.when(odd_start)
        def _():
            sums[...] = pair_ref[...]
            found = [(offset, at_refs(refs, place)) for offset, place in layout]
            add_low(sums, found, shift, coupling, phonon, even)

        for energy in (1, 0):

            @pl.when(pl.program_id(0) == 1 - energy)
            def _():
                for part in range(2):
                    result = jnp.where(even, pair_ref[energy, part], sums[energy, part])
                    for place in added[energy]:
                        piece = load(at_refs(refs, place), even, part)
                        result = result + piece.astype(jnp.float32)
                    out_ref[0, part] = result.astype(out_ref.dtype)

    arrays = [*args, pair, *operands.arrays, out]
    return pl.pallas_call(
        kernel,
        grid=(2,),
        out_shape=jax.ShapeDtypeStruct(out.shape, out.dtype),
        in_specs=[SMEM] + [VMEM] * (len(arrays) - 2) + [pl.BlockSpec(memory_space=pl.ANY)],
        out_specs=pl.BlockSpec((1, parts, size, size), lambda i: (1 - i, 0, 0, 0)),
        scratch_shapes=[pltpu.VMEM(pair.shape, pair.dtype)],
        input_output_aliases={len(arrays) - 1: 0},
        compiler_params=pltpu.CompilerParams(vmem_limit_bytes=LIMIT),
        cost_estimate=pl.CostEstimate(flops=1 << 33, bytes_accessed=1 << 24, transcendentals=0),
    )(*arrays)


def finish_call(energies, whole, total, sources, pieces, args):
    _, parts, size, _ = whole
    operands = Operands()
    layout = [(offset, operands.slots(slots, energies)) for offset, slots in sources]
    added = [[operands.place(place) for place in pieces[energy]] for energy in energies]

    def kernel(shift, coupling, phonon, total_ref, *refs):
        even = even_group()
        for at, energy in enumerate(energies):

            @pl.when(pl.program_id(0) == at)
            def _():
                results = [total_ref[at, part] for part in range(2)]
                for offset, slots in layout:
                    slots = {slot: at_refs(refs, place) for slot, place in slots.items()}
                    found = terms(energy, offset, shift, coupling, phonon, slots, even)
                    results = [result + term for result, term in zip(results, found)]
                for part in range(2):
                    for place in added[at]:
                        piece = load(at_refs(refs, place), even, part)
                        results[part] = results[part] + piece.astype(jnp.float32)
                    refs[-1][0, part] = results[part].astype(jnp.bfloat16)

    arrays = [*args, total, *operands.arrays]
    first = energies[0]
    return pl.pallas_call(
        kernel,
        grid=(len(energies),),
        out_shape=jax.ShapeDtypeStruct(whole, jnp.bfloat16),
        in_specs=[SMEM] + [VMEM] * (len(arrays) - 1),
        out_specs=pl.BlockSpec((1, parts, size, size), lambda i: (i + first, 0, 0, 0)),
        compiler_params=pltpu.CompilerParams(vmem_limit_bytes=LIMIT),
        cost_estimate=pl.CostEstimate(flops=1 << 33, bytes_accessed=1 << 24, transcendentals=0),
    )(*arrays)


def body(green, coupling, phonon, shift):
    own = green[0, 0]
    whole = own.shape
    last = whole[0] - 1
    offsets = phonon.shape[0]
    radius = (offsets - 1) // 2
    ups = range(-1, -radius - 1, -1)
    args = (shift.T, coupling, phonon)
    high = tuple(range(2, last + 1))

    def own_slots(block, below=None):
        slots = {energy: (block, block, energy) for energy in range(last + 1)}
        if below is not None:
            slots[-1] = (below, below, 0)
        return slots

    def send(energies, raw, *results, below=None, early=False):
        block = after(own, *results)
        made, arrived = {}, {}
        for q in ups:
            sources = [(radius - q, own_slots(block, below))]
            if early:
                made[q] = early_call(energies, radius - q, args, block)
            else:
                made[q] = sums_call(energies, sources, args, block, jnp.bfloat16, raw)
            ways = (-q, -q) if raw is None else (q, -q) if raw[1] else (-q, q)
            arrived[q] = passed_round(made[q], *ways)
        return list(made.values()), arrived

    own_top = own[last:]
    tops = {q: passed_round(own_top, q, q) for q in ups}
    made, high_1 = send(high, (1, True), own_top, early=True)
    below = passed_along(after(own_top, *made), "energy", 1)
    made, high_2 = send(high, (1, False), *made)
    block = after(own, *made)
    own_high = sums_call(high, [(radius, own_slots(block))], args, own, jnp.float32)
    pair = sums_call((0, 1), [(radius, own_slots(block, below))], args, own, jnp.float32)
    made, low_1 = send((1,), (0, True), *made, *tops.values())
    belows = {q: passed_along(after(tops[q], *made), "energy", 1) for q in ups}
    made, low_2 = send((1,), (0, False), *made, *high_1.values())
    made, lowest = send((0,), None, *made, *high_2.values(), below=below)

    sources = []
    pieces = {energy: [] for energy in range(last + 1)}
    for q in ups:
        slots = {slot: (high_1[q], high_2[q], slot - 1) for slot in range(1, last)}
        slots[last] = (tops[q], tops[q], 0)
        slots[0] = (low_1[q], low_2[q], 0)
        slots[-1] = (belows[q], belows[q], 0)
        sources.append((radius + q, slots))
        for energy in high:
            pieces[energy].append((high_2[q], high_1[q], energy - 2))
        pieces[1].append((low_2[q], low_1[q], 0))
        pieces[0].append((lowest[q], lowest[q], 0))
    out = finish_call(high, whole, own_high, sources, pieces, args)
    edges = [(offset, slots[-1], slots[1]) for offset, slots in sources]
    lows = [(offset, (low_1[q], low_1[q], 0)) for q, (offset, _) in zip(ups, sources)]
    pair = pair_call(pair, edges, args, on_even=False)
    pair = pair_call(pair, lows, args, on_even=True)
    lows = [(offset, (low_2[q], low_2[q], 0)) for q, (offset, _) in zip(ups, sources)]
    out = last_call(pair, lows, pieces, args, out)
    return out[None, None]


def solution(mesh):
    placed = (P("mom", "energy", None, None, None, None), P(), P(), P())
    return jax.shard_map(
        body,
        mesh=mesh,
        in_specs=placed,
        out_specs=P("mom", "energy", None, None, None, None),
        check_vma=False,
    )
```

```python
import jax
import jax.numpy as jnp
from jax import lax
from jax.experimental import pallas as pl
from jax.experimental.pallas import tpu as pltpu
from jax.sharding import PartitionSpec as P

SMAX = 1
HBM = pl.BlockSpec(memory_space=pltpu.HBM)
VMEM = pl.BlockSpec(memory_space=pltpu.VMEM)
SMEM = pl.BlockSpec(memory_space=pltpu.SMEM)
LIMIT = 32 * 1024 * 1024


def passed_along(x, axis, by):
    length = lax.axis_size(axis)
    pairs = [(i, i + by) for i in range(length) if 0 <= i + by < length]
    return lax.ppermute(x, axis, pairs)


def passed_round(x, even_by, odd_by):
    groups, points = lax.axis_size("energy"), lax.axis_size("mom")
    pairs = []
    for group in range(groups):
        by = even_by if group % 2 == 0 else odd_by
        for point in range(points):
            pairs.append((group * points + point, group * points + (point + by) % points))
    return lax.ppermute(x, ("energy", "mom"), pairs)


def after(x, *results):
    return lax.optimization_barrier((x, *results))[0]


def even_group():
    return lax.rem(lax.axis_index("energy"), 2) == 0


def products(blocks, coupling):
    lefts = [
        jnp.dot(coupling, block, preferred_element_type=jnp.float32).astype(jnp.bfloat16)
        for block in blocks
    ]
    return [jnp.dot(left, coupling, preferred_element_type=jnp.float32) for left in lefts]


def load(place, even, part, back=0):
    first, second, at = place
    if first is second:
        return first[at - back, part]
    return jnp.where(even, first[at - back, part], second[at - back, part])


def terms(energy, offset, shift, coupling, phonon, slots, even):
    modes = coupling.shape[0]
    low, high = slots[energy - SMAX], slots[energy]
    sums = None
    for mode in range(modes):
        step = shift[mode, offset]
        if low[0] is high[0] and low[1] is high[1]:
            blocks = [load(high, even, part, step) for part in range(2)]
        else:
            blocks = [
                jnp.where(step > 0, load(low, even, part), load(high, even, part))
                for part in range(2)
            ]
        found = mode_terms(mode, offset, blocks, coupling, phonon)
        sums = found if sums is None else [x + y for x, y in zip(sums, found)]
    return sums


def mode_terms(mode, offset, blocks, coupling, phonon):
    size = coupling.shape[1]
    first, second = products(blocks, coupling[mode])
    real = phonon[offset, pl.ds(2 * mode * size, size), :].astype(jnp.float32)
    imag = phonon[offset, pl.ds((2 * mode + 1) * size, size), :].astype(jnp.float32)
    return [first * real - second * imag, first * imag + second * real]


def add_edges(pair, sources, shift, coupling, phonon, even):
    for offset, below, above in sources:
        for mode in range(coupling.shape[0]):
            step = shift[mode, offset]
            blocks = [
                jnp.where(step > 0, load(below, even, part), load(above, even, part))
                for part in range(2)
            ]
            found = mode_terms(mode, offset, blocks, coupling, phonon)
            pair[1 - step, 0] += found[0]
            pair[1 - step, 1] += found[1]


class Operands:
    def __init__(self):
        self.arrays = []

    def add(self, array):
        for n, other in enumerate(self.arrays):
            if other is array:
                return n
        self.arrays.append(array)
        return len(self.arrays) - 1

    def place(self, place):
        return (self.add(place[0]), self.add(place[1]), place[2])

    def slots(self, slots, energies):
        used = {slot for energy in energies for slot in (energy - SMAX, energy)}
        return {slot: self.place(slots[slot]) for slot in slots if slot in used}


def at_refs(refs, place):
    return (refs[place[0]], refs[place[1]], place[2])


def estimate(coupling, energies):
    modes, size, _ = coupling.shape
    flops = 128 * energies * modes * size**3
    return pl.CostEstimate(flops=flops, bytes_accessed=1 << 24, transcendentals=0)


def sums_call(energies, sources, args, like, dtype, raw=None):
    _, parts, size, _ = like.shape
    count = len(energies)
    operands = Operands()
    layout = [(offset, operands.slots(slots, energies)) for offset, slots in sources]
    source = operands.add(like) if raw is not None else None

    def kernel(shift, coupling, phonon, *refs):
        out = refs[-1]
        even = even_group()

        def sums():
            for at, energy in enumerate(energies):
                for n, (offset, slots) in enumerate(layout):
                    slots = {slot: at_refs(refs, place) for slot, place in slots.items()}
                    real, imag = terms(energy, offset, shift, coupling, phonon, slots, even)
                    if n > 0:
                        real, imag = real + out[at, 0], imag + out[at, 1]
                    out[at, 0] = real.astype(out.dtype)
                    out[at, 1] = imag.astype(out.dtype)

        if raw is None:
            sums()
        else:
            first, on_even = raw
            sends_raw = even if on_even else jnp.logical_not(even)

            @pl.when(sends_raw)
            def _():
                out[...] = refs[source][first : first + count]

            @pl.when(jnp.logical_not(sends_raw))
            def _():
                sums()

    return pl.pallas_call(
        kernel,
        out_shape=jax.ShapeDtypeStruct((count, parts, size, size), dtype),
        in_specs=[SMEM] + [VMEM] * (2 + len(operands.arrays)),
        out_specs=VMEM,
        compiler_params=pltpu.CompilerParams(vmem_limit_bytes=LIMIT),
        cost_estimate=estimate(args[1], count * len(sources)),
    )(*args, *operands.arrays)


def early_call(energies, offset, args, like):
    shift, coupling, phonon = args
    _, parts, size, _ = like.shape
    count, first = len(energies), energies[0] - SMAX

    def kernel(shift_hbm, coupling_hbm, phonon_hbm, own_hbm, out, *scratch):
        shift, coupling, phonon, own, sems = scratch
        pairs = [(own_hbm.at[pl.ds(first, count + SMAX)], own), (shift_hbm, shift)]
        pairs += [(coupling_hbm, coupling), (phonon_hbm.at[offset], phonon.at[offset])]
        copies = [pltpu.make_async_copy(*pair, sems.at[n]) for n, pair in enumerate(pairs)]
        even = even_group()
        copies[0].start()

        @pl.when(even)
        def _():
            copies[0].wait()
            out[...] = own[:count]

        @pl.when(jnp.logical_not(even))
        def _():
            for copy in copies[1:]:
                copy.start()
            for copy in copies:
                copy.wait()
            slots = {first + n: (own, own, n) for n in range(count + SMAX)}
            for at, energy in enumerate(energies):
                real, imag = terms(energy, offset, shift, coupling, phonon, slots, even)
                out[at, 0] = real.astype(out.dtype)
                out[at, 1] = imag.astype(out.dtype)

    return pl.pallas_call(
        kernel,
        out_shape=jax.ShapeDtypeStruct((count, parts, size, size), like.dtype),
        in_specs=[HBM] * 4,
        out_specs=VMEM,
        scratch_shapes=[
            pltpu.SMEM(shift.shape, shift.dtype),
            pltpu.VMEM(coupling.shape, coupling.dtype),
            pltpu.VMEM(phonon.shape, phonon.dtype),
            pltpu.VMEM((count + SMAX, parts, size, size), like.dtype),
            pltpu.SemaphoreType.DMA((4,)),
        ],
        compiler_params=pltpu.CompilerParams(vmem_limit_bytes=60 * 1024 * 1024),
        cost_estimate=estimate(coupling, count),
    )(shift, coupling, phonon, like)


def pair_call(pair, sources, args):
    operands = Operands()
    layout = [(offset, *[operands.place(place) for place in places]) for offset, *places in sources]

    def kernel(shift, coupling, phonon, pair_ref, *refs):
        out = refs[-1]
        out[...] = pair_ref[...]
        found = [(offset, *[at_refs(refs, p) for p in places]) for offset, *places in layout]
        add_edges(out, found, shift, coupling, phonon, even_group())

    return pl.pallas_call(
        kernel,
        out_shape=jax.ShapeDtypeStruct(pair.shape, pair.dtype),
        in_specs=[SMEM] + [VMEM] * (len(args) + len(operands.arrays)),
        out_specs=VMEM,
        compiler_params=pltpu.CompilerParams(vmem_limit_bytes=LIMIT),
        cost_estimate=estimate(args[1], 1),
    )(*args, pair, *operands.arrays)


def last_call(pair, sources, pieces, args, out):
    _, parts, size, _ = out.shape
    modes = args[1].shape[0]
    operands = Operands()
    layout = [(offset, operands.place(place)) for offset, place in sources]
    added = [[operands.place(place) for place in pieces[energy]] for energy in (0, 1)]

    def kernel(shift, coupling, phonon, pair_ref, *refs):
        out_ref, made, sems = refs[-3:]
        even = even_group()
        found = []
        for offset, place in layout:
            blocks = [load(at_refs(refs, place), even, part) for part in range(2)]
            for mode in range(modes):
                step = shift[mode, offset]
                found.append((step, mode_terms(mode, offset, blocks, coupling, phonon)))
        copies = []
        for energy in (1, 0):
            for part in range(2):
                result = pair_ref[energy, part]
                for place in added[energy]:
                    result = result + load(at_refs(refs, place), even, part).astype(jnp.float32)
                for step, term in found:
                    result = result + jnp.where(step == energy, term[part], 0.0)
                made[energy, part] = result.astype(made.dtype)
            copies.append(pltpu.make_async_copy(made.at[energy], out_ref.at[energy], sems.at[energy]))
            copies[-1].start()
        for copy in copies:
            copy.wait()

    arrays = [*args, pair, *operands.arrays, out]
    return pl.pallas_call(
        kernel,
        out_shape=jax.ShapeDtypeStruct(out.shape, out.dtype),
        in_specs=[SMEM] + [VMEM] * (len(arrays) - 2) + [pl.BlockSpec(memory_space=pl.ANY)],
        out_specs=pl.BlockSpec(memory_space=pl.ANY),
        scratch_shapes=[
            pltpu.VMEM((2, parts, size, size), out.dtype),
            pltpu.SemaphoreType.DMA((2,)),
        ],
        input_output_aliases={len(arrays) - 1: 0},
        compiler_params=pltpu.CompilerParams(vmem_limit_bytes=LIMIT),
        cost_estimate=pl.CostEstimate(flops=1 << 33, bytes_accessed=1 << 24, transcendentals=0),
    )(*arrays)


def finish_call(energies, whole, total, sources, pieces, args):
    _, parts, size, _ = whole
    operands = Operands()
    layout = [(offset, operands.slots(slots, energies)) for offset, slots in sources]
    added = [[operands.place(place) for place in pieces[energy]] for energy in energies]

    def kernel(shift, coupling, phonon, total_ref, *refs):
        even = even_group()
        for at, energy in enumerate(energies):

            @pl.when(pl.program_id(0) == at)
            def _():
                results = [total_ref[at, part] for part in range(2)]
                for offset, slots in layout:
                    slots = {slot: at_refs(refs, place) for slot, place in slots.items()}
                    found = terms(energy, offset, shift, coupling, phonon, slots, even)
                    results = [result + term for result, term in zip(results, found)]
                for part in range(2):
                    for place in added[at]:
                        piece = load(at_refs(refs, place), even, part)
                        results[part] = results[part] + piece.astype(jnp.float32)
                    refs[-1][0, part] = results[part].astype(jnp.bfloat16)

    arrays = [*args, total, *operands.arrays]
    first = energies[0]
    return pl.pallas_call(
        kernel,
        grid=(len(energies),),
        out_shape=jax.ShapeDtypeStruct(whole, jnp.bfloat16),
        in_specs=[SMEM] + [VMEM] * (len(arrays) - 1),
        out_specs=pl.BlockSpec((1, parts, size, size), lambda i: (i + first, 0, 0, 0)),
        compiler_params=pltpu.CompilerParams(vmem_limit_bytes=LIMIT),
        cost_estimate=pl.CostEstimate(flops=1 << 33, bytes_accessed=1 << 24, transcendentals=0),
    )(*arrays)


def body(green, coupling, phonon, shift):
    own = green[0, 0]
    whole = own.shape
    last = whole[0] - 1
    offsets = phonon.shape[0]
    radius = (offsets - 1) // 2
    ups = range(-1, -radius - 1, -1)
    args = (shift.T, coupling, phonon)
    high = tuple(range(2, last + 1))

    def own_slots(block, below=None):
        slots = {energy: (block, block, energy) for energy in range(last + 1)}
        if below is not None:
            slots[-1] = (below, below, 0)
        return slots

    def send(energies, raw, *results, below=None, early=False):
        block = after(own, *results)
        made, arrived = {}, {}
        for q in ups:
            sources = [(radius - q, own_slots(block, below))]
            if early:
                made[q] = early_call(energies, radius - q, args, block)
            else:
                made[q] = sums_call(energies, sources, args, block, jnp.bfloat16, raw)
            ways = (-q, -q) if raw is None else (q, -q) if raw[1] else (-q, q)
            arrived[q] = passed_round(made[q], *ways)
        return list(made.values()), arrived

    own_top = own[last:]
    tops = {q: passed_round(own_top, q, q) for q in ups}
    made, high_1 = send(high, (1, True), own_top, early=True)
    below = passed_along(after(own_top, *made), "energy", 1)
    made, high_2 = send(high, (1, False), *made)
    block = after(own, *made)
    own_high = sums_call(high, [(radius, own_slots(block))], args, own, jnp.float32)
    pair = sums_call((0, 1), [(radius, own_slots(block, below))], args, own, jnp.float32)
    made, second = send((1,), None, *made, *tops.values())
    belows = {q: passed_along(after(tops[q], *made), "energy", 1) for q in ups}
    made, first = send((0,), None, *made, *high_1.values(), below=below)
    low = after(own, *made, *high_2.values())[:1]
    lows = {q: passed_round(low, q, q) for q in ups}

    sources = []
    pieces = {energy: [] for energy in range(last + 1)}
    for q in ups:
        slots = {slot: (high_1[q], high_2[q], slot - 1) for slot in range(1, last)}
        slots[last] = (tops[q], tops[q], 0)
        slots[-1] = (belows[q], belows[q], 0)
        sources.append((radius + q, slots))
        for energy in high:
            pieces[energy].append((high_2[q], high_1[q], energy - 2))
        pieces[1].append((second[q], second[q], 0))
        pieces[0].append((first[q], first[q], 0))
    out = finish_call(high, whole, own_high, sources, pieces, args)
    edges = [(offset, slots[-1], slots[1]) for offset, slots in sources]
    pair = pair_call(pair, edges, args)
    lows = [(offset, (lows[q], lows[q], 0)) for q, (offset, _) in zip(ups, sources)]
    out = last_call(pair, lows, pieces, args, out)
    return out[None, None]


def solution(mesh):
    placed = (P("mom", "energy", None, None, None, None), P(), P(), P())
    return jax.shard_map(
        body,
        mesh=mesh,
        in_specs=placed,
        out_specs=P("mom", "energy", None, None, None, None),
        check_vma=False,
    )
```

```python
import jax
import jax.numpy as jnp
from jax import lax
from jax.experimental import pallas as pl
from jax.experimental.pallas import tpu as pltpu
from jax.sharding import PartitionSpec as P

SMAX = 1
VMEM = pl.BlockSpec(memory_space=pltpu.VMEM)
SMEM = pl.BlockSpec(memory_space=pltpu.SMEM)
LIMIT = 32 * 1024 * 1024


def passed_along(x, axis, by):
    length = lax.axis_size(axis)
    pairs = [(i, i + by) for i in range(length) if 0 <= i + by < length]
    return lax.ppermute(x, axis, pairs)


def passed_round(x, by):
    length = lax.axis_size("mom")
    return lax.ppermute(x, "mom", [(i, (i + by) % length) for i in range(length)])


def after(x, *results):
    return lax.optimization_barrier((x, *results))[0]


def products(blocks, coupling):
    lefts = [
        jnp.dot(coupling, block, preferred_element_type=jnp.float32).astype(jnp.bfloat16)
        for block in blocks
    ]
    return [jnp.dot(left, coupling, preferred_element_type=jnp.float32) for left in lefts]


def terms(energy, offset, shift, coupling, phonon, blocks, below):
    modes, size, _ = coupling.shape
    real_sum, imag_sum = None, None
    for mode in range(modes):
        step = shift[mode, offset]
        if energy == 0:
            used = [jnp.where(step > 0, below[0, part], blocks[0, part]) for part in range(2)]
        else:
            used = [blocks[energy - step, part] for part in range(2)]
        first, second = products(used, coupling[mode])
        real = phonon[offset, pl.ds(2 * mode * size, size), :].astype(jnp.float32)
        imag = phonon[offset, pl.ds((2 * mode + 1) * size, size), :].astype(jnp.float32)
        real_term = first * real - second * imag
        imag_term = first * imag + second * real
        real_sum = real_term if real_sum is None else real_sum + real_term
        imag_sum = imag_term if imag_sum is None else imag_sum + imag_term
    return real_sum, imag_sum


def estimate(coupling, energies):
    modes, size, _ = coupling.shape
    flops = 128 * energies * modes * size**3
    return pl.CostEstimate(flops=flops, bytes_accessed=1 << 24, transcendentals=0)


def sums_call(energies, offset, args, blocks, below, dtype, start=None):
    _, parts, size, _ = blocks.shape
    extra = [x for x in (below, start) if x is not None]

    def kernel(shift, coupling, phonon, blocks, *refs):
        out = refs[-1]
        below_ref = refs[0] if below is not None else None
        for at, energy in enumerate(energies):
            sums = terms(energy, offset, shift, coupling, phonon, blocks, below_ref)
            for part in range(2):
                total = sums[part]
                if start is not None:
                    total = total + refs[-2][at, part]
                out[at, part] = total.astype(out.dtype)

    return pl.pallas_call(
        kernel,
        out_shape=jax.ShapeDtypeStruct((len(energies), parts, size, size), dtype),
        in_specs=[SMEM] + [VMEM] * (3 + len(extra)),
        out_specs=VMEM,
        compiler_params=pltpu.CompilerParams(vmem_limit_bytes=LIMIT),
        cost_estimate=estimate(args[1], len(energies)),
    )(*args, blocks, *extra)


def finish_call(group, whole, total, pieces, out=None):
    _, parts, size, _ = whole
    first = group[0]

    def kernel(total_ref, *refs):
        at = pl.program_id(0)
        result = total_ref[at + max(first - 1, 0)]
        for piece in refs[: len(pieces)]:
            result = result + piece[at].astype(jnp.float32)
        refs[-1][0] = result.astype(jnp.bfloat16)

    arrays = [total, *pieces]
    specs = [VMEM] * len(arrays)
    aliases = {}
    if out is not None:
        aliases = {len(arrays): 0}
        arrays.append(out)
        specs.append(pl.BlockSpec(memory_space=pl.ANY))
    return pl.pallas_call(
        kernel,
        grid=(len(group),),
        out_shape=jax.ShapeDtypeStruct(whole, jnp.bfloat16),
        in_specs=specs,
        out_specs=pl.BlockSpec((1, parts, size, size), lambda i: (i + first, 0, 0, 0)),
        input_output_aliases=aliases,
        compiler_params=pltpu.CompilerParams(vmem_limit_bytes=LIMIT),
        cost_estimate=pl.CostEstimate(flops=1 << 10, bytes_accessed=1 << 10, transcendentals=0),
    )(*arrays)


def body(green, coupling, phonon, shift):
    own = green[0, 0]
    whole = own.shape
    energies = whole[0]
    last = energies - 1
    offsets = phonon.shape[0]
    radius = (offsets - 1) // 2
    ups = range(1, radius + 1)
    args = (shift.T, coupling, phonon)

    raws = {q: passed_round(green, q)[0, 0] for q in ups}

    def parts_of(group, block, below=None):
        return {q: sums_call(group, radius - q, args, block, below, jnp.bfloat16) for q in ups}

    def send(parts, *results):
        return {q: passed_round(after(x, *results), -q) for q, x in parts.items()}

    high = tuple(range(2, energies))
    parts = parts_of(high, own)
    arrived = {high: send(parts)}
    block = after(own, *parts.values())
    below = passed_along(block[last:], "energy", 1)
    every = tuple(range(energies))
    own_terms = [
        sums_call(every[1:], radius, args, block, None, jnp.float32),
        sums_call(every[:1], radius, args, block, below, jnp.float32),
    ]
    for group in ((1,), (0,)):
        parts = parts_of(group, after(block, *parts.values()), below if group == (0,) else None)
        arrived[group] = send(parts, *raws.values())
    held = {q: raws[q][last:] for q in ups}
    belows = {q: passed_along(held[q], "energy", 1) for q in ups}
    upper, lowest = own_terms
    for q in ups:
        upper = sums_call(every[1:], radius + q, args, raws[q], None, jnp.float32, upper)
        lowest = sums_call(every[:1], radius + q, args, raws[q], belows[q], jnp.float32, lowest)
    out = None
    for group, pieces in arrived.items():
        total = lowest if group == (0,) else upper
        out = finish_call(group, whole, total, list(pieces.values()), out)
    return out[None, None]


def solution(mesh):
    placed = (P("mom", "energy", None, None, None, None), P(), P(), P())
    return jax.shard_map(
        body,
        mesh=mesh,
        in_specs=placed,
        out_specs=P("mom", "energy", None, None, None, None),
        check_vma=False,
    )
```

```python
import jax
import jax.numpy as jnp
from jax import lax
from jax.experimental import pallas as pl
from jax.experimental.pallas import tpu as pltpu
from jax.sharding import PartitionSpec as P

SMAX = 1
HBM = pl.BlockSpec(memory_space=pltpu.HBM)
VMEM = pl.BlockSpec(memory_space=pltpu.VMEM)
SMEM = pl.BlockSpec(memory_space=pltpu.SMEM)
LIMIT = 32 * 1024 * 1024


def passed_along(x, axis, by):
    length = lax.axis_size(axis)
    pairs = [(i, i + by) for i in range(length) if 0 <= i + by < length]
    return lax.ppermute(x, axis, pairs)


def passed_round(x, even_by, odd_by):
    groups, points = lax.axis_size("energy"), lax.axis_size("mom")
    pairs = []
    for group in range(groups):
        by = even_by if group % 2 == 0 else odd_by
        for point in range(points):
            pairs.append((group * points + point, group * points + (point + by) % points))
    return lax.ppermute(x, ("energy", "mom"), pairs)


def after(x, *results):
    return lax.optimization_barrier((x, *results))[0]


def even_group():
    return lax.rem(lax.axis_index("energy"), 2) == 0


def products(blocks, coupling):
    lefts = [
        jnp.dot(coupling, block, preferred_element_type=jnp.float32).astype(jnp.bfloat16)
        for block in blocks
    ]
    return [jnp.dot(left, coupling, preferred_element_type=jnp.float32) for left in lefts]


def load(place, even, part, back=0):
    first, second, at = place
    if first is second:
        return first[at - back, part]
    return jnp.where(even, first[at - back, part], second[at - back, part])


def terms(energy, offset, shift, coupling, phonon, slots, even):
    modes = coupling.shape[0]
    low, high = slots[energy - SMAX], slots[energy]
    sums = None
    for mode in range(modes):
        step = shift[mode, offset]
        if low[0] is high[0] and low[1] is high[1]:
            blocks = [load(high, even, part, step) for part in range(2)]
        else:
            blocks = [
                jnp.where(step > 0, load(low, even, part), load(high, even, part))
                for part in range(2)
            ]
        found = mode_terms(mode, offset, blocks, coupling, phonon)
        sums = found if sums is None else [x + y for x, y in zip(sums, found)]
    return sums


def mode_terms(mode, offset, blocks, coupling, phonon):
    size = coupling.shape[1]
    first, second = products(blocks, coupling[mode])
    real = phonon[offset, pl.ds(2 * mode * size, size), :].astype(jnp.float32)
    imag = phonon[offset, pl.ds((2 * mode + 1) * size, size), :].astype(jnp.float32)
    return [first * real - second * imag, first * imag + second * real]


def add_low(pair, sources, shift, coupling, phonon, even):
    for offset, place in sources:
        for mode in range(coupling.shape[0]):
            blocks = [load(place, even, part) for part in range(2)]
            found = mode_terms(mode, offset, blocks, coupling, phonon)
            step = shift[mode, offset]
            pair[step, 0] += found[0]
            pair[step, 1] += found[1]


def add_edges(pair, sources, shift, coupling, phonon, even):
    for offset, below, above in sources:
        for mode in range(coupling.shape[0]):
            step = shift[mode, offset]
            blocks = [
                jnp.where(step > 0, load(below, even, part), load(above, even, part))
                for part in range(2)
            ]
            found = mode_terms(mode, offset, blocks, coupling, phonon)
            pair[1 - step, 0] += found[0]
            pair[1 - step, 1] += found[1]


class Operands:
    def __init__(self):
        self.arrays = []

    def add(self, array):
        for n, other in enumerate(self.arrays):
            if other is array:
                return n
        self.arrays.append(array)
        return len(self.arrays) - 1

    def place(self, place):
        return (self.add(place[0]), self.add(place[1]), place[2])

    def slots(self, slots, energies):
        used = {slot for energy in energies for slot in (energy - SMAX, energy)}
        return {slot: self.place(slots[slot]) for slot in slots if slot in used}


def at_refs(refs, place):
    return (refs[place[0]], refs[place[1]], place[2])


def estimate(coupling, energies):
    modes, size, _ = coupling.shape
    flops = 128 * energies * modes * size**3
    return pl.CostEstimate(flops=flops, bytes_accessed=1 << 24, transcendentals=0)


def sums_call(energies, sources, args, like, dtype, raw=None):
    _, parts, size, _ = like.shape
    count = len(energies)
    operands = Operands()
    layout = [(offset, operands.slots(slots, energies)) for offset, slots in sources]
    source = operands.add(like) if raw is not None else None

    def kernel(shift, coupling, phonon, *refs):
        out = refs[-1]
        even = even_group()

        def sums():
            for at, energy in enumerate(energies):
                for n, (offset, slots) in enumerate(layout):
                    slots = {slot: at_refs(refs, place) for slot, place in slots.items()}
                    real, imag = terms(energy, offset, shift, coupling, phonon, slots, even)
                    if n > 0:
                        real, imag = real + out[at, 0], imag + out[at, 1]
                    out[at, 0] = real.astype(out.dtype)
                    out[at, 1] = imag.astype(out.dtype)

        if raw is None:
            sums()
        else:
            first, on_even = raw
            sends_raw = even if on_even else jnp.logical_not(even)

            @pl.when(sends_raw)
            def _():
                out[...] = refs[source][first : first + count]

            @pl.when(jnp.logical_not(sends_raw))
            def _():
                sums()

    return pl.pallas_call(
        kernel,
        out_shape=jax.ShapeDtypeStruct((count, parts, size, size), dtype),
        in_specs=[SMEM] + [VMEM] * (2 + len(operands.arrays)),
        out_specs=VMEM,
        compiler_params=pltpu.CompilerParams(vmem_limit_bytes=LIMIT),
        cost_estimate=estimate(args[1], count * len(sources)),
    )(*args, *operands.arrays)


def early_call(energies, offset, args, like):
    shift, coupling, phonon = args
    _, parts, size, _ = like.shape
    count, first = len(energies), energies[0] - SMAX

    def kernel(shift_hbm, coupling_hbm, phonon_hbm, own_hbm, out, *scratch):
        shift, coupling, phonon, own, sems = scratch
        pairs = [(own_hbm.at[pl.ds(first, count + SMAX)], own), (shift_hbm, shift)]
        pairs += [(coupling_hbm, coupling), (phonon_hbm.at[offset], phonon.at[offset])]
        copies = [pltpu.make_async_copy(*pair, sems.at[n]) for n, pair in enumerate(pairs)]
        even = even_group()
        copies[0].start()

        @pl.when(even)
        def _():
            copies[0].wait()
            out[...] = own[:count]

        @pl.when(jnp.logical_not(even))
        def _():
            for copy in copies[1:]:
                copy.start()
            for copy in copies:
                copy.wait()
            slots = {first + n: (own, own, n) for n in range(count + SMAX)}
            for at, energy in enumerate(energies):
                real, imag = terms(energy, offset, shift, coupling, phonon, slots, even)
                out[at, 0] = real.astype(out.dtype)
                out[at, 1] = imag.astype(out.dtype)

    return pl.pallas_call(
        kernel,
        out_shape=jax.ShapeDtypeStruct((count, parts, size, size), like.dtype),
        in_specs=[HBM] * 4,
        out_specs=VMEM,
        scratch_shapes=[
            pltpu.SMEM(shift.shape, shift.dtype),
            pltpu.VMEM(coupling.shape, coupling.dtype),
            pltpu.VMEM(phonon.shape, phonon.dtype),
            pltpu.VMEM((count + SMAX, parts, size, size), like.dtype),
            pltpu.SemaphoreType.DMA((4,)),
        ],
        compiler_params=pltpu.CompilerParams(vmem_limit_bytes=60 * 1024 * 1024),
        cost_estimate=estimate(coupling, count),
    )(shift, coupling, phonon, like)


def pair_call(pair, sources, args, add):
    operands = Operands()
    layout = [(offset, *[operands.place(place) for place in places]) for offset, *places in sources]

    def kernel(shift, coupling, phonon, pair_ref, *refs):
        out = refs[-1]
        out[...] = pair_ref[...]
        found = [(offset, *[at_refs(refs, p) for p in places]) for offset, *places in layout]
        add(out, found, shift, coupling, phonon, even_group())

    return pl.pallas_call(
        kernel,
        out_shape=jax.ShapeDtypeStruct(pair.shape, pair.dtype),
        in_specs=[SMEM] + [VMEM] * (len(args) + len(operands.arrays)),
        out_specs=VMEM,
        compiler_params=pltpu.CompilerParams(vmem_limit_bytes=LIMIT),
        cost_estimate=estimate(args[1], 1),
    )(*args, pair, *operands.arrays)


def add_call(energy, pair, pieces, out):
    _, parts, size, _ = out.shape
    arrays = [place[0] for place in pieces]

    def kernel(pair_ref, *refs):
        result = pair_ref[energy]
        for (_, _, at), ref in zip(pieces, refs):
            result = result + ref[at].astype(jnp.float32)
        refs[-1][0] = result.astype(out.dtype)

    return pl.pallas_call(
        kernel,
        grid=(1,),
        out_shape=jax.ShapeDtypeStruct(out.shape, out.dtype),
        in_specs=[VMEM] * (1 + len(arrays)) + [pl.BlockSpec(memory_space=pl.ANY)],
        out_specs=pl.BlockSpec((1, parts, size, size), lambda i: (i + energy, 0, 0, 0)),
        input_output_aliases={1 + len(arrays): 0},
        compiler_params=pltpu.CompilerParams(vmem_limit_bytes=LIMIT),
        cost_estimate=pl.CostEstimate(flops=1 << 33, bytes_accessed=1 << 24, transcendentals=0),
    )(pair, *arrays, out)


def finish_call(energies, whole, total, sources, pieces, args, out=None):
    _, parts, size, _ = whole
    operands = Operands()
    base = operands.add(total)
    layout = [(offset, operands.slots(slots, energies)) for offset, slots in sources]
    added = {energy: [operands.place(p) for p in pieces[energy]] for energy in energies}

    def kernel(*refs):
        shift, coupling, phonon = refs[: len(args)] if args else (None,) * 3
        refs = refs[len(args) :]
        even = even_group()
        for at, energy in enumerate(energies):

            @pl.when(pl.program_id(0) == at)
            def _():
                results = [refs[base][at, part] for part in range(2)]
                for offset, slots in layout:
                    slots = {slot: at_refs(refs, place) for slot, place in slots.items()}
                    found = terms(energy, offset, shift, coupling, phonon, slots, even)
                    results = [result + term for result, term in zip(results, found)]
                for part in range(2):
                    for place in added[energy]:
                        piece = load(at_refs(refs, place), even, part)
                        results[part] = results[part] + piece.astype(jnp.float32)
                    refs[-1][0, part] = results[part].astype(jnp.bfloat16)

    arrays = [*args, *operands.arrays]
    specs = [SMEM] * min(len(args), 1) + [VMEM] * (len(arrays) - min(len(args), 1))
    aliases = {}
    if out is not None:
        aliases = {len(arrays): 0}
        arrays.append(out)
        specs.append(pl.BlockSpec(memory_space=pl.ANY))
    first = energies[0]
    return pl.pallas_call(
        kernel,
        grid=(len(energies),),
        out_shape=jax.ShapeDtypeStruct(whole, jnp.bfloat16),
        in_specs=specs,
        out_specs=pl.BlockSpec((1, parts, size, size), lambda i: (i + first, 0, 0, 0)),
        input_output_aliases=aliases,
        compiler_params=pltpu.CompilerParams(vmem_limit_bytes=LIMIT),
        cost_estimate=pl.CostEstimate(flops=1 << 33, bytes_accessed=1 << 24, transcendentals=0),
    )(*arrays)


def body(green, coupling, phonon, shift):
    own = green[0, 0]
    whole = own.shape
    last = whole[0] - 1
    offsets = phonon.shape[0]
    radius = (offsets - 1) // 2
    ups = range(1, radius + 1)
    args = (shift.T, coupling, phonon)
    high = tuple(range(2, last + 1))

    def own_slots(block, below=None):
        slots = {energy: (block, block, energy) for energy in range(last + 1)}
        if below is not None:
            slots[-1] = (below, below, 0)
        return slots

    def send(energies, raw, *results, below=None, early=False):
        block = after(own, *results)
        made, arrived = {}, {}
        for q in ups:
            sources = [(radius - q, own_slots(block, below))]
            if early:
                made[q] = early_call(energies, radius - q, args, block)
            else:
                made[q] = sums_call(energies, sources, args, block, jnp.bfloat16, raw)
            ways = (-q, -q) if raw is None else (q, -q) if raw[1] else (-q, q)
            arrived[q] = passed_round(made[q], *ways)
        return list(made.values()), arrived

    own_top = own[last:]
    tops = {q: passed_round(own_top, q, q) for q in ups}
    made, high_1 = send(high, (1, True), own_top, early=True)
    below = passed_along(after(own_top, *made), "energy", 1)
    made, high_2 = send(high, (1, False), *made)
    block = after(own, *made)
    own_high = sums_call(high, [(radius, own_slots(block))], args, own, jnp.float32)
    pair = sums_call((0, 1), [(radius, own_slots(block, below))], args, own, jnp.float32)
    low = after(own, *made, *tops.values())[:1]
    lows = {q: passed_round(low, q, q) for q in ups}
    belows = {q: passed_along(after(tops[q], low), "energy", 1) for q in ups}
    made, second = send((1,), None, *made, low, *high_1.values())
    made, first = send((0,), None, *made, *high_2.values(), below=below)

    sources = []
    pieces = {energy: [] for energy in range(last + 1)}
    for q in ups:
        slots = {slot: (high_1[q], high_2[q], slot - 1) for slot in range(1, last)}
        slots[last] = (tops[q], tops[q], 0)
        slots[-1] = (belows[q], belows[q], 0)
        sources.append((radius + q, slots))
        for energy in high:
            pieces[energy].append((high_2[q], high_1[q], energy - 2))
        pieces[1].append((second[q], second[q], 0))
        pieces[0].append((first[q], first[q], 0))
    out = finish_call(high, whole, own_high, sources, pieces, args)
    edges = [(offset, slots[-1], slots[1]) for offset, slots in sources]
    pair = pair_call(pair, edges, args, add_edges)
    lowest = [(offset, (lows[q], lows[q], 0)) for q, (offset, _) in zip(ups, sources)]
    pair = pair_call(pair, lowest, args, add_low)
    for energy in (1, 0):
        out = add_call(energy, pair, pieces[energy], out)
    return out[None, None]


def solution(mesh):
    placed = (P("mom", "energy", None, None, None, None), P(), P(), P())
    return jax.shard_map(
        body,
        mesh=mesh,
        in_specs=placed,
        out_specs=P("mom", "energy", None, None, None, None),
        check_vma=False,
    )
```

```python
import jax
import jax.numpy as jnp
from jax import lax
from jax.experimental import pallas as pl
from jax.experimental.pallas import tpu as pltpu
from jax.sharding import PartitionSpec as P

SMAX = 1
HBM = pl.BlockSpec(memory_space=pltpu.HBM)
VMEM = pl.BlockSpec(memory_space=pltpu.VMEM)
SMEM = pl.BlockSpec(memory_space=pltpu.SMEM)
LIMIT = 32 * 1024 * 1024


def passed_along(x, axis, by):
    length = lax.axis_size(axis)
    pairs = [(i, i + by) for i in range(length) if 0 <= i + by < length]
    return lax.ppermute(x, axis, pairs)


def passed_round(x, even_by, odd_by):
    groups, points = lax.axis_size("energy"), lax.axis_size("mom")
    pairs = []
    for group in range(groups):
        by = even_by if group % 2 == 0 else odd_by
        for point in range(points):
            pairs.append((group * points + point, group * points + (point + by) % points))
    return lax.ppermute(x, ("energy", "mom"), pairs)


def after(x, *results):
    return lax.optimization_barrier((x, *results))[0]


def even_group():
    return lax.rem(lax.axis_index("energy"), 2) == 0


def products(blocks, coupling):
    lefts = [
        jnp.dot(coupling, block, preferred_element_type=jnp.float32).astype(jnp.bfloat16)
        for block in blocks
    ]
    return [jnp.dot(left, coupling, preferred_element_type=jnp.float32) for left in lefts]


def load(place, even, part, back=0):
    (first, at), (second, odd_at) = place
    if first is second and at == odd_at:
        return first[at - back, part]
    return jnp.where(even, first[at - back, part], second[odd_at - back, part])


def both(array, at):
    return ((array, at), (array, at))


def terms(energy, offset, shift, coupling, phonon, slots, even):
    modes = coupling.shape[0]
    low, high = slots[energy - SMAX], slots[energy]
    sums = None
    for mode in range(modes):
        step = shift[mode, offset]
        if low[0][0] is high[0][0] and low[1][0] is high[1][0]:
            blocks = [load(high, even, part, step) for part in range(2)]
        else:
            blocks = [
                jnp.where(step > 0, load(low, even, part), load(high, even, part))
                for part in range(2)
            ]
        found = mode_terms(mode, offset, blocks, coupling, phonon)
        sums = found if sums is None else [x + y for x, y in zip(sums, found)]
    return sums


def mode_terms(mode, offset, blocks, coupling, phonon):
    size = coupling.shape[1]
    first, second = products(blocks, coupling[mode])
    real = phonon[offset, pl.ds(2 * mode * size, size), :].astype(jnp.float32)
    imag = phonon[offset, pl.ds((2 * mode + 1) * size, size), :].astype(jnp.float32)
    return [first * real - second * imag, first * imag + second * real]


def add_low(pair, sources, shift, coupling, phonon, even):
    for offset, place in sources:
        for mode in range(coupling.shape[0]):
            blocks = [load(place, even, part) for part in range(2)]
            found = mode_terms(mode, offset, blocks, coupling, phonon)
            step = shift[mode, offset]
            pair[step, 0] += found[0]
            pair[step, 1] += found[1]


def add_edges(pair, sources, shift, coupling, phonon, even):
    for offset, below, above in sources:
        for mode in range(coupling.shape[0]):
            step = shift[mode, offset]
            blocks = [
                jnp.where(step > 0, load(below, even, part), load(above, even, part))
                for part in range(2)
            ]
            found = mode_terms(mode, offset, blocks, coupling, phonon)
            pair[1 - step, 0] += found[0]
            pair[1 - step, 1] += found[1]


class Operands:
    def __init__(self):
        self.arrays = []

    def add(self, array):
        for n, other in enumerate(self.arrays):
            if other is array:
                return n
        self.arrays.append(array)
        return len(self.arrays) - 1

    def place(self, place):
        return tuple((self.add(array), at) for array, at in place)

    def slots(self, slots, energies):
        used = {slot for energy in energies for slot in (energy - SMAX, energy)}
        return {slot: self.place(slots[slot]) for slot in slots if slot in used}


def at_refs(refs, place):
    return tuple((refs[n], at) for n, at in place)


def estimate(coupling, energies):
    modes, size, _ = coupling.shape
    flops = 128 * energies * modes * size**3
    return pl.CostEstimate(flops=flops, bytes_accessed=1 << 24, transcendentals=0)


def sums_call(energies, offset, slots, args, like, dtype):
    _, parts, size, _ = like.shape
    operands = Operands()
    layout = operands.slots(slots, energies)

    def kernel(shift, coupling, phonon, *refs):
        out = refs[-1]
        places = {slot: at_refs(refs, place) for slot, place in layout.items()}
        for at, energy in enumerate(energies):
            real, imag = terms(energy, offset, shift, coupling, phonon, places, even_group())
            out[at, 0] = real.astype(out.dtype)
            out[at, 1] = imag.astype(out.dtype)

    return pl.pallas_call(
        kernel,
        out_shape=jax.ShapeDtypeStruct((len(energies), parts, size, size), dtype),
        in_specs=[SMEM] + [VMEM] * (2 + len(operands.arrays)),
        out_specs=VMEM,
        compiler_params=pltpu.CompilerParams(vmem_limit_bytes=LIMIT),
        cost_estimate=estimate(args[1], len(energies)),
    )(*args, *operands.arrays)


def early_call(energies, offset, args, like):
    shift, coupling, phonon = args
    _, parts, size, _ = like.shape
    count, first = len(energies), energies[0] - SMAX

    def kernel(shift_hbm, coupling_hbm, phonon_hbm, own_hbm, out, *scratch):
        shift, coupling, phonon, own, sems = scratch
        pairs = [(shift_hbm, shift), (coupling_hbm, coupling)]
        pairs += [(own_hbm.at[pl.ds(first, count + SMAX)], own)]
        pairs += [(phonon_hbm.at[offset], phonon.at[offset])]
        copies = [pltpu.make_async_copy(*pair, sems.at[n]) for n, pair in enumerate(pairs)]
        for copy in copies:
            copy.start()
        for copy in copies:
            copy.wait()
        places = {first + n: both(own, n) for n in range(count + SMAX)}
        for at, energy in enumerate(energies):
            real, imag = terms(energy, offset, shift, coupling, phonon, places, even_group())
            out[at, 0] = real.astype(out.dtype)
            out[at, 1] = imag.astype(out.dtype)

    return pl.pallas_call(
        kernel,
        out_shape=jax.ShapeDtypeStruct((count, parts, size, size), like.dtype),
        in_specs=[HBM] * 4,
        out_specs=VMEM,
        scratch_shapes=[
            pltpu.SMEM(shift.shape, shift.dtype),
            pltpu.VMEM(coupling.shape, coupling.dtype),
            pltpu.VMEM(phonon.shape, phonon.dtype),
            pltpu.VMEM((count + SMAX, parts, size, size), like.dtype),
            pltpu.SemaphoreType.DMA((4,)),
        ],
        compiler_params=pltpu.CompilerParams(vmem_limit_bytes=60 * 1024 * 1024),
        cost_estimate=estimate(coupling, count),
    )(shift, coupling, phonon, like)


def pair_call(pair, sources, args, add):
    operands = Operands()
    layout = [(offset, *[operands.place(place) for place in places]) for offset, *places in sources]

    def kernel(shift, coupling, phonon, pair_ref, *refs):
        out = refs[-1]
        out[...] = pair_ref[...]
        found = [(offset, *[at_refs(refs, p) for p in places]) for offset, *places in layout]
        add(out, found, shift, coupling, phonon, even_group())

    return pl.pallas_call(
        kernel,
        out_shape=jax.ShapeDtypeStruct(pair.shape, pair.dtype),
        in_specs=[SMEM] + [VMEM] * (len(args) + len(operands.arrays)),
        out_specs=VMEM,
        compiler_params=pltpu.CompilerParams(vmem_limit_bytes=LIMIT),
        cost_estimate=estimate(args[1], 1),
    )(*args, pair, *operands.arrays)


def add_call(energy, pair, pieces, out):
    _, parts, size, _ = out.shape
    arrays = list(pieces)

    def kernel(pair_ref, *refs):
        result = pair_ref[energy]
        for ref in refs[: len(arrays)]:
            result = result + ref[0].astype(jnp.float32)
        refs[-1][0] = result.astype(out.dtype)

    return pl.pallas_call(
        kernel,
        grid=(1,),
        out_shape=jax.ShapeDtypeStruct(out.shape, out.dtype),
        in_specs=[VMEM] * (1 + len(arrays)) + [pl.BlockSpec(memory_space=pl.ANY)],
        out_specs=pl.BlockSpec((1, parts, size, size), lambda i: (i + energy, 0, 0, 0)),
        input_output_aliases={1 + len(arrays): 0},
        compiler_params=pltpu.CompilerParams(vmem_limit_bytes=LIMIT),
        cost_estimate=pl.CostEstimate(flops=1 << 33, bytes_accessed=1 << 24, transcendentals=0),
    )(pair, *arrays, out)


def finish_call(energies, whole, total, sources, pieces, args, out=None):
    _, parts, size, _ = whole
    operands = Operands()
    base = operands.add(total)
    layout = [(offset, operands.slots(slots, energies)) for offset, slots in sources]
    added = {energy: [operands.place(p) for p in pieces[energy]] for energy in energies}

    def kernel(*refs):
        shift, coupling, phonon = refs[: len(args)] if args else (None,) * 3
        refs = refs[len(args) :]
        even = even_group()
        for at, energy in enumerate(energies):

            @pl.when(pl.program_id(0) == at)
            def _():
                results = [refs[base][at, part] for part in range(2)]
                for offset, slots in layout:
                    slots = {slot: at_refs(refs, place) for slot, place in slots.items()}
                    found = terms(energy, offset, shift, coupling, phonon, slots, even)
                    results = [result + term for result, term in zip(results, found)]
                for part in range(2):
                    for place in added[energy]:
                        piece = load(at_refs(refs, place), even, part)
                        results[part] = results[part] + piece.astype(jnp.float32)
                    refs[-1][0, part] = results[part].astype(jnp.bfloat16)

    arrays = [*args, *operands.arrays]
    specs = [SMEM] * min(len(args), 1) + [VMEM] * (len(arrays) - min(len(args), 1))
    aliases = {}
    if out is not None:
        aliases = {len(arrays): 0}
        arrays.append(out)
        specs.append(pl.BlockSpec(memory_space=pl.ANY))
    first = energies[0]
    return pl.pallas_call(
        kernel,
        grid=(len(energies),),
        out_shape=jax.ShapeDtypeStruct(whole, jnp.bfloat16),
        in_specs=specs,
        out_specs=pl.BlockSpec((1, parts, size, size), lambda i: (i + first, 0, 0, 0)),
        input_output_aliases=aliases,
        compiler_params=pltpu.CompilerParams(vmem_limit_bytes=LIMIT),
        cost_estimate=pl.CostEstimate(flops=1 << 33, bytes_accessed=1 << 24, transcendentals=0),
    )(*arrays)


def body(green, coupling, phonon, shift):
    own = green[0, 0]
    whole = own.shape
    last = whole[0] - 1
    offsets = phonon.shape[0]
    radius = (offsets - 1) // 2
    ups = range(1, radius + 1)
    args = (shift.T, coupling, phonon)
    high = tuple(range(2, last + 1))

    def own_slots(block, below=None):
        slots = {energy: both(block, energy) for energy in range(last + 1)}
        if below is not None:
            slots[-1] = both(below, 0)
        return slots

    def part_of(energy, block, below=None):
        slots = own_slots(block, below)
        return {
            q: sums_call((energy,), radius - q, slots, args, own, jnp.bfloat16) for q in ups
        }

    wholes = {q: passed_round(green, 0, q)[0, 0] for q in ups}
    own_top = own[last:]
    tops = {q: passed_round(own_top, q, 0) for q in ups}
    block = after(own, own_top)
    highs = {q: early_call(high, radius - q, args, block) for q in ups}
    high_even = {q: passed_round(highs[q], -q, 0) for q in ups}
    block = after(block, *highs.values())
    below = passed_along(after(own_top, *highs.values()), "energy", 1)
    mid = block[1:last]
    mids = {q: passed_round(mid, q, 0) for q in ups}
    block = after(block, mid)
    own_high = sums_call(high, radius, own_slots(block), args, own, jnp.float32)
    pair = sums_call((0, 1), radius, own_slots(block, below), args, own, jnp.float32)
    low = after(block, *tops.values())[:1]
    lows = {q: passed_round(low, q, 0) for q in ups}
    held = {q: after(highs[q], low, *high_even.values()) for q in ups}
    high_odd = {q: passed_round(held[q], 0, -q) for q in ups}
    made = part_of(1, after(block, low, *wholes.values(), *mids.values()))
    second = {q: passed_round(made[q], -q, -q) for q in ups}
    even = lax.rem(lax.axis_index("energy"), 2) == 0
    belows = {}
    for q in ups:
        top = jnp.where(even, tops[q], wholes[q][last:])
        belows[q] = passed_along(after(top, *made.values()), "energy", 1)
    made = part_of(0, after(block, *made.values(), *high_odd.values()), below)
    first = {q: passed_round(made[q], -q, -q) for q in ups}

    sources = []
    pieces = {energy: [] for energy in high}
    for q in ups:
        slots = {slot: ((mids[q], slot - 1), (wholes[q], slot)) for slot in range(1, last)}
        slots[last] = ((tops[q], 0), (wholes[q], last))
        slots[0] = ((lows[q], 0), (wholes[q], 0))
        slots[-1] = both(belows[q], 0)
        sources.append((radius + q, slots))
        for energy in high:
            pieces[energy].append(((high_even[q], energy - 2), (high_odd[q], energy - 2)))
    out = finish_call(high, whole, own_high, sources, pieces, args)
    edges = [(offset, slots[-1], slots[1]) for offset, slots in sources]
    pair = pair_call(pair, edges, args, add_edges)
    lowest = [(offset, slots[0]) for offset, slots in sources]
    pair = pair_call(pair, lowest, args, add_low)
    out = add_call(1, pair, second.values(), out)
    out = add_call(0, pair, first.values(), out)
    return out[None, None]


def solution(mesh):
    placed = (P("mom", "energy", None, None, None, None), P(), P(), P())
    return jax.shard_map(
        body,
        mesh=mesh,
        in_specs=placed,
        out_specs=P("mom", "energy", None, None, None, None),
        check_vma=False,
    )
```

```python
import jax
import jax.numpy as jnp
from jax import lax
from jax.experimental import pallas as pl
from jax.experimental.pallas import tpu as pltpu
from jax.sharding import PartitionSpec as P

SMAX = 1
HBM = pl.BlockSpec(memory_space=pltpu.HBM)
VMEM = pl.BlockSpec(memory_space=pltpu.VMEM)
SMEM = pl.BlockSpec(memory_space=pltpu.SMEM)
LIMIT = 32 * 1024 * 1024


def passed_along(x, axis, by):
    length = lax.axis_size(axis)
    pairs = [(i, i + by) for i in range(length) if 0 <= i + by < length]
    return lax.ppermute(x, axis, pairs)


def passed_round(x, even_by, odd_by):
    groups, points = lax.axis_size("energy"), lax.axis_size("mom")
    pairs = []
    for group in range(groups):
        by = even_by if group % 2 == 0 else odd_by
        for point in range(points if by != 0 else 0):
            pairs.append((group * points + point, group * points + (point + by) % points))
    return lax.ppermute(x, ("energy", "mom"), pairs)


def after(x, *results):
    return lax.optimization_barrier((x, *results))[0]


def even_group():
    return lax.rem(lax.axis_index("energy"), 2) == 0


def products(blocks, coupling):
    lefts = [
        jnp.dot(coupling, block, preferred_element_type=jnp.float32).astype(jnp.bfloat16)
        for block in blocks
    ]
    return [jnp.dot(left, coupling, preferred_element_type=jnp.float32) for left in lefts]


def load(place, even, part, back=0):
    (first, at), (second, odd_at) = place
    if first is second and at == odd_at:
        return first[at - back, part]
    return jnp.where(even, first[at - back, part], second[odd_at - back, part])


def both(array, at):
    return ((array, at), (array, at))


def terms(energy, offset, shift, coupling, phonon, slots, even):
    modes = coupling.shape[0]
    low, high = slots[energy - SMAX], slots[energy]
    sums = None
    for mode in range(modes):
        step = shift[mode, offset]
        if low[0][0] is high[0][0] and low[1][0] is high[1][0]:
            blocks = [load(high, even, part, step) for part in range(2)]
        else:
            blocks = [
                jnp.where(step > 0, load(low, even, part), load(high, even, part))
                for part in range(2)
            ]
        found = mode_terms(mode, offset, blocks, coupling, phonon)
        sums = found if sums is None else [x + y for x, y in zip(sums, found)]
    return sums


def mode_terms(mode, offset, blocks, coupling, phonon):
    size = coupling.shape[1]
    first, second = products(blocks, coupling[mode])
    real = phonon[offset, pl.ds(2 * mode * size, size), :].astype(jnp.float32)
    imag = phonon[offset, pl.ds((2 * mode + 1) * size, size), :].astype(jnp.float32)
    return [first * real - second * imag, first * imag + second * real]


def add_low(pair, sources, shift, coupling, phonon, even):
    for offset, place in sources:
        for mode in range(coupling.shape[0]):
            blocks = [load(place, even, part) for part in range(2)]
            found = mode_terms(mode, offset, blocks, coupling, phonon)
            step = shift[mode, offset]
            pair[step, 0] += found[0]
            pair[step, 1] += found[1]


def add_edges(pair, sources, shift, coupling, phonon, even):
    for offset, below, above in sources:
        for mode in range(coupling.shape[0]):
            step = shift[mode, offset]
            blocks = [
                jnp.where(step > 0, load(below, even, part), load(above, even, part))
                for part in range(2)
            ]
            found = mode_terms(mode, offset, blocks, coupling, phonon)
            pair[1 - step, 0] += found[0]
            pair[1 - step, 1] += found[1]


class Operands:
    def __init__(self):
        self.arrays = []

    def add(self, array):
        for n, other in enumerate(self.arrays):
            if other is array:
                return n
        self.arrays.append(array)
        return len(self.arrays) - 1

    def place(self, place):
        return tuple((self.add(array), at) for array, at in place)

    def slots(self, slots, energies):
        used = {slot for energy in energies for slot in (energy - SMAX, energy)}
        return {slot: self.place(slots[slot]) for slot in slots if slot in used}


def at_refs(refs, place):
    return tuple((refs[n], at) for n, at in place)


def estimate(coupling, energies):
    modes, size, _ = coupling.shape
    flops = 128 * energies * modes * size**3
    return pl.CostEstimate(flops=flops, bytes_accessed=1 << 24, transcendentals=0)


def sums_call(energies, offset, slots, args, like, dtype):
    _, parts, size, _ = like.shape
    operands = Operands()
    layout = operands.slots(slots, energies)

    def kernel(shift, coupling, phonon, *refs):
        out = refs[-1]
        places = {slot: at_refs(refs, place) for slot, place in layout.items()}
        for at, energy in enumerate(energies):
            real, imag = terms(energy, offset, shift, coupling, phonon, places, even_group())
            out[at, 0] = real.astype(out.dtype)
            out[at, 1] = imag.astype(out.dtype)

    return pl.pallas_call(
        kernel,
        out_shape=jax.ShapeDtypeStruct((len(energies), parts, size, size), dtype),
        in_specs=[SMEM] + [VMEM] * (2 + len(operands.arrays)),
        out_specs=VMEM,
        compiler_params=pltpu.CompilerParams(vmem_limit_bytes=LIMIT),
        cost_estimate=estimate(args[1], len(energies)),
    )(*args, *operands.arrays)


def early_call(energies, offset, args, like):
    shift, coupling, phonon = args
    _, parts, size, _ = like.shape
    count, first = len(energies), energies[0] - SMAX

    def kernel(shift_hbm, coupling_hbm, phonon_hbm, own_hbm, out, *scratch):
        shift, coupling, phonon, own, sems = scratch
        pairs = [(shift_hbm, shift), (coupling_hbm, coupling)]
        pairs += [(own_hbm.at[pl.ds(first, count + SMAX)], own)]
        pairs += [(phonon_hbm.at[offset], phonon.at[offset])]
        copies = [pltpu.make_async_copy(*pair, sems.at[n]) for n, pair in enumerate(pairs)]
        for copy in copies:
            copy.start()
        for copy in copies:
            copy.wait()
        places = {first + n: both(own, n) for n in range(count + SMAX)}
        for at, energy in enumerate(energies):
            real, imag = terms(energy, offset, shift, coupling, phonon, places, even_group())
            out[at, 0] = real.astype(out.dtype)
            out[at, 1] = imag.astype(out.dtype)

    return pl.pallas_call(
        kernel,
        out_shape=jax.ShapeDtypeStruct((count, parts, size, size), like.dtype),
        in_specs=[HBM] * 4,
        out_specs=VMEM,
        scratch_shapes=[
            pltpu.SMEM(shift.shape, shift.dtype),
            pltpu.VMEM(coupling.shape, coupling.dtype),
            pltpu.VMEM(phonon.shape, phonon.dtype),
            pltpu.VMEM((count + SMAX, parts, size, size), like.dtype),
            pltpu.SemaphoreType.DMA((4,)),
        ],
        compiler_params=pltpu.CompilerParams(vmem_limit_bytes=60 * 1024 * 1024),
        cost_estimate=estimate(coupling, count),
    )(shift, coupling, phonon, like)


def pair_call(pair, sources, args, add):
    operands = Operands()
    layout = [(offset, *[operands.place(place) for place in places]) for offset, *places in sources]

    def kernel(shift, coupling, phonon, pair_ref, *refs):
        out = refs[-1]
        out[...] = pair_ref[...]
        found = [(offset, *[at_refs(refs, p) for p in places]) for offset, *places in layout]
        add(out, found, shift, coupling, phonon, even_group())

    return pl.pallas_call(
        kernel,
        out_shape=jax.ShapeDtypeStruct(pair.shape, pair.dtype),
        in_specs=[SMEM] + [VMEM] * (len(args) + len(operands.arrays)),
        out_specs=VMEM,
        compiler_params=pltpu.CompilerParams(vmem_limit_bytes=LIMIT),
        cost_estimate=estimate(args[1], 1),
    )(*args, pair, *operands.arrays)


def add_call(energy, pair, pieces, out):
    _, parts, size, _ = out.shape
    arrays = list(pieces)

    def kernel(pair_ref, *refs):
        result = pair_ref[energy]
        for ref in refs[: len(arrays)]:
            result = result + ref[0].astype(jnp.float32)
        refs[-1][0] = result.astype(out.dtype)

    return pl.pallas_call(
        kernel,
        grid=(1,),
        out_shape=jax.ShapeDtypeStruct(out.shape, out.dtype),
        in_specs=[VMEM] * (1 + len(arrays)) + [pl.BlockSpec(memory_space=pl.ANY)],
        out_specs=pl.BlockSpec((1, parts, size, size), lambda i: (i + energy, 0, 0, 0)),
        input_output_aliases={1 + len(arrays): 0},
        compiler_params=pltpu.CompilerParams(vmem_limit_bytes=LIMIT),
        cost_estimate=pl.CostEstimate(flops=1 << 33, bytes_accessed=1 << 24, transcendentals=0),
    )(pair, *arrays, out)


def finish_call(energies, whole, total, sources, pieces, args, out=None):
    _, parts, size, _ = whole
    operands = Operands()
    base = operands.add(total)
    layout = [(offset, operands.slots(slots, energies)) for offset, slots in sources]
    added = {energy: [operands.place(p) for p in pieces[energy]] for energy in energies}

    def kernel(*refs):
        shift, coupling, phonon = refs[: len(args)] if args else (None,) * 3
        refs = refs[len(args) :]
        even = even_group()
        for at, energy in enumerate(energies):

            @pl.when(pl.program_id(0) == at)
            def _():
                results = [refs[base][at, part] for part in range(2)]
                for offset, slots in layout:
                    slots = {slot: at_refs(refs, place) for slot, place in slots.items()}
                    found = terms(energy, offset, shift, coupling, phonon, slots, even)
                    results = [result + term for result, term in zip(results, found)]
                for part in range(2):
                    for place in added[energy]:
                        piece = load(at_refs(refs, place), even, part)
                        results[part] = results[part] + piece.astype(jnp.float32)
                    refs[-1][0, part] = results[part].astype(jnp.bfloat16)

    arrays = [*args, *operands.arrays]
    specs = [SMEM] * min(len(args), 1) + [VMEM] * (len(arrays) - min(len(args), 1))
    aliases = {}
    if out is not None:
        aliases = {len(arrays): 0}
        arrays.append(out)
        specs.append(pl.BlockSpec(memory_space=pl.ANY))
    first = energies[0]
    return pl.pallas_call(
        kernel,
        grid=(len(energies),),
        out_shape=jax.ShapeDtypeStruct(whole, jnp.bfloat16),
        in_specs=specs,
        out_specs=pl.BlockSpec((1, parts, size, size), lambda i: (i + first, 0, 0, 0)),
        input_output_aliases=aliases,
        compiler_params=pltpu.CompilerParams(vmem_limit_bytes=LIMIT),
        cost_estimate=pl.CostEstimate(flops=1 << 33, bytes_accessed=1 << 24, transcendentals=0),
    )(*arrays)


def body(green, coupling, phonon, shift):
    own = green[0, 0]
    whole = own.shape
    last = whole[0] - 1
    offsets = phonon.shape[0]
    radius = (offsets - 1) // 2
    ups = range(1, radius + 1)
    args = (shift.T, coupling, phonon)
    high = tuple(range(2, last + 1))

    def own_slots(block, below=None):
        slots = {energy: both(block, energy) for energy in range(last + 1)}
        if below is not None:
            slots[-1] = both(below, 0)
        return slots

    def part_of(energy, block, below=None):
        slots = own_slots(block, below)
        return {
            q: sums_call((energy,), radius - q, slots, args, own, jnp.bfloat16) for q in ups
        }

    wholes = {q: passed_round(green, 0, q)[0, 0] for q in ups}
    own_top = own[last:]
    tops = {q: passed_round(own_top, q, 0) for q in ups}
    block = after(own, own_top)
    highs = {q: early_call(high, radius - q, args, block) for q in ups}
    high_even = {q: passed_round(highs[q], -q, 0) for q in ups}
    block = after(block, *highs.values())
    below = passed_along(after(own_top, *highs.values()), "energy", 1)
    mid = block[1:last]
    mids = {q: passed_round(mid, q, 0) for q in ups}
    block = after(block, mid)
    own_high = sums_call(high, radius, own_slots(block), args, own, jnp.float32)
    pair = sums_call((0, 1), radius, own_slots(block, below), args, own, jnp.float32)
    low = after(block, *tops.values())[:1]
    lows = {q: passed_round(low, q, 0) for q in ups}
    held = {q: after(highs[q], low, *high_even.values()) for q in ups}
    high_odd = {q: passed_round(held[q], 0, -q) for q in ups}
    made = part_of(1, after(block, low, *wholes.values(), *mids.values()))
    second = {q: passed_round(made[q], -q, -q) for q in ups}
    even = lax.rem(lax.axis_index("energy"), 2) == 0
    belows = {}
    for q in ups:
        top = jnp.where(even, tops[q], wholes[q][last:])
        belows[q] = passed_along(after(top, *made.values()), "energy", 1)
    made = part_of(0, after(block, *made.values(), *lows.values()), below)
    first = {q: passed_round(made[q], -q, -q) for q in ups}

    sources = []
    pieces = {energy: [] for energy in high}
    for q in ups:
        slots = {slot: ((mids[q], slot - 1), (wholes[q], slot)) for slot in range(1, last)}
        slots[last] = ((tops[q], 0), (wholes[q], last))
        slots[0] = ((lows[q], 0), (wholes[q], 0))
        slots[-1] = both(belows[q], 0)
        sources.append((radius + q, slots))
        for energy in high:
            pieces[energy].append(((high_even[q], energy - 2), (high_odd[q], energy - 2)))
    out = finish_call(high, whole, own_high, sources, pieces, args)
    edges = [(offset, slots[-1], slots[1]) for offset, slots in sources]
    pair = pair_call(pair, edges, args, add_edges)
    lowest = [(offset, slots[0]) for offset, slots in sources]
    pair = pair_call(pair, lowest, args, add_low)
    out = add_call(1, pair, second.values(), out)
    out = add_call(0, pair, first.values(), out)
    return out[None, None]


def solution(mesh):
    placed = (P("mom", "energy", None, None, None, None), P(), P(), P())
    return jax.shard_map(
        body,
        mesh=mesh,
        in_specs=placed,
        out_specs=P("mom", "energy", None, None, None, None),
        check_vma=False,
    )
```

```python
import jax
import jax.numpy as jnp
from jax import lax
from jax.experimental import pallas as pl
from jax.experimental.pallas import tpu as pltpu
from jax.sharding import PartitionSpec as P

SMAX = 1
VMEM = pl.BlockSpec(memory_space=pltpu.VMEM)
SMEM = pl.BlockSpec(memory_space=pltpu.SMEM)
LIMIT = 32 * 1024 * 1024


def passed_along(x, axis, by):
    length = lax.axis_size(axis)
    pairs = [(i, i + by) for i in range(length) if 0 <= i + by < length]
    return lax.ppermute(x, axis, pairs)


def passed_round(x, by):
    length = lax.axis_size("mom")
    return lax.ppermute(x, "mom", [(i, (i + by) % length) for i in range(length)])


def passed_apart(x, by, around):
    length = lax.axis_size("mom")
    steps = [(i, i + by) for i in range(length)]
    pairs = [(i, j % length) for i, j in steps if (0 <= j < length) != around]
    return lax.ppermute(x, "mom", pairs)


def after(x, *results):
    return lax.optimization_barrier((x, *results))[0]


def products(blocks, coupling):
    lefts = [
        jnp.dot(coupling, block, preferred_element_type=jnp.float32).astype(jnp.bfloat16)
        for block in blocks
    ]
    return [jnp.dot(left, coupling, preferred_element_type=jnp.float32) for left in lefts]


def terms(energy, offset, shift, coupling, phonon, blocks, below):
    modes, size, _ = coupling.shape
    real_sum, imag_sum = None, None
    for mode in range(modes):
        step = shift[mode, offset]
        if energy == 0:
            used = [jnp.where(step > 0, below[0, part], blocks[0, part]) for part in range(2)]
        else:
            used = [blocks[energy - step, part] for part in range(2)]
        first, second = products(used, coupling[mode])
        real = phonon[offset, pl.ds(2 * mode * size, size), :].astype(jnp.float32)
        imag = phonon[offset, pl.ds((2 * mode + 1) * size, size), :].astype(jnp.float32)
        real_term = first * real - second * imag
        imag_term = first * imag + second * real
        real_sum = real_term if real_sum is None else real_sum + real_term
        imag_sum = imag_term if imag_sum is None else imag_sum + imag_term
    return real_sum, imag_sum


def estimate(coupling, energies):
    modes, size, _ = coupling.shape
    flops = 16 * energies * modes * size**3
    return pl.CostEstimate(flops=flops, bytes_accessed=1 << 24, transcendentals=0)


def sums_call(energies, offset, args, blocks, below, dtype, start=None):
    _, parts, size, _ = blocks.shape
    extra = [x for x in (below, start) if x is not None]

    def kernel(shift, coupling, phonon, blocks, *refs):
        out = refs[-1]
        below_ref = refs[0] if below is not None else None
        for at, energy in enumerate(energies):
            sums = terms(energy, offset, shift, coupling, phonon, blocks, below_ref)
            for part in range(2):
                total = sums[part]
                if start is not None:
                    total = total + refs[-2][at, part]
                out[at, part] = total.astype(out.dtype)

    return pl.pallas_call(
        kernel,
        out_shape=jax.ShapeDtypeStruct((len(energies), parts, size, size), dtype),
        in_specs=[SMEM] + [VMEM] * (3 + len(extra)),
        out_specs=VMEM,
        compiler_params=pltpu.CompilerParams(vmem_limit_bytes=LIMIT),
        cost_estimate=estimate(args[1], len(energies)),
    )(*args, blocks, *extra)


def finish_call(group, whole, total, pieces, out=None):
    _, parts, size, _ = whole
    first = group[0]

    def kernel(total_ref, *refs):
        at = pl.program_id(0)
        result = total_ref[at]
        for piece in refs[: len(pieces)]:
            result = result + piece[at].astype(jnp.float32)
        refs[-1][0] = result.astype(jnp.bfloat16)

    arrays = [total, *pieces]
    specs = [VMEM] * len(arrays)
    aliases = {}
    if out is not None:
        aliases = {len(arrays): 0}
        arrays.append(out)
        specs.append(pl.BlockSpec(memory_space=pl.ANY))
    return pl.pallas_call(
        kernel,
        grid=(len(group),),
        out_shape=jax.ShapeDtypeStruct(whole, jnp.bfloat16),
        in_specs=specs,
        out_specs=pl.BlockSpec((1, parts, size, size), lambda i: (i + first, 0, 0, 0)),
        input_output_aliases=aliases,
        compiler_params=pltpu.CompilerParams(vmem_limit_bytes=LIMIT),
        cost_estimate=pl.CostEstimate(flops=1 << 10, bytes_accessed=1 << 10, transcendentals=0),
    )(*arrays)


def body(green, coupling, phonon, shift):
    own = green[0, 0]
    whole = own.shape
    last = whole[0] - 1
    offsets = phonon.shape[0]
    radius = (offsets - 1) // 2
    ups = range(1, radius + 1)
    args = (shift.T, coupling, phonon)
    high, low = tuple(range(2, last + 1)), (0, 1)

    raws = {q: passed_round(green, q)[0, 0] for q in ups}

    def parts_of(group, block, below=None):
        return {q: sums_call(group, radius - q, args, block, below, jnp.bfloat16) for q in ups}

    high_parts = parts_of(high, own)
    arrived = {high: [passed_apart(x, -q, False) for q, x in high_parts.items()]}
    block = after(own, *high_parts.values())
    below = passed_along(block[last:], "energy", 1)
    low_parts = parts_of(low, block, below)
    arrived[low] = [passed_apart(x, -q, False) for q, x in low_parts.items()]
    block = after(block, *low_parts.values())
    own_upper = sums_call(high, radius, args, block, None, jnp.float32)
    own_lower = sums_call(low, radius, args, block, below, jnp.float32)
    for group, parts in ((high, high_parts), (low, low_parts)):
        for q, x in parts.items():
            arrived[group].append(passed_apart(after(x, *raws.values()), -q, True))
    belows = {q: passed_along(raws[q][last:], "energy", 1) for q in ups}
    for q in ups:
        own_upper = sums_call(high, radius + q, args, raws[q], None, jnp.float32, own_upper)
        own_lower = sums_call(low, radius + q, args, raws[q], belows[q], jnp.float32, own_lower)
    out = finish_call(high, whole, own_upper, arrived[high])
    out = finish_call(low, whole, own_lower, arrived[low], out)
    return out[None, None]


def solution(mesh):
    placed = (P("mom", "energy", None, None, None, None), P(), P(), P())
    return jax.shard_map(
        body,
        mesh=mesh,
        in_specs=placed,
        out_specs=P("mom", "energy", None, None, None, None),
        check_vma=False,
    )
```

```python
import jax
import jax.numpy as jnp
from jax import lax
from jax.experimental import pallas as pl
from jax.experimental.pallas import tpu as pltpu
from jax.sharding import PartitionSpec as P

SMAX = 1
VMEM = pl.BlockSpec(memory_space=pltpu.VMEM)
SMEM = pl.BlockSpec(memory_space=pltpu.SMEM)
LIMIT = 32 * 1024 * 1024


def passed_along(x, axis, by):
    length = lax.axis_size(axis)
    pairs = [(i, i + by) for i in range(length) if 0 <= i + by < length]
    return lax.ppermute(x, axis, pairs)


def passed_round(x, by):
    length = lax.axis_size("mom")
    return lax.ppermute(x, "mom", [(i, (i + by) % length) for i in range(length)])


def passed_first(x, by):
    length = lax.axis_size("mom")
    pairs = [(i, (i + by) % length) for i in range(length)]
    return lax.ppermute(x, "mom", pairs[by:]), lax.ppermute(x, "mom", pairs[:by])


def after(x, *results):
    return lax.optimization_barrier((x, *results))[0]


def products(blocks, coupling):
    lefts = [
        jnp.dot(coupling, block, preferred_element_type=jnp.float32).astype(jnp.bfloat16)
        for block in blocks
    ]
    return [jnp.dot(left, coupling, preferred_element_type=jnp.float32) for left in lefts]


def terms(energy, offset, shift, coupling, phonon, blocks, below):
    modes, size, _ = coupling.shape
    real_sum, imag_sum = None, None
    for mode in range(modes):
        step = shift[mode, offset]
        if energy == 0:
            used = [jnp.where(step > 0, below[0, part], blocks[0, part]) for part in range(2)]
        else:
            used = [blocks[energy - step, part] for part in range(2)]
        first, second = products(used, coupling[mode])
        real = phonon[offset, pl.ds(2 * mode * size, size), :].astype(jnp.float32)
        imag = phonon[offset, pl.ds((2 * mode + 1) * size, size), :].astype(jnp.float32)
        real_term = first * real - second * imag
        imag_term = first * imag + second * real
        real_sum = real_term if real_sum is None else real_sum + real_term
        imag_sum = imag_term if imag_sum is None else imag_sum + imag_term
    return real_sum, imag_sum


def estimate(coupling, energies):
    modes, size, _ = coupling.shape
    flops = 128 * energies * modes * size**3
    return pl.CostEstimate(flops=flops, bytes_accessed=1 << 24, transcendentals=0)


def sums_call(energies, offset, args, blocks, below, dtype, start=None):
    _, parts, size, _ = blocks.shape
    extra = [x for x in (below, start) if x is not None]

    def kernel(shift, coupling, phonon, blocks, *refs):
        out = refs[-1]
        below_ref = refs[0] if below is not None else None
        for at, energy in enumerate(energies):
            sums = terms(energy, offset, shift, coupling, phonon, blocks, below_ref)
            for part in range(2):
                total = sums[part]
                if start is not None:
                    total = total + refs[-2][at, part]
                out[at, part] = total.astype(out.dtype)

    return pl.pallas_call(
        kernel,
        out_shape=jax.ShapeDtypeStruct((len(energies), parts, size, size), dtype),
        in_specs=[SMEM] + [VMEM] * (3 + len(extra)),
        out_specs=VMEM,
        compiler_params=pltpu.CompilerParams(vmem_limit_bytes=LIMIT),
        cost_estimate=estimate(args[1], len(energies)),
    )(*args, blocks, *extra)


def finish_call(group, whole, total, pieces, out=None):
    _, parts, size, _ = whole
    first = group[0]

    def kernel(total_ref, *refs):
        at = pl.program_id(0)
        result = total_ref[at]
        for piece in refs[: len(pieces)]:
            result = result + piece[at].astype(jnp.float32)
        refs[-1][0] = result.astype(jnp.bfloat16)

    arrays = [total, *pieces]
    specs = [VMEM] * len(arrays)
    aliases = {}
    if out is not None:
        aliases = {len(arrays): 0}
        arrays.append(out)
        specs.append(pl.BlockSpec(memory_space=pl.ANY))
    return pl.pallas_call(
        kernel,
        grid=(len(group),),
        out_shape=jax.ShapeDtypeStruct(whole, jnp.bfloat16),
        in_specs=specs,
        out_specs=pl.BlockSpec((1, parts, size, size), lambda i: (i + first, 0, 0, 0)),
        input_output_aliases=aliases,
        compiler_params=pltpu.CompilerParams(vmem_limit_bytes=LIMIT),
        cost_estimate=pl.CostEstimate(flops=1 << 10, bytes_accessed=1 << 10, transcendentals=0),
    )(*arrays)


def body(green, coupling, phonon, shift):
    own = green[0, 0]
    whole = own.shape
    last = whole[0] - 1
    offsets = phonon.shape[0]
    radius = (offsets - 1) // 2
    ups = range(1, radius + 1)
    args = (shift.T, coupling, phonon)
    high = tuple(range(2, last + 1))

    def parts_of(group, block, below=None):
        return {q: sums_call(group, radius - q, args, block, below, jnp.bfloat16) for q in ups}

    def send(parts):
        return [passed_round(x, -q) for q, x in parts.items()]

    halves = {q: passed_first(green, q) for q in ups}
    parts = parts_of(high, own)
    arrived = {high: send(parts)}
    block = after(own, *parts.values())
    below = passed_along(block[last:], "energy", 1)
    own_sums = {high: sums_call(high, radius, args, block, None, jnp.float32)}
    for energy in (1, 0):
        group = (energy,)
        under = below if energy == 0 else None
        parts = parts_of(group, block, under)
        arrived[group] = send(parts)
        block = after(block, *parts.values())
        own_sums[group] = sums_call(group, radius, args, block, under, jnp.float32)
    raws = {q: (first + second)[0, 0] for q, (first, second) in halves.items()}
    belows = {q: passed_along(raws[q][last:], "energy", 1) for q in ups}
    out = None
    for group, total in own_sums.items():
        for q in ups:
            under = belows[q] if group == (0,) else None
            total = sums_call(group, radius + q, args, raws[q], under, jnp.float32, total)
        out = finish_call(group, whole, total, arrived[group], out)
    return out[None, None]


def solution(mesh):
    placed = (P("mom", "energy", None, None, None, None), P(), P(), P())
    return jax.shard_map(
        body,
        mesh=mesh,
        in_specs=placed,
        out_specs=P("mom", "energy", None, None, None, None),
        check_vma=False,
    )
```

```python
import jax
import jax.numpy as jnp
from jax import lax
from jax.experimental import pallas as pl
from jax.experimental.pallas import tpu as pltpu
from jax.sharding import PartitionSpec as P

SMAX = 1
HBM = pl.BlockSpec(memory_space=pltpu.HBM)
VMEM = pl.BlockSpec(memory_space=pltpu.VMEM)
SMEM = pl.BlockSpec(memory_space=pltpu.SMEM)
LIMIT = 32 * 1024 * 1024


def passed_along(x, axis, by):
    length = lax.axis_size(axis)
    pairs = [(i, i + by) for i in range(length) if 0 <= i + by < length]
    return lax.ppermute(x, axis, pairs)


def passed_round(x, even_by, odd_by):
    groups, points = lax.axis_size("energy"), lax.axis_size("mom")
    pairs = []
    for group in range(groups):
        by = even_by if group % 2 == 0 else odd_by
        for point in range(points):
            pairs.append((group * points + point, group * points + (point + by) % points))
    return lax.ppermute(x, ("energy", "mom"), pairs)


def after(x, *results):
    return lax.optimization_barrier((x, *results))[0]


def even_group():
    return lax.rem(lax.axis_index("energy"), 2) == 0


def products(blocks, coupling):
    lefts = [
        jnp.dot(coupling, block, preferred_element_type=jnp.float32).astype(jnp.bfloat16)
        for block in blocks
    ]
    return [jnp.dot(left, coupling, preferred_element_type=jnp.float32) for left in lefts]


def load(place, even, part, back=0):
    first, second, at = place
    if first is second:
        return first[at - back, part]
    return jnp.where(even, first[at - back, part], second[at - back, part])


def terms(energy, offset, shift, coupling, phonon, slots, even):
    modes = coupling.shape[0]
    low, high = slots[energy - SMAX], slots[energy]
    sums = None
    for mode in range(modes):
        step = shift[mode, offset]
        if low[0] is high[0] and low[1] is high[1]:
            blocks = [load(high, even, part, step) for part in range(2)]
        else:
            blocks = [
                jnp.where(step > 0, load(low, even, part), load(high, even, part))
                for part in range(2)
            ]
        found = mode_terms(mode, offset, blocks, coupling, phonon)
        sums = found if sums is None else [x + y for x, y in zip(sums, found)]
    return sums


def mode_terms(mode, offset, blocks, coupling, phonon):
    size = coupling.shape[1]
    first, second = products(blocks, coupling[mode])
    real = phonon[offset, pl.ds(2 * mode * size, size), :].astype(jnp.float32)
    imag = phonon[offset, pl.ds((2 * mode + 1) * size, size), :].astype(jnp.float32)
    return [first * real - second * imag, first * imag + second * real]


def add_low(pair, sources, shift, coupling, phonon, even):
    for offset, place in sources:
        for mode in range(coupling.shape[0]):
            blocks = [load(place, even, part) for part in range(2)]
            found = mode_terms(mode, offset, blocks, coupling, phonon)
            step = shift[mode, offset]
            pair[step, 0] += found[0]
            pair[step, 1] += found[1]


def add_edges(pair, sources, shift, coupling, phonon, even):
    for offset, below, above in sources:
        for mode in range(coupling.shape[0]):
            step = shift[mode, offset]
            blocks = [
                jnp.where(step > 0, load(below, even, part), load(above, even, part))
                for part in range(2)
            ]
            found = mode_terms(mode, offset, blocks, coupling, phonon)
            pair[1 - step, 0] += found[0]
            pair[1 - step, 1] += found[1]


class Operands:
    def __init__(self):
        self.arrays = []

    def add(self, array):
        for n, other in enumerate(self.arrays):
            if other is array:
                return n
        self.arrays.append(array)
        return len(self.arrays) - 1

    def place(self, place):
        return (self.add(place[0]), self.add(place[1]), place[2])

    def slots(self, slots, energies):
        used = {slot for energy in energies for slot in (energy - SMAX, energy)}
        return {slot: self.place(slots[slot]) for slot in slots if slot in used}


def at_refs(refs, place):
    return (refs[place[0]], refs[place[1]], place[2])


def estimate(coupling, energies):
    modes, size, _ = coupling.shape
    flops = 128 * energies * modes * size**3
    return pl.CostEstimate(flops=flops, bytes_accessed=1 << 24, transcendentals=0)


def sums_call(energies, sources, args, like, dtype, raw=None):
    _, parts, size, _ = like.shape
    count = len(energies)
    operands = Operands()
    layout = [(offset, operands.slots(slots, energies)) for offset, slots in sources]
    source = operands.add(like) if raw is not None else None

    def kernel(shift, coupling, phonon, *refs):
        out = refs[-1]
        even = even_group()

        def sums():
            for at, energy in enumerate(energies):
                for n, (offset, slots) in enumerate(layout):
                    slots = {slot: at_refs(refs, place) for slot, place in slots.items()}
                    real, imag = terms(energy, offset, shift, coupling, phonon, slots, even)
                    if n > 0:
                        real, imag = real + out[at, 0], imag + out[at, 1]
                    out[at, 0] = real.astype(out.dtype)
                    out[at, 1] = imag.astype(out.dtype)

        if raw is None:
            sums()
        else:
            first, on_even = raw
            sends_raw = even if on_even else jnp.logical_not(even)

            @pl.when(sends_raw)
            def _():
                out[...] = refs[source][first : first + count]

            @pl.when(jnp.logical_not(sends_raw))
            def _():
                sums()

    return pl.pallas_call(
        kernel,
        out_shape=jax.ShapeDtypeStruct((count, parts, size, size), dtype),
        in_specs=[SMEM] + [VMEM] * (2 + len(operands.arrays)),
        out_specs=VMEM,
        compiler_params=pltpu.CompilerParams(vmem_limit_bytes=LIMIT),
        cost_estimate=estimate(args[1], count * len(sources)),
    )(*args, *operands.arrays)


def early_call(energies, offset, args, like):
    shift, coupling, phonon = args
    _, parts, size, _ = like.shape
    count, first = len(energies), energies[0] - SMAX

    def kernel(shift_hbm, coupling_hbm, phonon_hbm, own_hbm, out, *scratch):
        shift, coupling, phonon, own, sems = scratch
        pairs = [(own_hbm.at[pl.ds(first, count + SMAX)], own), (shift_hbm, shift)]
        pairs += [(coupling_hbm, coupling), (phonon_hbm.at[offset], phonon.at[offset])]
        copies = [pltpu.make_async_copy(*pair, sems.at[n]) for n, pair in enumerate(pairs)]
        even = even_group()
        copies[0].start()

        @pl.when(even)
        def _():
            copies[0].wait()
            out[...] = own[:count]

        @pl.when(jnp.logical_not(even))
        def _():
            for copy in copies[1:]:
                copy.start()
            for copy in copies:
                copy.wait()
            slots = {first + n: (own, own, n) for n in range(count + SMAX)}
            for at, energy in enumerate(energies):
                real, imag = terms(energy, offset, shift, coupling, phonon, slots, even)
                out[at, 0] = real.astype(out.dtype)
                out[at, 1] = imag.astype(out.dtype)

    return pl.pallas_call(
        kernel,
        out_shape=jax.ShapeDtypeStruct((count, parts, size, size), like.dtype),
        in_specs=[HBM] * 4,
        out_specs=VMEM,
        scratch_shapes=[
            pltpu.SMEM(shift.shape, shift.dtype),
            pltpu.VMEM(coupling.shape, coupling.dtype),
            pltpu.VMEM(phonon.shape, phonon.dtype),
            pltpu.VMEM((count + SMAX, parts, size, size), like.dtype),
            pltpu.SemaphoreType.DMA((4,)),
        ],
        compiler_params=pltpu.CompilerParams(vmem_limit_bytes=60 * 1024 * 1024),
        cost_estimate=estimate(coupling, count),
    )(shift, coupling, phonon, like)


def pair_call(pair, sources, args, add):
    operands = Operands()
    layout = [(offset, *[operands.place(place) for place in places]) for offset, *places in sources]

    def kernel(shift, coupling, phonon, pair_ref, *refs):
        out = refs[-1]
        out[...] = pair_ref[...]
        found = [(offset, *[at_refs(refs, p) for p in places]) for offset, *places in layout]
        add(out, found, shift, coupling, phonon, even_group())

    return pl.pallas_call(
        kernel,
        out_shape=jax.ShapeDtypeStruct(pair.shape, pair.dtype),
        in_specs=[SMEM] + [VMEM] * (len(args) + len(operands.arrays)),
        out_specs=VMEM,
        compiler_params=pltpu.CompilerParams(vmem_limit_bytes=LIMIT),
        cost_estimate=estimate(args[1], 1),
    )(*args, pair, *operands.arrays)


def add_call(energy, pair, pieces, out):
    _, parts, size, _ = out.shape
    arrays = [place[0] for place in pieces]

    def kernel(pair_ref, *refs):
        result = pair_ref[energy]
        for (_, _, at), ref in zip(pieces, refs):
            result = result + ref[at].astype(jnp.float32)
        refs[-1][0] = result.astype(out.dtype)

    return pl.pallas_call(
        kernel,
        grid=(1,),
        out_shape=jax.ShapeDtypeStruct(out.shape, out.dtype),
        in_specs=[VMEM] * (1 + len(arrays)) + [pl.BlockSpec(memory_space=pl.ANY)],
        out_specs=pl.BlockSpec((1, parts, size, size), lambda i: (i + energy, 0, 0, 0)),
        input_output_aliases={1 + len(arrays): 0},
        compiler_params=pltpu.CompilerParams(vmem_limit_bytes=LIMIT),
        cost_estimate=pl.CostEstimate(flops=1 << 33, bytes_accessed=1 << 24, transcendentals=0),
    )(pair, *arrays, out)


def finish_call(energies, whole, total, sources, pieces, args, out=None):
    _, parts, size, _ = whole
    operands = Operands()
    base = operands.add(total)
    layout = [(offset, operands.slots(slots, energies)) for offset, slots in sources]
    added = {energy: [operands.place(p) for p in pieces[energy]] for energy in energies}

    def kernel(*refs):
        shift, coupling, phonon = refs[: len(args)] if args else (None,) * 3
        refs = refs[len(args) :]
        even = even_group()
        for at, energy in enumerate(energies):

            @pl.when(pl.program_id(0) == at)
            def _():
                results = [refs[base][at, part] for part in range(2)]
                for offset, slots in layout:
                    slots = {slot: at_refs(refs, place) for slot, place in slots.items()}
                    found = terms(energy, offset, shift, coupling, phonon, slots, even)
                    results = [result + term for result, term in zip(results, found)]
                for part in range(2):
                    for place in added[energy]:
                        piece = load(at_refs(refs, place), even, part)
                        results[part] = results[part] + piece.astype(jnp.float32)
                    refs[-1][0, part] = results[part].astype(jnp.bfloat16)

    arrays = [*args, *operands.arrays]
    specs = [SMEM] * min(len(args), 1) + [VMEM] * (len(arrays) - min(len(args), 1))
    aliases = {}
    if out is not None:
        aliases = {len(arrays): 0}
        arrays.append(out)
        specs.append(pl.BlockSpec(memory_space=pl.ANY))
    first = energies[0]
    return pl.pallas_call(
        kernel,
        grid=(len(energies),),
        out_shape=jax.ShapeDtypeStruct(whole, jnp.bfloat16),
        in_specs=specs,
        out_specs=pl.BlockSpec((1, parts, size, size), lambda i: (i + first, 0, 0, 0)),
        input_output_aliases=aliases,
        compiler_params=pltpu.CompilerParams(vmem_limit_bytes=LIMIT),
        cost_estimate=pl.CostEstimate(flops=1 << 33, bytes_accessed=1 << 24, transcendentals=0),
    )(*arrays)


def body(green, coupling, phonon, shift):
    own = green[0, 0]
    whole = own.shape
    last = whole[0] - 1
    offsets = phonon.shape[0]
    radius = (offsets - 1) // 2
    ups = range(1, radius + 1)
    args = (shift.T, coupling, phonon)
    high = tuple(range(2, last + 1))

    def own_slots(block, below=None):
        slots = {energy: (block, block, energy) for energy in range(last + 1)}
        if below is not None:
            slots[-1] = (below, below, 0)
        return slots

    def send(energies, raw, *results, below=None, early=False):
        block = after(own, *results)
        made, arrived = {}, {}
        for q in ups:
            sources = [(radius - q, own_slots(block, below))]
            if early:
                made[q] = early_call(energies, radius - q, args, block)
            else:
                made[q] = sums_call(energies, sources, args, block, jnp.bfloat16, raw)
            ways = (-q, -q) if raw is None else (q, -q) if raw[1] else (-q, q)
            arrived[q] = passed_round(made[q], *ways)
        return list(made.values()), arrived

    own_top = own[last:]
    tops = {q: passed_round(own_top, q, q) for q in ups}
    made, high_1 = send(high, (1, True), own_top, early=True)
    below = passed_along(after(own_top, *made), "energy", 1)
    made, high_2 = send(high, (1, False), *made)
    block = after(own, *made)
    own_high = sums_call(high, [(radius, own_slots(block))], args, own, jnp.float32)
    pair = sums_call((0, 1), [(radius, own_slots(block, below))], args, own, jnp.float32)
    low = after(own, *made, *tops.values())[:1]
    lows = {q: passed_round(low, q, q) for q in ups}
    belows = {q: passed_along(after(tops[q], low), "energy", 1) for q in ups}
    made, second = send((1,), None, *made, low, *high_1.values())
    made, first = send((0,), None, *made, *high_2.values(), below=below)

    sources = []
    pieces = {energy: [] for energy in range(last + 1)}
    for q in ups:
        slots = {slot: (high_1[q], high_2[q], slot - 1) for slot in range(1, last)}
        slots[last] = (tops[q], tops[q], 0)
        slots[-1] = (belows[q], belows[q], 0)
        sources.append((radius + q, slots))
        for energy in high:
            pieces[energy].append((high_2[q], high_1[q], energy - 2))
        pieces[1].append((second[q], second[q], 0))
        pieces[0].append((first[q], first[q], 0))
    out = finish_call(high, whole, own_high, sources, pieces, args)
    edges = [(offset, slots[-1], slots[1]) for offset, slots in sources]
    pair = pair_call(pair, edges, args, add_edges)
    lowest = [(offset, (lows[q], lows[q], 0)) for q, (offset, _) in zip(ups, sources)]
    pair = pair_call(pair, lowest, args, add_low)
    out = add_call(1, pair, pieces[1], out)
    bottom = pair[:1]
    for (piece, _, at) in pieces[0]:
        bottom = bottom + piece[at : at + 1].astype(jnp.float32)
    out = lax.dynamic_update_slice(out, bottom.astype(out.dtype), (0, 0, 0, 0))
    return out[None, None]


def solution(mesh):
    placed = (P("mom", "energy", None, None, None, None), P(), P(), P())
    return jax.shard_map(
        body,
        mesh=mesh,
        in_specs=placed,
        out_specs=P("mom", "energy", None, None, None, None),
        check_vma=False,
    )
```

```python
import jax
import jax.numpy as jnp
from jax import lax
from jax.experimental import pallas as pl
from jax.experimental.pallas import tpu as pltpu
from jax.sharding import PartitionSpec as P

SMAX = 1
HBM = pl.BlockSpec(memory_space=pltpu.HBM)
VMEM = pl.BlockSpec(memory_space=pltpu.VMEM)
SMEM = pl.BlockSpec(memory_space=pltpu.SMEM)
LIMIT = 32 * 1024 * 1024


def passed_along(x, axis, by):
    length = lax.axis_size(axis)
    pairs = [(i, i + by) for i in range(length) if 0 <= i + by < length]
    return lax.ppermute(x, axis, pairs)


def passed_round(x, even_by, odd_by):
    groups, points = lax.axis_size("energy"), lax.axis_size("mom")
    pairs = []
    for group in range(groups):
        by = even_by if group % 2 == 0 else odd_by
        for point in range(points):
            pairs.append((group * points + point, group * points + (point + by) % points))
    return lax.ppermute(x, ("energy", "mom"), pairs)


def after(x, *results):
    return lax.optimization_barrier((x, *results))[0]


def even_group():
    return lax.rem(lax.axis_index("energy"), 2) == 0


def products(blocks, coupling):
    lefts = [
        jnp.dot(coupling, block, preferred_element_type=jnp.float32).astype(jnp.bfloat16)
        for block in blocks
    ]
    return [jnp.dot(left, coupling, preferred_element_type=jnp.float32) for left in lefts]


def load(place, even, part, back=0):
    first, second, at = place
    if first is second:
        return first[at - back, part]
    return jnp.where(even, first[at - back, part], second[at - back, part])


def terms(energy, offset, shift, coupling, phonon, slots, even):
    modes = coupling.shape[0]
    low, high = slots[energy - SMAX], slots[energy]
    sums = None
    for mode in range(modes):
        step = shift[mode, offset]
        if low[0] is high[0] and low[1] is high[1]:
            blocks = [load(high, even, part, step) for part in range(2)]
        else:
            blocks = [
                jnp.where(step > 0, load(low, even, part), load(high, even, part))
                for part in range(2)
            ]
        found = mode_terms(mode, offset, blocks, coupling, phonon)
        sums = found if sums is None else [x + y for x, y in zip(sums, found)]
    return sums


def mode_terms(mode, offset, blocks, coupling, phonon):
    size = coupling.shape[1]
    first, second = products(blocks, coupling[mode])
    real = phonon[offset, pl.ds(2 * mode * size, size), :].astype(jnp.float32)
    imag = phonon[offset, pl.ds((2 * mode + 1) * size, size), :].astype(jnp.float32)
    return [first * real - second * imag, first * imag + second * real]


def add_low(pair, sources, shift, coupling, phonon, even):
    for offset, place in sources:
        for mode in range(coupling.shape[0]):
            blocks = [load(place, even, part) for part in range(2)]
            found = mode_terms(mode, offset, blocks, coupling, phonon)
            step = shift[mode, offset]
            pair[step, 0] += found[0]
            pair[step, 1] += found[1]


def add_edges(pair, sources, shift, coupling, phonon, even):
    for offset, below, above in sources:
        for mode in range(coupling.shape[0]):
            step = shift[mode, offset]
            blocks = [
                jnp.where(step > 0, load(below, even, part), load(above, even, part))
                for part in range(2)
            ]
            found = mode_terms(mode, offset, blocks, coupling, phonon)
            pair[1 - step, 0] += found[0]
            pair[1 - step, 1] += found[1]


class Operands:
    def __init__(self):
        self.arrays = []

    def add(self, array):
        for n, other in enumerate(self.arrays):
            if other is array:
                return n
        self.arrays.append(array)
        return len(self.arrays) - 1

    def place(self, place):
        return (self.add(place[0]), self.add(place[1]), place[2])

    def slots(self, slots, energies):
        used = {slot for energy in energies for slot in (energy - SMAX, energy)}
        return {slot: self.place(slots[slot]) for slot in slots if slot in used}


def at_refs(refs, place):
    return (refs[place[0]], refs[place[1]], place[2])


def estimate(coupling, energies):
    modes, size, _ = coupling.shape
    flops = 128 * energies * modes * size**3
    return pl.CostEstimate(flops=flops, bytes_accessed=1 << 24, transcendentals=0)


def sums_call(energies, sources, args, like, dtype, raw=None):
    _, parts, size, _ = like.shape
    count = len(energies)
    operands = Operands()
    layout = [(offset, operands.slots(slots, energies)) for offset, slots in sources]
    source = operands.add(like) if raw is not None else None

    def kernel(shift, coupling, phonon, *refs):
        out = refs[-1]
        even = even_group()

        def sums():
            for at, energy in enumerate(energies):
                for n, (offset, slots) in enumerate(layout):
                    slots = {slot: at_refs(refs, place) for slot, place in slots.items()}
                    real, imag = terms(energy, offset, shift, coupling, phonon, slots, even)
                    if n > 0:
                        real, imag = real + out[at, 0], imag + out[at, 1]
                    out[at, 0] = real.astype(out.dtype)
                    out[at, 1] = imag.astype(out.dtype)

        if raw is None:
            sums()
        else:
            first, on_even = raw
            sends_raw = even if on_even else jnp.logical_not(even)

            @pl.when(sends_raw)
            def _():
                out[...] = refs[source][first : first + count]

            @pl.when(jnp.logical_not(sends_raw))
            def _():
                sums()

    return pl.pallas_call(
        kernel,
        out_shape=jax.ShapeDtypeStruct((count, parts, size, size), dtype),
        in_specs=[SMEM] + [VMEM] * (2 + len(operands.arrays)),
        out_specs=VMEM,
        compiler_params=pltpu.CompilerParams(vmem_limit_bytes=LIMIT),
        cost_estimate=estimate(args[1], count * len(sources)),
    )(*args, *operands.arrays)


def early_call(energies, offset, args, like):
    shift, coupling, phonon = args
    _, parts, size, _ = like.shape
    count, first = len(energies), energies[0] - SMAX

    def kernel(shift_hbm, coupling_hbm, phonon_hbm, own_hbm, out, *scratch):
        shift, coupling, phonon, own, sems = scratch
        pairs = [(own_hbm.at[pl.ds(first, count + SMAX)], own), (shift_hbm, shift)]
        pairs += [(coupling_hbm, coupling), (phonon_hbm.at[offset], phonon.at[offset])]
        copies = [pltpu.make_async_copy(*pair, sems.at[n]) for n, pair in enumerate(pairs)]
        even = even_group()
        copies[0].start()

        @pl.when(jnp.logical_not(even))
        def _():
            copies[0].wait()
            out[...] = own[:count]

        @pl.when(even)
        def _():
            for copy in copies[1:]:
                copy.start()
            for copy in copies:
                copy.wait()
            slots = {first + n: (own, own, n) for n in range(count + SMAX)}
            for at, energy in enumerate(energies):
                real, imag = terms(energy, offset, shift, coupling, phonon, slots, even)
                out[at, 0] = real.astype(out.dtype)
                out[at, 1] = imag.astype(out.dtype)

    return pl.pallas_call(
        kernel,
        out_shape=jax.ShapeDtypeStruct((count, parts, size, size), like.dtype),
        in_specs=[HBM] * 4,
        out_specs=VMEM,
        scratch_shapes=[
            pltpu.SMEM(shift.shape, shift.dtype),
            pltpu.VMEM(coupling.shape, coupling.dtype),
            pltpu.VMEM(phonon.shape, phonon.dtype),
            pltpu.VMEM((count + SMAX, parts, size, size), like.dtype),
            pltpu.SemaphoreType.DMA((4,)),
        ],
        compiler_params=pltpu.CompilerParams(vmem_limit_bytes=60 * 1024 * 1024),
        cost_estimate=estimate(coupling, count),
    )(shift, coupling, phonon, like)


def pair_call(pair, sources, args, add):
    operands = Operands()
    layout = [(offset, *[operands.place(place) for place in places]) for offset, *places in sources]

    def kernel(shift, coupling, phonon, pair_ref, *refs):
        out = refs[-1]
        out[...] = pair_ref[...]
        found = [(offset, *[at_refs(refs, p) for p in places]) for offset, *places in layout]
        add(out, found, shift, coupling, phonon, even_group())

    return pl.pallas_call(
        kernel,
        out_shape=jax.ShapeDtypeStruct(pair.shape, pair.dtype),
        in_specs=[SMEM] + [VMEM] * (len(args) + len(operands.arrays)),
        out_specs=VMEM,
        compiler_params=pltpu.CompilerParams(vmem_limit_bytes=LIMIT),
        cost_estimate=estimate(args[1], 1),
    )(*args, pair, *operands.arrays)


def add_call(energy, pair, pieces, out):
    _, parts, size, _ = out.shape
    arrays = [place[0] for place in pieces]

    def kernel(pair_ref, *refs):
        result = pair_ref[energy]
        for (_, _, at), ref in zip(pieces, refs):
            result = result + ref[at].astype(jnp.float32)
        refs[-1][0] = result.astype(out.dtype)

    return pl.pallas_call(
        kernel,
        grid=(1,),
        out_shape=jax.ShapeDtypeStruct(out.shape, out.dtype),
        in_specs=[VMEM] * (1 + len(arrays)) + [pl.BlockSpec(memory_space=pl.ANY)],
        out_specs=pl.BlockSpec((1, parts, size, size), lambda i: (i + energy, 0, 0, 0)),
        input_output_aliases={1 + len(arrays): 0},
        compiler_params=pltpu.CompilerParams(vmem_limit_bytes=LIMIT),
        cost_estimate=pl.CostEstimate(flops=1 << 33, bytes_accessed=1 << 24, transcendentals=0),
    )(pair, *arrays, out)


def finish_call(energies, whole, total, sources, pieces, args, out=None):
    _, parts, size, _ = whole
    operands = Operands()
    base = operands.add(total)
    layout = [(offset, operands.slots(slots, energies)) for offset, slots in sources]
    added = {energy: [operands.place(p) for p in pieces[energy]] for energy in energies}

    def kernel(*refs):
        shift, coupling, phonon = refs[: len(args)] if args else (None,) * 3
        refs = refs[len(args) :]
        even = even_group()
        for at, energy in enumerate(energies):

            @pl.when(pl.program_id(0) == at)
            def _():
                results = [refs[base][at, part] for part in range(2)]
                for offset, slots in layout:
                    slots = {slot: at_refs(refs, place) for slot, place in slots.items()}
                    found = terms(energy, offset, shift, coupling, phonon, slots, even)
                    results = [result + term for result, term in zip(results, found)]
                for part in range(2):
                    for place in added[energy]:
                        piece = load(at_refs(refs, place), even, part)
                        results[part] = results[part] + piece.astype(jnp.float32)
                    refs[-1][0, part] = results[part].astype(jnp.bfloat16)

    arrays = [*args, *operands.arrays]
    specs = [SMEM] * min(len(args), 1) + [VMEM] * (len(arrays) - min(len(args), 1))
    aliases = {}
    if out is not None:
        aliases = {len(arrays): 0}
        arrays.append(out)
        specs.append(pl.BlockSpec(memory_space=pl.ANY))
    first = energies[0]
    return pl.pallas_call(
        kernel,
        grid=(len(energies),),
        out_shape=jax.ShapeDtypeStruct(whole, jnp.bfloat16),
        in_specs=specs,
        out_specs=pl.BlockSpec((1, parts, size, size), lambda i: (i + first, 0, 0, 0)),
        input_output_aliases=aliases,
        compiler_params=pltpu.CompilerParams(vmem_limit_bytes=LIMIT),
        cost_estimate=pl.CostEstimate(flops=1 << 33, bytes_accessed=1 << 24, transcendentals=0),
    )(*arrays)


def body(green, coupling, phonon, shift):
    own = green[0, 0]
    whole = own.shape
    last = whole[0] - 1
    offsets = phonon.shape[0]
    radius = (offsets - 1) // 2
    ups = range(1, radius + 1)
    args = (shift.T, coupling, phonon)
    high = tuple(range(2, last + 1))

    def own_slots(block, below=None):
        slots = {energy: (block, block, energy) for energy in range(last + 1)}
        if below is not None:
            slots[-1] = (below, below, 0)
        return slots

    def send(energies, raw, *results, below=None, early=False):
        block = after(own, *results)
        made, arrived = {}, {}
        for q in ups:
            sources = [(radius - q, own_slots(block, below))]
            if early:
                made[q] = early_call(energies, radius - q, args, block)
            else:
                made[q] = sums_call(energies, sources, args, block, jnp.bfloat16, raw)
            ways = (-q, -q) if raw is None else (q, -q) if raw[1] else (-q, q)
            arrived[q] = passed_round(made[q], *ways)
        return list(made.values()), arrived

    own_top = own[last:]
    tops = {q: passed_round(own_top, q, q) for q in ups}
    made, high_1 = send(high, (1, False), own_top, early=True)
    below = passed_along(after(own_top, *made), "energy", 1)
    made, high_2 = send(high, (1, True), *made)
    block = after(own, *made)
    own_high = sums_call(high, [(radius, own_slots(block))], args, own, jnp.float32)
    pair = sums_call((0, 1), [(radius, own_slots(block, below))], args, own, jnp.float32)
    low = after(own, *made, *tops.values())[:1]
    lows = {q: passed_round(low, q, q) for q in ups}
    belows = {q: passed_along(after(tops[q], low), "energy", 1) for q in ups}
    made, second = send((1,), None, *made, low, *high_1.values())
    made, first = send((0,), None, *made, *high_2.values(), below=below)

    sources = []
    pieces = {energy: [] for energy in range(last + 1)}
    for q in ups:
        slots = {slot: (high_2[q], high_1[q], slot - 1) for slot in range(1, last)}
        slots[last] = (tops[q], tops[q], 0)
        slots[-1] = (belows[q], belows[q], 0)
        sources.append((radius + q, slots))
        for energy in high:
            pieces[energy].append((high_1[q], high_2[q], energy - 2))
        pieces[1].append((second[q], second[q], 0))
        pieces[0].append((first[q], first[q], 0))
    out = finish_call(high, whole, own_high, sources, pieces, args)
    edges = [(offset, slots[-1], slots[1]) for offset, slots in sources]
    pair = pair_call(pair, edges, args, add_edges)
    lowest = [(offset, (lows[q], lows[q], 0)) for q, (offset, _) in zip(ups, sources)]
    pair = pair_call(pair, lowest, args, add_low)
    for energy in (1, 0):
        out = add_call(energy, pair, pieces[energy], out)
    return out[None, None]


def solution(mesh):
    placed = (P("mom", "energy", None, None, None, None), P(), P(), P())
    return jax.shard_map(
        body,
        mesh=mesh,
        in_specs=placed,
        out_specs=P("mom", "energy", None, None, None, None),
        check_vma=False,
    )
```

```python
import jax
import jax.numpy as jnp
from jax import lax
from jax.experimental import pallas as pl
from jax.experimental.pallas import tpu as pltpu
from jax.sharding import PartitionSpec as P

SMAX = 1
HBM = pl.BlockSpec(memory_space=pltpu.HBM)
VMEM = pl.BlockSpec(memory_space=pltpu.VMEM)
SMEM = pl.BlockSpec(memory_space=pltpu.SMEM)
LIMIT = 32 * 1024 * 1024


def passed_along(x, axis, by):
    length = lax.axis_size(axis)
    pairs = [(i, i + by) for i in range(length) if 0 <= i + by < length]
    return lax.ppermute(x, axis, pairs)


def passed_round(x, even_by, odd_by):
    groups, points = lax.axis_size("energy"), lax.axis_size("mom")
    pairs = []
    for group in range(groups):
        by = even_by if group % 2 == 0 else odd_by
        for point in range(points):
            pairs.append((group * points + point, group * points + (point + by) % points))
    return lax.ppermute(x, ("energy", "mom"), pairs)


def passed_apart(x, by, around):
    length = lax.axis_size("mom")
    steps = [(i, i + by) for i in range(length)]
    pairs = [(i, j % length) for i, j in steps if (0 <= j < length) != around]
    return lax.ppermute(x, "mom", pairs)


def after(x, *results):
    return lax.optimization_barrier((x, *results))[0]


def even_group():
    return lax.rem(lax.axis_index("energy"), 2) == 0


def products(blocks, coupling):
    lefts = [
        jnp.dot(coupling, block, preferred_element_type=jnp.float32).astype(jnp.bfloat16)
        for block in blocks
    ]
    return [jnp.dot(left, coupling, preferred_element_type=jnp.float32) for left in lefts]


def load(place, even, part, back=0):
    first, second, at = place
    if first is second:
        return first[at - back, part]
    return jnp.where(even, first[at - back, part], second[at - back, part])


def terms(energy, offset, shift, coupling, phonon, slots, even):
    modes = coupling.shape[0]
    low, high = slots[energy - SMAX], slots[energy]
    sums = None
    for mode in range(modes):
        step = shift[mode, offset]
        if low[0] is high[0] and low[1] is high[1]:
            blocks = [load(high, even, part, step) for part in range(2)]
        else:
            blocks = [
                jnp.where(step > 0, load(low, even, part), load(high, even, part))
                for part in range(2)
            ]
        found = mode_terms(mode, offset, blocks, coupling, phonon)
        sums = found if sums is None else [x + y for x, y in zip(sums, found)]
    return sums


def mode_terms(mode, offset, blocks, coupling, phonon):
    size = coupling.shape[1]
    first, second = products(blocks, coupling[mode])
    real = phonon[offset, pl.ds(2 * mode * size, size), :].astype(jnp.float32)
    imag = phonon[offset, pl.ds((2 * mode + 1) * size, size), :].astype(jnp.float32)
    return [first * real - second * imag, first * imag + second * real]


def add_low(pair, sources, shift, coupling, phonon, even):
    for offset, place in sources:
        for mode in range(coupling.shape[0]):
            blocks = [load(place, even, part) for part in range(2)]
            found = mode_terms(mode, offset, blocks, coupling, phonon)
            step = shift[mode, offset]
            pair[step, 0] += found[0]
            pair[step, 1] += found[1]


def add_edges(pair, sources, shift, coupling, phonon, even):
    for offset, below, above in sources:
        for mode in range(coupling.shape[0]):
            step = shift[mode, offset]
            blocks = [
                jnp.where(step > 0, load(below, even, part), load(above, even, part))
                for part in range(2)
            ]
            found = mode_terms(mode, offset, blocks, coupling, phonon)
            pair[1 - step, 0] += found[0]
            pair[1 - step, 1] += found[1]


class Operands:
    def __init__(self):
        self.arrays = []

    def add(self, array):
        for n, other in enumerate(self.arrays):
            if other is array:
                return n
        self.arrays.append(array)
        return len(self.arrays) - 1

    def place(self, place):
        return (self.add(place[0]), self.add(place[1]), place[2])

    def slots(self, slots, energies):
        used = {slot for energy in energies for slot in (energy - SMAX, energy)}
        return {slot: self.place(slots[slot]) for slot in slots if slot in used}


def at_refs(refs, place):
    return (refs[place[0]], refs[place[1]], place[2])


def estimate(coupling, energies):
    modes, size, _ = coupling.shape
    flops = 128 * energies * modes * size**3
    return pl.CostEstimate(flops=flops, bytes_accessed=1 << 24, transcendentals=0)


def sums_call(energies, sources, args, like, dtype, raw=None):
    _, parts, size, _ = like.shape
    count = len(energies)
    operands = Operands()
    layout = [(offset, operands.slots(slots, energies)) for offset, slots in sources]
    source = operands.add(like) if raw is not None else None

    def kernel(shift, coupling, phonon, *refs):
        out = refs[-1]
        even = even_group()

        def sums():
            for at, energy in enumerate(energies):
                for n, (offset, slots) in enumerate(layout):
                    slots = {slot: at_refs(refs, place) for slot, place in slots.items()}
                    real, imag = terms(energy, offset, shift, coupling, phonon, slots, even)
                    if n > 0:
                        real, imag = real + out[at, 0], imag + out[at, 1]
                    out[at, 0] = real.astype(out.dtype)
                    out[at, 1] = imag.astype(out.dtype)

        if raw is None:
            sums()
        else:
            first, on_even = raw
            sends_raw = even if on_even else jnp.logical_not(even)

            @pl.when(sends_raw)
            def _():
                out[...] = refs[source][first : first + count]

            @pl.when(jnp.logical_not(sends_raw))
            def _():
                sums()

    return pl.pallas_call(
        kernel,
        out_shape=jax.ShapeDtypeStruct((count, parts, size, size), dtype),
        in_specs=[SMEM] + [VMEM] * (2 + len(operands.arrays)),
        out_specs=VMEM,
        compiler_params=pltpu.CompilerParams(vmem_limit_bytes=LIMIT),
        cost_estimate=estimate(args[1], count * len(sources)),
    )(*args, *operands.arrays)


def early_call(energies, offset, args, like):
    shift, coupling, phonon = args
    _, parts, size, _ = like.shape
    count, first = len(energies), energies[0] - SMAX

    def kernel(shift_hbm, coupling_hbm, phonon_hbm, own_hbm, out, *scratch):
        shift, coupling, phonon, own, sems = scratch
        pairs = [(own_hbm.at[pl.ds(first, count + SMAX)], own), (shift_hbm, shift)]
        pairs += [(coupling_hbm, coupling), (phonon_hbm.at[offset], phonon.at[offset])]
        copies = [pltpu.make_async_copy(*pair, sems.at[n]) for n, pair in enumerate(pairs)]
        even = even_group()
        copies[0].start()

        @pl.when(even)
        def _():
            copies[0].wait()
            out[...] = own[:count]

        @pl.when(jnp.logical_not(even))
        def _():
            for copy in copies[1:]:
                copy.start()
            for copy in copies:
                copy.wait()
            slots = {first + n: (own, own, n) for n in range(count + SMAX)}
            for at, energy in enumerate(energies):
                real, imag = terms(energy, offset, shift, coupling, phonon, slots, even)
                out[at, 0] = real.astype(out.dtype)
                out[at, 1] = imag.astype(out.dtype)

    return pl.pallas_call(
        kernel,
        out_shape=jax.ShapeDtypeStruct((count, parts, size, size), like.dtype),
        in_specs=[HBM] * 4,
        out_specs=VMEM,
        scratch_shapes=[
            pltpu.SMEM(shift.shape, shift.dtype),
            pltpu.VMEM(coupling.shape, coupling.dtype),
            pltpu.VMEM(phonon.shape, phonon.dtype),
            pltpu.VMEM((count + SMAX, parts, size, size), like.dtype),
            pltpu.SemaphoreType.DMA((4,)),
        ],
        compiler_params=pltpu.CompilerParams(vmem_limit_bytes=60 * 1024 * 1024),
        cost_estimate=estimate(coupling, count),
    )(shift, coupling, phonon, like)


def pair_call(pair, sources, args, add):
    operands = Operands()
    layout = [(offset, *[operands.place(place) for place in places]) for offset, *places in sources]

    def kernel(shift, coupling, phonon, pair_ref, *refs):
        out = refs[-1]
        out[...] = pair_ref[...]
        found = [(offset, *[at_refs(refs, p) for p in places]) for offset, *places in layout]
        add(out, found, shift, coupling, phonon, even_group())

    return pl.pallas_call(
        kernel,
        out_shape=jax.ShapeDtypeStruct(pair.shape, pair.dtype),
        in_specs=[SMEM] + [VMEM] * (len(args) + len(operands.arrays)),
        out_specs=VMEM,
        compiler_params=pltpu.CompilerParams(vmem_limit_bytes=LIMIT),
        cost_estimate=estimate(args[1], 1),
    )(*args, pair, *operands.arrays)


def add_call(pair, along, out):
    _, parts, size, _ = out.shape

    def kernel(pair_ref, *refs):
        at = pl.program_id(0)
        result = pair_ref[at]
        for ref in refs[: len(along)]:
            result = result + ref[at].astype(jnp.float32)
        refs[-1][0] = result.astype(out.dtype)

    return pl.pallas_call(
        kernel,
        grid=(2,),
        out_shape=jax.ShapeDtypeStruct(out.shape, out.dtype),
        in_specs=[VMEM] * (1 + len(along)) + [pl.BlockSpec(memory_space=pl.ANY)],
        out_specs=pl.BlockSpec((1, parts, size, size), lambda i: (i, 0, 0, 0)),
        input_output_aliases={1 + len(along): 0},
        compiler_params=pltpu.CompilerParams(vmem_limit_bytes=LIMIT),
        cost_estimate=pl.CostEstimate(flops=1 << 33, bytes_accessed=1 << 24, transcendentals=0),
    )(pair, *along, out)


def ends_call(pair, along, around, out):
    _, parts, size, _ = out.shape
    count = len(along)

    def kernel(pair_ref, *refs):
        out_ref, made, sem = refs[-3:]

        @pl.when(lax.axis_index("mom") >= lax.axis_size("mom") - count)
        def _():
            result = pair_ref[...]
            for ref in refs[: 2 * count]:
                result = result + ref[...].astype(jnp.float32)
            made[...] = result.astype(made.dtype)
            copy = pltpu.make_async_copy(made, out_ref.at[pl.ds(0, 2)], sem)
            copy.start()
            copy.wait()

    return pl.pallas_call(
        kernel,
        out_shape=jax.ShapeDtypeStruct(out.shape, out.dtype),
        in_specs=[VMEM] * (1 + 2 * count) + [pl.BlockSpec(memory_space=pl.ANY)],
        out_specs=pl.BlockSpec(memory_space=pl.ANY),
        scratch_shapes=[pltpu.VMEM((2, parts, size, size), out.dtype), pltpu.SemaphoreType.DMA],
        input_output_aliases={1 + 2 * count: 0},
        compiler_params=pltpu.CompilerParams(vmem_limit_bytes=LIMIT),
        cost_estimate=pl.CostEstimate(flops=1 << 33, bytes_accessed=1 << 24, transcendentals=0),
    )(pair, *along, *around, out)


def finish_call(energies, whole, total, sources, pieces, args, out=None):
    _, parts, size, _ = whole
    operands = Operands()
    base = operands.add(total)
    layout = [(offset, operands.slots(slots, energies)) for offset, slots in sources]
    added = {energy: [operands.place(p) for p in pieces[energy]] for energy in energies}

    def kernel(*refs):
        shift, coupling, phonon = refs[: len(args)] if args else (None,) * 3
        refs = refs[len(args) :]
        even = even_group()
        for at, energy in enumerate(energies):

            @pl.when(pl.program_id(0) == at)
            def _():
                results = [refs[base][at, part] for part in range(2)]
                for offset, slots in layout:
                    slots = {slot: at_refs(refs, place) for slot, place in slots.items()}
                    found = terms(energy, offset, shift, coupling, phonon, slots, even)
                    results = [result + term for result, term in zip(results, found)]
                for part in range(2):
                    for place in added[energy]:
                        piece = load(at_refs(refs, place), even, part)
                        results[part] = results[part] + piece.astype(jnp.float32)
                    refs[-1][0, part] = results[part].astype(jnp.bfloat16)

    arrays = [*args, *operands.arrays]
    specs = [SMEM] * min(len(args), 1) + [VMEM] * (len(arrays) - min(len(args), 1))
    aliases = {}
    if out is not None:
        aliases = {len(arrays): 0}
        arrays.append(out)
        specs.append(pl.BlockSpec(memory_space=pl.ANY))
    first = energies[0]
    return pl.pallas_call(
        kernel,
        grid=(len(energies),),
        out_shape=jax.ShapeDtypeStruct(whole, jnp.bfloat16),
        in_specs=specs,
        out_specs=pl.BlockSpec((1, parts, size, size), lambda i: (i + first, 0, 0, 0)),
        input_output_aliases=aliases,
        compiler_params=pltpu.CompilerParams(vmem_limit_bytes=LIMIT),
        cost_estimate=pl.CostEstimate(flops=1 << 33, bytes_accessed=1 << 24, transcendentals=0),
    )(*arrays)


def body(green, coupling, phonon, shift):
    own = green[0, 0]
    whole = own.shape
    last = whole[0] - 1
    offsets = phonon.shape[0]
    radius = (offsets - 1) // 2
    ups = range(1, radius + 1)
    args = (shift.T, coupling, phonon)
    high = tuple(range(2, last + 1))

    def own_slots(block, below=None):
        slots = {energy: (block, block, energy) for energy in range(last + 1)}
        if below is not None:
            slots[-1] = (below, below, 0)
        return slots

    def send(energies, raw, *results, below=None, early=False):
        block = after(own, *results)
        made, arrived = {}, {}
        for q in ups:
            sources = [(radius - q, own_slots(block, below))]
            if early:
                made[q] = early_call(energies, radius - q, args, block)
            else:
                made[q] = sums_call(energies, sources, args, block, jnp.bfloat16, raw)
            ways = (-q, -q) if raw is None else (q, -q) if raw[1] else (-q, q)
            arrived[q] = passed_round(made[q], *ways)
        return list(made.values()), arrived

    own_top = own[last:]
    tops = {q: passed_round(own_top, q, q) for q in ups}
    made, high_1 = send(high, (1, True), own_top, early=True)
    below = passed_along(after(own_top, *made), "energy", 1)
    made, high_2 = send(high, (1, False), *made)
    block = after(own, *made)
    own_high = sums_call(high, [(radius, own_slots(block))], args, own, jnp.float32)
    pair = sums_call((0, 1), [(radius, own_slots(block, below))], args, own, jnp.float32)
    low = after(own, *made, *tops.values())[:1]
    lows = {q: passed_round(low, q, q) for q in ups}
    belows = {q: passed_along(after(tops[q], low), "energy", 1) for q in ups}
    block = after(own, *made, low, *high_1.values())
    along, around = {}, {}
    for q in ups:
        sources = [(radius - q, own_slots(block, below))]
        made_low = sums_call((0, 1), sources, args, block, jnp.bfloat16)
        along[q] = passed_apart(made_low, -q, False)
        around[q] = passed_apart(made_low, -q, True)

    sources = []
    pieces = {energy: [] for energy in range(last + 1)}
    for q in ups:
        slots = {slot: (high_1[q], high_2[q], slot - 1) for slot in range(1, last)}
        slots[last] = (tops[q], tops[q], 0)
        slots[-1] = (belows[q], belows[q], 0)
        sources.append((radius + q, slots))
        for energy in high:
            pieces[energy].append((high_2[q], high_1[q], energy - 2))
    out = finish_call(high, whole, own_high, sources, pieces, args)
    edges = [(offset, slots[-1], slots[1]) for offset, slots in sources]
    pair = pair_call(pair, edges, args, add_edges)
    lowest = [(offset, (lows[q], lows[q], 0)) for q, (offset, _) in zip(ups, sources)]
    pair = pair_call(pair, lowest, args, add_low)
    out = add_call(pair, list(along.values()), out)
    out = ends_call(pair, list(along.values()), list(around.values()), out)
    return out[None, None]


def solution(mesh):
    placed = (P("mom", "energy", None, None, None, None), P(), P(), P())
    return jax.shard_map(
        body,
        mesh=mesh,
        in_specs=placed,
        out_specs=P("mom", "energy", None, None, None, None),
        check_vma=False,
    )
```

```python
import jax
import jax.numpy as jnp
from jax import lax
from jax.experimental import pallas as pl
from jax.experimental.pallas import tpu as pltpu
from jax.sharding import PartitionSpec as P

SMAX = 1
HBM = pl.BlockSpec(memory_space=pltpu.HBM)
VMEM = pl.BlockSpec(memory_space=pltpu.VMEM)
SMEM = pl.BlockSpec(memory_space=pltpu.SMEM)
LIMIT = 32 * 1024 * 1024


def passed_along(x, axis, by):
    length = lax.axis_size(axis)
    pairs = [(i, i + by) for i in range(length) if 0 <= i + by < length]
    return lax.ppermute(x, axis, pairs)


def passed_round(x, even_by, odd_by):
    groups, points = lax.axis_size("energy"), lax.axis_size("mom")
    pairs = []
    for group in range(groups):
        by = even_by if group % 2 == 0 else odd_by
        for point in range(points):
            pairs.append((group * points + point, group * points + (point + by) % points))
    return lax.ppermute(x, ("energy", "mom"), pairs)


def after(x, *results):
    return lax.optimization_barrier((x, *results))[0]


def even_group():
    return lax.rem(lax.axis_index("energy"), 2) == 0


def products(blocks, coupling):
    lefts = [
        jnp.dot(coupling, block, preferred_element_type=jnp.float32).astype(jnp.bfloat16)
        for block in blocks
    ]
    return [jnp.dot(left, coupling, preferred_element_type=jnp.float32) for left in lefts]


def load(place, even, part, back=0):
    first, second, at = place
    if first is second:
        return first[at - back, part]
    return jnp.where(even, first[at - back, part], second[at - back, part])


def terms(energy, offset, shift, coupling, phonon, slots, even):
    modes = coupling.shape[0]
    low, high = slots[energy - SMAX], slots[energy]
    sums = None
    for mode in range(modes):
        step = shift[mode, offset]
        if low[0] is high[0] and low[1] is high[1]:
            blocks = [load(high, even, part, step) for part in range(2)]
        else:
            blocks = [
                jnp.where(step > 0, load(low, even, part), load(high, even, part))
                for part in range(2)
            ]
        found = mode_terms(mode, offset, blocks, coupling, phonon)
        sums = found if sums is None else [x + y for x, y in zip(sums, found)]
    return sums


def mode_terms(mode, offset, blocks, coupling, phonon):
    size = coupling.shape[1]
    first, second = products(blocks, coupling[mode])
    real = phonon[offset, pl.ds(2 * mode * size, size), :].astype(jnp.float32)
    imag = phonon[offset, pl.ds((2 * mode + 1) * size, size), :].astype(jnp.float32)
    return [first * real - second * imag, first * imag + second * real]


def add_low(pair, sources, shift, coupling, phonon, even):
    for offset, place in sources:
        for mode in range(coupling.shape[0]):
            blocks = [load(place, even, part) for part in range(2)]
            found = mode_terms(mode, offset, blocks, coupling, phonon)
            step = shift[mode, offset]
            pair[step, 0] += found[0]
            pair[step, 1] += found[1]


def add_edges(pair, sources, shift, coupling, phonon, even):
    for offset, below, above in sources:
        for mode in range(coupling.shape[0]):
            step = shift[mode, offset]
            blocks = [
                jnp.where(step > 0, load(below, even, part), load(above, even, part))
                for part in range(2)
            ]
            found = mode_terms(mode, offset, blocks, coupling, phonon)
            pair[1 - step, 0] += found[0]
            pair[1 - step, 1] += found[1]


class Operands:
    def __init__(self):
        self.arrays = []

    def add(self, array):
        for n, other in enumerate(self.arrays):
            if other is array:
                return n
        self.arrays.append(array)
        return len(self.arrays) - 1

    def place(self, place):
        return (self.add(place[0]), self.add(place[1]), place[2])

    def slots(self, slots, energies):
        used = {slot for energy in energies for slot in (energy - SMAX, energy)}
        return {slot: self.place(slots[slot]) for slot in slots if slot in used}


def at_refs(refs, place):
    return (refs[place[0]], refs[place[1]], place[2])


def estimate(coupling, energies):
    modes, size, _ = coupling.shape
    flops = 128 * energies * modes * size**3
    return pl.CostEstimate(flops=flops, bytes_accessed=1 << 24, transcendentals=0)


def sums_call(energies, sources, args, like, dtype, raw=None):
    _, parts, size, _ = like.shape
    count = len(energies)
    operands = Operands()
    layout = [(offset, operands.slots(slots, energies)) for offset, slots in sources]
    source = operands.add(like) if raw is not None else None

    def kernel(shift, coupling, phonon, *refs):
        out = refs[-1]
        even = even_group()

        def sums():
            for at, energy in enumerate(energies):
                for n, (offset, slots) in enumerate(layout):
                    slots = {slot: at_refs(refs, place) for slot, place in slots.items()}
                    real, imag = terms(energy, offset, shift, coupling, phonon, slots, even)
                    if n > 0:
                        real, imag = real + out[at, 0], imag + out[at, 1]
                    out[at, 0] = real.astype(out.dtype)
                    out[at, 1] = imag.astype(out.dtype)

        if raw is None:
            sums()
        else:
            first, on_even = raw
            sends_raw = even if on_even else jnp.logical_not(even)

            @pl.when(sends_raw)
            def _():
                out[...] = refs[source][first : first + count]

            @pl.when(jnp.logical_not(sends_raw))
            def _():
                sums()

    return pl.pallas_call(
        kernel,
        out_shape=jax.ShapeDtypeStruct((count, parts, size, size), dtype),
        in_specs=[SMEM] + [VMEM] * (2 + len(operands.arrays)),
        out_specs=VMEM,
        compiler_params=pltpu.CompilerParams(vmem_limit_bytes=LIMIT),
        cost_estimate=estimate(args[1], count * len(sources)),
    )(*args, *operands.arrays)


def early_call(energies, offset, args, like):
    shift, coupling, phonon = args
    _, parts, size, _ = like.shape
    count, first = len(energies), energies[0] - SMAX

    def kernel(shift_hbm, coupling_hbm, phonon_hbm, own_hbm, out, *scratch):
        shift, coupling, phonon, own, sems = scratch
        pairs = [(own_hbm.at[pl.ds(first, count + SMAX)], own), (shift_hbm, shift)]
        pairs += [(coupling_hbm, coupling), (phonon_hbm.at[offset], phonon.at[offset])]
        copies = [pltpu.make_async_copy(*pair, sems.at[n]) for n, pair in enumerate(pairs)]
        even = even_group()
        copies[0].start()

        @pl.when(even)
        def _():
            copies[0].wait()
            out[...] = own[:count]

        @pl.when(jnp.logical_not(even))
        def _():
            for copy in copies[1:]:
                copy.start()
            for copy in copies:
                copy.wait()
            slots = {first + n: (own, own, n) for n in range(count + SMAX)}
            for at, energy in enumerate(energies):
                real, imag = terms(energy, offset, shift, coupling, phonon, slots, even)
                out[at, 0] = real.astype(out.dtype)
                out[at, 1] = imag.astype(out.dtype)

    return pl.pallas_call(
        kernel,
        out_shape=jax.ShapeDtypeStruct((count, parts, size, size), like.dtype),
        in_specs=[HBM] * 4,
        out_specs=VMEM,
        scratch_shapes=[
            pltpu.SMEM(shift.shape, shift.dtype),
            pltpu.VMEM(coupling.shape, coupling.dtype),
            pltpu.VMEM(phonon.shape, phonon.dtype),
            pltpu.VMEM((count + SMAX, parts, size, size), like.dtype),
            pltpu.SemaphoreType.DMA((4,)),
        ],
        compiler_params=pltpu.CompilerParams(vmem_limit_bytes=60 * 1024 * 1024),
        cost_estimate=estimate(coupling, count),
    )(shift, coupling, phonon, like)


def pair_call(pair, sources, args, add):
    operands = Operands()
    layout = [(offset, *[operands.place(place) for place in places]) for offset, *places in sources]

    def kernel(shift, coupling, phonon, pair_ref, *refs):
        out = refs[-1]
        out[...] = pair_ref[...]
        found = [(offset, *[at_refs(refs, p) for p in places]) for offset, *places in layout]
        add(out, found, shift, coupling, phonon, even_group())

    return pl.pallas_call(
        kernel,
        out_shape=jax.ShapeDtypeStruct(pair.shape, pair.dtype),
        in_specs=[SMEM] + [VMEM] * (len(args) + len(operands.arrays)),
        out_specs=VMEM,
        compiler_params=pltpu.CompilerParams(vmem_limit_bytes=LIMIT),
        cost_estimate=estimate(args[1], 1),
    )(*args, pair, *operands.arrays)


def add_call(energy, pair, pieces, out):
    _, parts, size, _ = out.shape
    arrays = [place[0] for place in pieces]

    def kernel(pair_ref, *refs):
        result = pair_ref[energy]
        for (_, _, at), ref in zip(pieces, refs):
            result = result + ref[at].astype(jnp.float32)
        refs[-1][0] = result.astype(out.dtype)

    return pl.pallas_call(
        kernel,
        grid=(1,),
        out_shape=jax.ShapeDtypeStruct(out.shape, out.dtype),
        in_specs=[VMEM] * (1 + len(arrays)) + [pl.BlockSpec(memory_space=pl.ANY)],
        out_specs=pl.BlockSpec((1, parts, size, size), lambda i: (i + energy, 0, 0, 0)),
        input_output_aliases={1 + len(arrays): 0},
        compiler_params=pltpu.CompilerParams(vmem_limit_bytes=LIMIT),
        cost_estimate=pl.CostEstimate(flops=1 << 33, bytes_accessed=1 << 24, transcendentals=0),
    )(pair, *arrays, out)


def top_call(own, limit):
    last = own.shape[0] - 1

    def kernel(own_ref, out_ref, sem):
        copy = pltpu.make_async_copy(own_ref.at[pl.ds(last, 1)], out_ref, sem)
        copy.start()
        copy.wait()

    return pl.pallas_call(
        kernel,
        out_shape=jax.ShapeDtypeStruct((1,) + own.shape[1:], own.dtype),
        in_specs=[HBM],
        out_specs=VMEM,
        scratch_shapes=[pltpu.SemaphoreType.DMA],
        compiler_params=pltpu.CompilerParams(vmem_limit_bytes=limit),
        cost_estimate=pl.CostEstimate(flops=0, bytes_accessed=1 << 20, transcendentals=0),
    )(own)


def finish_call(energies, whole, total, sources, pieces, args, out=None):
    _, parts, size, _ = whole
    operands = Operands()
    base = operands.add(total)
    layout = [(offset, operands.slots(slots, energies)) for offset, slots in sources]
    added = {energy: [operands.place(p) for p in pieces[energy]] for energy in energies}

    def kernel(*refs):
        shift, coupling, phonon = refs[: len(args)] if args else (None,) * 3
        refs = refs[len(args) :]
        even = even_group()
        for at, energy in enumerate(energies):

            @pl.when(pl.program_id(0) == at)
            def _():
                results = [refs[base][at, part] for part in range(2)]
                for offset, slots in layout:
                    slots = {slot: at_refs(refs, place) for slot, place in slots.items()}
                    found = terms(energy, offset, shift, coupling, phonon, slots, even)
                    results = [result + term for result, term in zip(results, found)]
                for part in range(2):
                    for place in added[energy]:
                        piece = load(at_refs(refs, place), even, part)
                        results[part] = results[part] + piece.astype(jnp.float32)
                    refs[-1][0, part] = results[part].astype(jnp.bfloat16)

    arrays = [*args, *operands.arrays]
    specs = [SMEM] * min(len(args), 1) + [VMEM] * (len(arrays) - min(len(args), 1))
    aliases = {}
    if out is not None:
        aliases = {len(arrays): 0}
        arrays.append(out)
        specs.append(pl.BlockSpec(memory_space=pl.ANY))
    first = energies[0]
    return pl.pallas_call(
        kernel,
        grid=(len(energies),),
        out_shape=jax.ShapeDtypeStruct(whole, jnp.bfloat16),
        in_specs=specs,
        out_specs=pl.BlockSpec((1, parts, size, size), lambda i: (i + first, 0, 0, 0)),
        input_output_aliases=aliases,
        compiler_params=pltpu.CompilerParams(vmem_limit_bytes=LIMIT),
        cost_estimate=pl.CostEstimate(flops=1 << 33, bytes_accessed=1 << 24, transcendentals=0),
    )(*arrays)


def body(green, coupling, phonon, shift):
    own = green[0, 0]
    whole = own.shape
    last = whole[0] - 1
    offsets = phonon.shape[0]
    radius = (offsets - 1) // 2
    ups = range(1, radius + 1)
    args = (shift.T, coupling, phonon)
    high = tuple(range(2, last + 1))

    def own_slots(block, below=None):
        slots = {energy: (block, block, energy) for energy in range(last + 1)}
        if below is not None:
            slots[-1] = (below, below, 0)
        return slots

    def send(energies, raw, *results, below=None, early=False):
        block = after(own, *results)
        made, arrived = {}, {}
        for q in ups:
            sources = [(radius - q, own_slots(block, below))]
            if early:
                made[q] = early_call(energies, radius - q, args, block)
            else:
                made[q] = sums_call(energies, sources, args, block, jnp.bfloat16, raw)
            ways = (-q, -q) if raw is None else (q, -q) if raw[1] else (-q, q)
            arrived[q] = passed_round(made[q], *ways)
        return list(made.values()), arrived

    own_top = top_call(own, 53 * 1024 * 1024)
    tops = {q: passed_round(own_top, q, q) for q in ups}
    made, high_1 = send(high, (1, True), own_top, early=True)
    below = passed_along(after(own_top, *made), "energy", 1)
    made, high_2 = send(high, (1, False), *made)
    block = after(own, *made)
    own_high = sums_call(high, [(radius, own_slots(block))], args, own, jnp.float32)
    pair = sums_call((0, 1), [(radius, own_slots(block, below))], args, own, jnp.float32)
    low = after(own, *made, *tops.values())[:1]
    lows = {q: passed_round(low, q, q) for q in ups}
    belows = {q: passed_along(after(tops[q], low), "energy", 1) for q in ups}
    made, second = send((1,), None, *made, low, *high_1.values())
    made, first = send((0,), None, *made, *high_2.values(), below=below)

    sources = []
    pieces = {energy: [] for energy in range(last + 1)}
    for q in ups:
        slots = {slot: (high_1[q], high_2[q], slot - 1) for slot in range(1, last)}
        slots[last] = (tops[q], tops[q], 0)
        slots[-1] = (belows[q], belows[q], 0)
        sources.append((radius + q, slots))
        for energy in high:
            pieces[energy].append((high_2[q], high_1[q], energy - 2))
        pieces[1].append((second[q], second[q], 0))
        pieces[0].append((first[q], first[q], 0))
    out = finish_call(high, whole, own_high, sources, pieces, args)
    edges = [(offset, slots[-1], slots[1]) for offset, slots in sources]
    pair = pair_call(pair, edges, args, add_edges)
    lowest = [(offset, (lows[q], lows[q], 0)) for q, (offset, _) in zip(ups, sources)]
    pair = pair_call(pair, lowest, args, add_low)
    for energy in (1, 0):
        out = add_call(energy, pair, pieces[energy], out)
    return out[None, None]


def solution(mesh):
    placed = (P("mom", "energy", None, None, None, None), P(), P(), P())
    return jax.shard_map(
        body,
        mesh=mesh,
        in_specs=placed,
        out_specs=P("mom", "energy", None, None, None, None),
        check_vma=False,
    )
```

```python
import jax
import jax.numpy as jnp
from jax import lax
from jax.experimental import pallas as pl
from jax.experimental.pallas import tpu as pltpu
from jax.sharding import PartitionSpec as P

SMAX = 1
HBM = pl.BlockSpec(memory_space=pltpu.HBM)
VMEM = pl.BlockSpec(memory_space=pltpu.VMEM)
SMEM = pl.BlockSpec(memory_space=pltpu.SMEM)
LIMIT = 32 * 1024 * 1024


def passed_along(x, axis, by):
    length = lax.axis_size(axis)
    pairs = [(i, i + by) for i in range(length) if 0 <= i + by < length]
    return lax.ppermute(x, axis, pairs)


def passed_round(x, even_by, odd_by):
    groups, points = lax.axis_size("energy"), lax.axis_size("mom")
    pairs = []
    for group in range(groups):
        by = even_by if group % 2 == 0 else odd_by
        for point in range(points):
            pairs.append((group * points + point, group * points + (point + by) % points))
    return lax.ppermute(x, ("energy", "mom"), pairs)


def after(x, *results):
    return lax.optimization_barrier((x, *results))[0]


def even_group():
    return lax.rem(lax.axis_index("energy"), 2) == 0


def products(blocks, coupling):
    lefts = [
        jnp.dot(coupling, block, preferred_element_type=jnp.float32).astype(jnp.bfloat16)
        for block in blocks
    ]
    return [jnp.dot(left, coupling, preferred_element_type=jnp.float32) for left in lefts]


def load(place, even, part, back=0):
    first, second, at = place
    if first is second:
        return first[at - back, part]
    return jnp.where(even, first[at - back, part], second[at - back, part])


def terms(energy, offset, shift, coupling, phonon, slots, even):
    modes = coupling.shape[0]
    low, high = slots[energy - SMAX], slots[energy]
    sums = None
    for mode in range(modes):
        step = shift[mode, offset]
        if low[0] is high[0] and low[1] is high[1]:
            blocks = [load(high, even, part, step) for part in range(2)]
        else:
            blocks = [
                jnp.where(step > 0, load(low, even, part), load(high, even, part))
                for part in range(2)
            ]
        found = mode_terms(mode, offset, blocks, coupling, phonon)
        sums = found if sums is None else [x + y for x, y in zip(sums, found)]
    return sums


def mode_terms(mode, offset, blocks, coupling, phonon):
    size = coupling.shape[1]
    first, second = products(blocks, coupling[mode])
    real = phonon[offset, pl.ds(2 * mode * size, size), :].astype(jnp.float32)
    imag = phonon[offset, pl.ds((2 * mode + 1) * size, size), :].astype(jnp.float32)
    return [first * real - second * imag, first * imag + second * real]


def add_low(pair, sources, shift, coupling, phonon, even):
    for offset, place in sources:
        for mode in range(coupling.shape[0]):
            blocks = [load(place, even, part) for part in range(2)]
            found = mode_terms(mode, offset, blocks, coupling, phonon)
            step = shift[mode, offset]
            pair[step, 0] += found[0]
            pair[step, 1] += found[1]


def add_edges(pair, sources, shift, coupling, phonon, even):
    for offset, below, above in sources:
        for mode in range(coupling.shape[0]):
            step = shift[mode, offset]
            blocks = [
                jnp.where(step > 0, load(below, even, part), load(above, even, part))
                for part in range(2)
            ]
            found = mode_terms(mode, offset, blocks, coupling, phonon)
            pair[1 - step, 0] += found[0]
            pair[1 - step, 1] += found[1]


class Operands:
    def __init__(self):
        self.arrays = []

    def add(self, array):
        for n, other in enumerate(self.arrays):
            if other is array:
                return n
        self.arrays.append(array)
        return len(self.arrays) - 1

    def place(self, place):
        return (self.add(place[0]), self.add(place[1]), place[2])

    def slots(self, slots, energies):
        used = {slot for energy in energies for slot in (energy - SMAX, energy)}
        return {slot: self.place(slots[slot]) for slot in slots if slot in used}


def at_refs(refs, place):
    return (refs[place[0]], refs[place[1]], place[2])


def estimate(coupling, energies):
    modes, size, _ = coupling.shape
    flops = 128 * energies * modes * size**3
    return pl.CostEstimate(flops=flops, bytes_accessed=1 << 24, transcendentals=0)


def sums_call(energies, sources, args, like, dtype, raw=None):
    _, parts, size, _ = like.shape
    count = len(energies)
    operands = Operands()
    layout = [(offset, operands.slots(slots, energies)) for offset, slots in sources]
    source = operands.add(like) if raw is not None else None

    def kernel(shift, coupling, phonon, *refs):
        out = refs[-1]
        even = even_group()

        def sums():
            for at, energy in enumerate(energies):
                for n, (offset, slots) in enumerate(layout):
                    slots = {slot: at_refs(refs, place) for slot, place in slots.items()}
                    real, imag = terms(energy, offset, shift, coupling, phonon, slots, even)
                    if n > 0:
                        real, imag = real + out[at, 0], imag + out[at, 1]
                    out[at, 0] = real.astype(out.dtype)
                    out[at, 1] = imag.astype(out.dtype)

        if raw is None:
            sums()
        else:
            first, on_even = raw
            sends_raw = even if on_even else jnp.logical_not(even)

            @pl.when(sends_raw)
            def _():
                out[...] = refs[source][first : first + count]

            @pl.when(jnp.logical_not(sends_raw))
            def _():
                sums()

    return pl.pallas_call(
        kernel,
        out_shape=jax.ShapeDtypeStruct((count, parts, size, size), dtype),
        in_specs=[SMEM] + [VMEM] * (2 + len(operands.arrays)),
        out_specs=VMEM,
        compiler_params=pltpu.CompilerParams(vmem_limit_bytes=LIMIT),
        cost_estimate=estimate(args[1], count * len(sources)),
    )(*args, *operands.arrays)


def early_call(energies, offset, args, like):
    shift, coupling, phonon = args
    _, parts, size, _ = like.shape
    count, first = len(energies), energies[0] - SMAX

    def kernel(shift_hbm, coupling_hbm, phonon_hbm, own_hbm, out, *scratch):
        shift, coupling, phonon, own, sems = scratch
        pairs = [(own_hbm.at[pl.ds(first, count + SMAX)], own), (shift_hbm, shift)]
        pairs += [(coupling_hbm, coupling), (phonon_hbm.at[offset], phonon.at[offset])]
        copies = [pltpu.make_async_copy(*pair, sems.at[n]) for n, pair in enumerate(pairs)]
        even = even_group()
        copies[0].start()

        @pl.when(even)
        def _():
            copies[0].wait()
            out[...] = own[:count]

        @pl.when(jnp.logical_not(even))
        def _():
            for copy in copies[1:]:
                copy.start()
            for copy in copies:
                copy.wait()
            slots = {first + n: (own, own, n) for n in range(count + SMAX)}
            for at, energy in enumerate(energies):
                real, imag = terms(energy, offset, shift, coupling, phonon, slots, even)
                out[at, 0] = real.astype(out.dtype)
                out[at, 1] = imag.astype(out.dtype)

    return pl.pallas_call(
        kernel,
        out_shape=jax.ShapeDtypeStruct((count, parts, size, size), like.dtype),
        in_specs=[HBM] * 4,
        out_specs=VMEM,
        scratch_shapes=[
            pltpu.SMEM(shift.shape, shift.dtype),
            pltpu.VMEM(coupling.shape, coupling.dtype),
            pltpu.VMEM(phonon.shape, phonon.dtype),
            pltpu.VMEM((count + SMAX, parts, size, size), like.dtype),
            pltpu.SemaphoreType.DMA((4,)),
        ],
        compiler_params=pltpu.CompilerParams(vmem_limit_bytes=60 * 1024 * 1024),
        cost_estimate=estimate(coupling, count),
    )(shift, coupling, phonon, like)


def pair_call(pair, sources, args, add):
    operands = Operands()
    layout = [(offset, *[operands.place(place) for place in places]) for offset, *places in sources]

    def kernel(shift, coupling, phonon, pair_ref, *refs):
        out = refs[-1]
        out[...] = pair_ref[...]
        found = [(offset, *[at_refs(refs, p) for p in places]) for offset, *places in layout]
        add(out, found, shift, coupling, phonon, even_group())

    return pl.pallas_call(
        kernel,
        out_shape=jax.ShapeDtypeStruct(pair.shape, pair.dtype),
        in_specs=[SMEM] + [VMEM] * (len(args) + len(operands.arrays)),
        out_specs=VMEM,
        compiler_params=pltpu.CompilerParams(vmem_limit_bytes=LIMIT),
        cost_estimate=estimate(args[1], 1),
    )(*args, pair, *operands.arrays)


def add_call(energy, pair, pieces, out):
    _, parts, size, _ = out.shape
    arrays = [place[0] for place in pieces]

    def kernel(pair_ref, *refs):
        result = pair_ref[energy]
        for (_, _, at), ref in zip(pieces, refs):
            result = result + ref[at].astype(jnp.float32)
        refs[-1][0] = result.astype(out.dtype)

    return pl.pallas_call(
        kernel,
        grid=(1,),
        out_shape=jax.ShapeDtypeStruct(out.shape, out.dtype),
        in_specs=[VMEM] * (1 + len(arrays)) + [pl.BlockSpec(memory_space=pl.ANY)],
        out_specs=pl.BlockSpec((1, parts, size, size), lambda i: (i + energy, 0, 0, 0)),
        input_output_aliases={1 + len(arrays): 0},
        compiler_params=pltpu.CompilerParams(vmem_limit_bytes=LIMIT),
        cost_estimate=pl.CostEstimate(flops=1 << 33, bytes_accessed=1 << 24, transcendentals=0),
    )(pair, *arrays, out)


def finish_call(energies, whole, total, sources, pieces, args, out=None):
    _, parts, size, _ = whole
    operands = Operands()
    base = operands.add(total)
    layout = [(offset, operands.slots(slots, energies)) for offset, slots in sources]
    added = {energy: [operands.place(p) for p in pieces[energy]] for energy in energies}

    def kernel(*refs):
        shift, coupling, phonon = refs[: len(args)] if args else (None,) * 3
        refs = refs[len(args) :]
        even = even_group()
        for at, energy in enumerate(energies):

            @pl.when(pl.program_id(0) == at)
            def _():
                results = [refs[base][at, part] for part in range(2)]
                for offset, slots in layout:
                    slots = {slot: at_refs(refs, place) for slot, place in slots.items()}
                    found = terms(energy, offset, shift, coupling, phonon, slots, even)
                    results = [result + term for result, term in zip(results, found)]
                for part in range(2):
                    for place in added[energy]:
                        piece = load(at_refs(refs, place), even, part)
                        results[part] = results[part] + piece.astype(jnp.float32)
                    refs[-1][0, part] = results[part].astype(jnp.bfloat16)

    arrays = [*args, *operands.arrays]
    specs = [SMEM] * min(len(args), 1) + [VMEM] * (len(arrays) - min(len(args), 1))
    aliases = {}
    if out is not None:
        aliases = {len(arrays): 0}
        arrays.append(out)
        specs.append(pl.BlockSpec(memory_space=pl.ANY))
    first = energies[0]
    return pl.pallas_call(
        kernel,
        grid=(len(energies),),
        out_shape=jax.ShapeDtypeStruct(whole, jnp.bfloat16),
        in_specs=specs,
        out_specs=pl.BlockSpec((1, parts, size, size), lambda i: (i + first, 0, 0, 0)),
        input_output_aliases=aliases,
        compiler_params=pltpu.CompilerParams(vmem_limit_bytes=LIMIT),
        cost_estimate=pl.CostEstimate(flops=1 << 33, bytes_accessed=1 << 24, transcendentals=0),
    )(*arrays)


def body(green, coupling, phonon, shift):
    own = green[0, 0]
    whole = own.shape
    last = whole[0] - 1
    offsets = phonon.shape[0]
    radius = (offsets - 1) // 2
    ups = range(1, radius + 1)
    args = (shift.T, coupling, phonon)
    high = tuple(range(2, last + 1))

    def own_slots(block, below=None):
        slots = {energy: (block, block, energy) for energy in range(last + 1)}
        if below is not None:
            slots[-1] = (below, below, 0)
        return slots

    def send(energies, raw, *results, below=None, early=False):
        block = after(own, *results)
        made, arrived = {}, {}
        for q in ups:
            sources = [(radius - q, own_slots(block, below))]
            if early:
                made[q] = early_call(energies, radius - q, args, block)
            else:
                made[q] = sums_call(energies, sources, args, block, jnp.bfloat16, raw)
            ways = (-q, -q) if raw is None else (q, -q) if raw[1] else (-q, q)
            arrived[q] = passed_round(made[q], *ways)
        return list(made.values()), arrived

    own_top = own[last:]
    tops = {q: passed_round(own_top, q, q) for q in ups}
    made, high_1 = send(high, (1, True), own_top, early=True)
    below = passed_along(after(own_top, *made), "energy", 1)
    made, high_2 = send(high, (1, False), *made)
    block = after(own, *made)
    own_high = sums_call(high, [(radius, own_slots(block))], args, own, jnp.float32)
    pair = sums_call((0, 1), [(radius, own_slots(block, below))], args, own, jnp.float32)
    low = after(own, *made, *tops.values())[:1]
    lows = {q: passed_round(low, q, q) for q in ups}
    belows = {q: passed_along(after(tops[q], low), "energy", 1) for q in ups}
    made, second = send((1,), None, *made, low)
    made, first = send((0,), None, *made, *high_1.values(), below=below)

    sources = []
    pieces = {energy: [] for energy in range(last + 1)}
    for q in ups:
        slots = {slot: (high_1[q], high_2[q], slot - 1) for slot in range(1, last)}
        slots[last] = (tops[q], tops[q], 0)
        slots[-1] = (belows[q], belows[q], 0)
        sources.append((radius + q, slots))
        for energy in high:
            pieces[energy].append((high_2[q], high_1[q], energy - 2))
        pieces[1].append((second[q], second[q], 0))
        pieces[0].append((first[q], first[q], 0))
    out = finish_call(high, whole, own_high, sources, pieces, args)
    edges = [(offset, slots[-1], slots[1]) for offset, slots in sources]
    pair = pair_call(pair, edges, args, add_edges)
    lowest = [(offset, (lows[q], lows[q], 0)) for q, (offset, _) in zip(ups, sources)]
    pair = pair_call(pair, lowest, args, add_low)
    for energy in (1, 0):
        out = add_call(energy, pair, pieces[energy], out)
    return out[None, None]


def solution(mesh):
    placed = (P("mom", "energy", None, None, None, None), P(), P(), P())
    return jax.shard_map(
        body,
        mesh=mesh,
        in_specs=placed,
        out_specs=P("mom", "energy", None, None, None, None),
        check_vma=False,
    )
```

```python
import jax
import jax.numpy as jnp
from jax import lax
from jax.experimental import pallas as pl
from jax.experimental.pallas import tpu as pltpu
from jax.sharding import PartitionSpec as P

SMAX = 1
HBM = pl.BlockSpec(memory_space=pltpu.HBM)
VMEM = pl.BlockSpec(memory_space=pltpu.VMEM)
SMEM = pl.BlockSpec(memory_space=pltpu.SMEM)
LIMIT = 32 * 1024 * 1024


def passed_along(x, axis, by):
    length = lax.axis_size(axis)
    pairs = [(i, i + by) for i in range(length) if 0 <= i + by < length]
    return lax.ppermute(x, axis, pairs)


def passed_round(x, even_by, odd_by):
    groups, points = lax.axis_size("energy"), lax.axis_size("mom")
    pairs = []
    for group in range(groups):
        by = even_by if group % 2 == 0 else odd_by
        for point in range(points):
            pairs.append((group * points + point, group * points + (point + by) % points))
    return lax.ppermute(x, ("energy", "mom"), pairs)


def after(x, *results):
    return lax.optimization_barrier((x, *results))[0]


def even_group():
    return lax.rem(lax.axis_index("energy"), 2) == 0


def products(blocks, coupling):
    lefts = [
        jnp.dot(coupling, block, preferred_element_type=jnp.float32).astype(jnp.bfloat16)
        for block in blocks
    ]
    return [jnp.dot(left, coupling, preferred_element_type=jnp.float32) for left in lefts]


def load(place, even, part, back=0):
    first, second, at = place
    if first is second:
        return first[at - back, part]
    return jnp.where(even, first[at - back, part], second[at - back, part])


def terms(energy, offset, shift, coupling, phonon, slots, even):
    modes = coupling.shape[0]
    low, high = slots[energy - SMAX], slots[energy]
    sums = None
    for mode in range(modes):
        step = shift[mode, offset]
        if low[0] is high[0] and low[1] is high[1]:
            blocks = [load(high, even, part, step) for part in range(2)]
        else:
            blocks = [
                jnp.where(step > 0, load(low, even, part), load(high, even, part))
                for part in range(2)
            ]
        found = mode_terms(mode, offset, blocks, coupling, phonon)
        sums = found if sums is None else [x + y for x, y in zip(sums, found)]
    return sums


def mode_terms(mode, offset, blocks, coupling, phonon):
    size = coupling.shape[1]
    first, second = products(blocks, coupling[mode])
    real = phonon[offset, pl.ds(2 * mode * size, size), :].astype(jnp.float32)
    imag = phonon[offset, pl.ds((2 * mode + 1) * size, size), :].astype(jnp.float32)
    return [first * real - second * imag, first * imag + second * real]


def add_low(pair, sources, shift, coupling, phonon, even):
    for offset, place in sources:
        for mode in range(coupling.shape[0]):
            blocks = [load(place, even, part) for part in range(2)]
            found = mode_terms(mode, offset, blocks, coupling, phonon)
            step = shift[mode, offset]
            pair[step, 0] += found[0]
            pair[step, 1] += found[1]


def add_edges(pair, sources, shift, coupling, phonon, even):
    for offset, below, above in sources:
        for mode in range(coupling.shape[0]):
            step = shift[mode, offset]
            blocks = [
                jnp.where(step > 0, load(below, even, part), load(above, even, part))
                for part in range(2)
            ]
            found = mode_terms(mode, offset, blocks, coupling, phonon)
            pair[1 - step, 0] += found[0]
            pair[1 - step, 1] += found[1]


class Operands:
    def __init__(self):
        self.arrays = []

    def add(self, array):
        for n, other in enumerate(self.arrays):
            if other is array:
                return n
        self.arrays.append(array)
        return len(self.arrays) - 1

    def place(self, place):
        return (self.add(place[0]), self.add(place[1]), place[2])

    def slots(self, slots, energies):
        used = {slot for energy in energies for slot in (energy - SMAX, energy)}
        return {slot: self.place(slots[slot]) for slot in slots if slot in used}


def at_refs(refs, place):
    return (refs[place[0]], refs[place[1]], place[2])


def estimate(coupling, energies):
    modes, size, _ = coupling.shape
    flops = 128 * energies * modes * size**3
    return pl.CostEstimate(flops=flops, bytes_accessed=1 << 24, transcendentals=0)


def sums_call(energies, sources, args, like, dtype, raw=None):
    _, parts, size, _ = like.shape
    count = len(energies)
    operands = Operands()
    layout = [(offset, operands.slots(slots, energies)) for offset, slots in sources]
    source = operands.add(like) if raw is not None else None

    def kernel(shift, coupling, phonon, *refs):
        out = refs[-1]
        even = even_group()

        def sums():
            for at, energy in enumerate(energies):
                for n, (offset, slots) in enumerate(layout):
                    slots = {slot: at_refs(refs, place) for slot, place in slots.items()}
                    real, imag = terms(energy, offset, shift, coupling, phonon, slots, even)
                    if n > 0:
                        real, imag = real + out[at, 0], imag + out[at, 1]
                    out[at, 0] = real.astype(out.dtype)
                    out[at, 1] = imag.astype(out.dtype)

        if raw is None:
            sums()
        else:
            first, on_even = raw
            sends_raw = even if on_even else jnp.logical_not(even)

            @pl.when(sends_raw)
            def _():
                out[...] = refs[source][first : first + count]

            @pl.when(jnp.logical_not(sends_raw))
            def _():
                sums()

    return pl.pallas_call(
        kernel,
        out_shape=jax.ShapeDtypeStruct((count, parts, size, size), dtype),
        in_specs=[SMEM] + [VMEM] * (2 + len(operands.arrays)),
        out_specs=VMEM,
        compiler_params=pltpu.CompilerParams(vmem_limit_bytes=LIMIT),
        cost_estimate=estimate(args[1], count * len(sources)),
    )(*args, *operands.arrays)


def early_call(energies, offset, args, like):
    shift, coupling, phonon = args
    _, parts, size, _ = like.shape
    count, first = len(energies), energies[0] - SMAX

    def kernel(shift_hbm, coupling_hbm, phonon_hbm, own_hbm, out, *scratch):
        shift, coupling, phonon, own, sems = scratch
        pairs = [(own_hbm.at[pl.ds(first, count + SMAX)], own), (shift_hbm, shift)]
        pairs += [(coupling_hbm, coupling), (phonon_hbm.at[offset], phonon.at[offset])]
        copies = [pltpu.make_async_copy(*pair, sems.at[n]) for n, pair in enumerate(pairs)]
        even = even_group()
        copies[0].start()

        @pl.when(even)
        def _():
            copies[0].wait()
            out[...] = own[:count]

        @pl.when(jnp.logical_not(even))
        def _():
            for copy in copies[1:]:
                copy.start()
            for copy in copies:
                copy.wait()
            slots = {first + n: (own, own, n) for n in range(count + SMAX)}
            for at, energy in enumerate(energies):
                real, imag = terms(energy, offset, shift, coupling, phonon, slots, even)
                out[at, 0] = real.astype(out.dtype)
                out[at, 1] = imag.astype(out.dtype)

    return pl.pallas_call(
        kernel,
        out_shape=jax.ShapeDtypeStruct((count, parts, size, size), like.dtype),
        in_specs=[HBM] * 4,
        out_specs=VMEM,
        scratch_shapes=[
            pltpu.SMEM(shift.shape, shift.dtype),
            pltpu.VMEM(coupling.shape, coupling.dtype),
            pltpu.VMEM(phonon.shape, phonon.dtype),
            pltpu.VMEM((count + SMAX, parts, size, size), like.dtype),
            pltpu.SemaphoreType.DMA((4,)),
        ],
        compiler_params=pltpu.CompilerParams(vmem_limit_bytes=60 * 1024 * 1024),
        cost_estimate=estimate(coupling, count),
    )(shift, coupling, phonon, like)


def pair_call(pair, sources, args, add):
    operands = Operands()
    layout = [(offset, *[operands.place(place) for place in places]) for offset, *places in sources]

    def kernel(shift, coupling, phonon, pair_ref, *refs):
        out = refs[-1]
        out[...] = pair_ref[...]
        found = [(offset, *[at_refs(refs, p) for p in places]) for offset, *places in layout]
        add(out, found, shift, coupling, phonon, even_group())

    return pl.pallas_call(
        kernel,
        out_shape=jax.ShapeDtypeStruct(pair.shape, pair.dtype),
        in_specs=[SMEM] + [VMEM] * (len(args) + len(operands.arrays)),
        out_specs=VMEM,
        compiler_params=pltpu.CompilerParams(vmem_limit_bytes=LIMIT),
        cost_estimate=estimate(args[1], 1),
    )(*args, pair, *operands.arrays)


def add_call(energy, pair, pieces, out):
    _, parts, size, _ = out.shape
    arrays = [place[0] for place in pieces]

    def kernel(pair_ref, *refs):
        result = pair_ref[energy]
        for (_, _, at), ref in zip(pieces, refs):
            result = result + ref[at].astype(jnp.float32)
        refs[-1][0] = result.astype(out.dtype)

    return pl.pallas_call(
        kernel,
        grid=(1,),
        out_shape=jax.ShapeDtypeStruct(out.shape, out.dtype),
        in_specs=[VMEM] * (1 + len(arrays)) + [pl.BlockSpec(memory_space=pl.ANY)],
        out_specs=pl.BlockSpec((1, parts, size, size), lambda i: (i + energy, 0, 0, 0)),
        input_output_aliases={1 + len(arrays): 0},
        compiler_params=pltpu.CompilerParams(vmem_limit_bytes=LIMIT),
        cost_estimate=pl.CostEstimate(flops=1 << 33, bytes_accessed=1 << 24, transcendentals=0),
    )(pair, *arrays, out)


def finish_call(energies, whole, total, sources, pieces, args, out=None):
    _, parts, size, _ = whole
    operands = Operands()
    base = operands.add(total)
    layout = [(offset, operands.slots(slots, energies)) for offset, slots in sources]
    added = {energy: [operands.place(p) for p in pieces[energy]] for energy in energies}

    def kernel(*refs):
        shift, coupling, phonon = refs[: len(args)] if args else (None,) * 3
        refs = refs[len(args) :]
        even = even_group()
        for at, energy in enumerate(energies):

            @pl.when(pl.program_id(0) == at)
            def _():
                results = [refs[base][at, part] for part in range(2)]
                for offset, slots in layout:
                    slots = {slot: at_refs(refs, place) for slot, place in slots.items()}
                    found = terms(energy, offset, shift, coupling, phonon, slots, even)
                    results = [result + term for result, term in zip(results, found)]
                for part in range(2):
                    for place in added[energy]:
                        piece = load(at_refs(refs, place), even, part)
                        results[part] = results[part] + piece.astype(jnp.float32)
                    refs[-1][0, part] = results[part].astype(jnp.bfloat16)

    arrays = [*args, *operands.arrays]
    specs = [SMEM] * min(len(args), 1) + [VMEM] * (len(arrays) - min(len(args), 1))
    aliases = {}
    if out is not None:
        aliases = {len(arrays): 0}
        arrays.append(out)
        specs.append(pl.BlockSpec(memory_space=pl.ANY))
    first = energies[0]
    return pl.pallas_call(
        kernel,
        grid=(len(energies),),
        out_shape=jax.ShapeDtypeStruct(whole, jnp.bfloat16),
        in_specs=specs,
        out_specs=pl.BlockSpec((1, parts, size, size), lambda i: (i + first, 0, 0, 0)),
        input_output_aliases=aliases,
        compiler_params=pltpu.CompilerParams(vmem_limit_bytes=LIMIT),
        cost_estimate=pl.CostEstimate(flops=1 << 33, bytes_accessed=1 << 24, transcendentals=0),
    )(*arrays)


def body(green, coupling, phonon, shift):
    own = green[0, 0]
    whole = own.shape
    last = whole[0] - 1
    offsets = phonon.shape[0]
    radius = (offsets - 1) // 2
    ups = range(1, radius + 1)
    args = (shift.T, coupling, phonon)
    high = tuple(range(2, last + 1))

    def own_slots(block, below=None):
        slots = {energy: (block, block, energy) for energy in range(last + 1)}
        if below is not None:
            slots[-1] = (below, below, 0)
        return slots

    def send(energies, raw, *results, below=None, early=False):
        block = after(own, *results)
        made, arrived = {}, {}
        for q in ups:
            sources = [(radius - q, own_slots(block, below))]
            if early:
                made[q] = early_call(energies, radius - q, args, block)
            else:
                made[q] = sums_call(energies, sources, args, block, jnp.bfloat16, raw)
            ways = (-q, -q) if raw is None else (q, -q) if raw[1] else (-q, q)
            arrived[q] = passed_round(made[q], *ways)
        return list(made.values()), arrived

    own_top = own[last:]
    tops = {q: passed_round(own_top, q, q) for q in ups}
    made, high_1 = send(high, (1, True), own_top, early=True)
    below = passed_along(after(own_top, *made), "energy", 1)
    made, high_2 = send(high, (1, False), *made)
    block = after(own, *made)
    own_high = sums_call(high, [(radius, own_slots(block))], args, own, jnp.float32)
    pair = sums_call((0, 1), [(radius, own_slots(block, below))], args, own, jnp.float32)
    made, second = send((1,), None, *made, *tops.values())
    low = after(own, *made, *high_1.values())[:1]
    lows = {q: passed_round(low, q, q) for q in ups}
    belows = {q: passed_along(after(tops[q], low), "energy", 1) for q in ups}
    made, first = send((0,), None, *made, low, *high_2.values(), below=below)

    sources = []
    pieces = {energy: [] for energy in range(last + 1)}
    for q in ups:
        slots = {slot: (high_1[q], high_2[q], slot - 1) for slot in range(1, last)}
        slots[last] = (tops[q], tops[q], 0)
        slots[-1] = (belows[q], belows[q], 0)
        sources.append((radius + q, slots))
        for energy in high:
            pieces[energy].append((high_2[q], high_1[q], energy - 2))
        pieces[1].append((second[q], second[q], 0))
        pieces[0].append((first[q], first[q], 0))
    out = finish_call(high, whole, own_high, sources, pieces, args)
    edges = [(offset, slots[-1], slots[1]) for offset, slots in sources]
    pair = pair_call(pair, edges, args, add_edges)
    lowest = [(offset, (lows[q], lows[q], 0)) for q, (offset, _) in zip(ups, sources)]
    pair = pair_call(pair, lowest, args, add_low)
    for energy in (1, 0):
        out = add_call(energy, pair, pieces[energy], out)
    return out[None, None]


def solution(mesh):
    placed = (P("mom", "energy", None, None, None, None), P(), P(), P())
    return jax.shard_map(
        body,
        mesh=mesh,
        in_specs=placed,
        out_specs=P("mom", "energy", None, None, None, None),
        check_vma=False,
    )
```

```python
import jax
import jax.numpy as jnp
from jax import lax
from jax.experimental import pallas as pl
from jax.experimental.pallas import tpu as pltpu
from jax.sharding import PartitionSpec as P

SMAX = 1
HBM = pl.BlockSpec(memory_space=pltpu.HBM)
VMEM = pl.BlockSpec(memory_space=pltpu.VMEM)
SMEM = pl.BlockSpec(memory_space=pltpu.SMEM)
LIMIT = 32 * 1024 * 1024


def passed_along(x, axis, by):
    length = lax.axis_size(axis)
    pairs = [(i, i + by) for i in range(length) if 0 <= i + by < length]
    return lax.ppermute(x, axis, pairs)


def passed_round(x, even_by, odd_by):
    groups, points = lax.axis_size("energy"), lax.axis_size("mom")
    pairs = []
    for group in range(groups):
        by = even_by if group % 2 == 0 else odd_by
        for point in range(points):
            pairs.append((group * points + point, group * points + (point + by) % points))
    return lax.ppermute(x, ("energy", "mom"), pairs)


def after(x, *results):
    return lax.optimization_barrier((x, *results))[0]


def even_group():
    return lax.rem(lax.axis_index("energy"), 2) == 0


def products(blocks, coupling):
    lefts = [
        jnp.dot(coupling, block, preferred_element_type=jnp.float32).astype(jnp.bfloat16)
        for block in blocks
    ]
    return [jnp.dot(left, coupling, preferred_element_type=jnp.float32) for left in lefts]


def load(place, even, part, back=0):
    first, second, at = place
    if first is second:
        return first[at - back, part]
    return jnp.where(even, first[at - back, part], second[at - back, part])


def terms(energy, offset, shift, coupling, phonon, slots, even):
    modes = coupling.shape[0]
    low, high = slots[energy - SMAX], slots[energy]
    sums = None
    for mode in range(modes):
        step = shift[mode, offset]
        if low[0] is high[0] and low[1] is high[1]:
            blocks = [load(high, even, part, step) for part in range(2)]
        else:
            blocks = [
                jnp.where(step > 0, load(low, even, part), load(high, even, part))
                for part in range(2)
            ]
        found = mode_terms(mode, offset, blocks, coupling, phonon)
        sums = found if sums is None else [x + y for x, y in zip(sums, found)]
    return sums


def mode_terms(mode, offset, blocks, coupling, phonon):
    size = coupling.shape[1]
    first, second = products(blocks, coupling[mode])
    real = phonon[offset, pl.ds(2 * mode * size, size), :].astype(jnp.float32)
    imag = phonon[offset, pl.ds((2 * mode + 1) * size, size), :].astype(jnp.float32)
    return [first * real - second * imag, first * imag + second * real]


def add_low(pair, sources, shift, coupling, phonon, even):
    for offset, place in sources:
        for mode in range(coupling.shape[0]):
            blocks = [load(place, even, part) for part in range(2)]
            found = mode_terms(mode, offset, blocks, coupling, phonon)
            step = shift[mode, offset]
            pair[step, 0] += found[0]
            pair[step, 1] += found[1]


def add_edges(pair, sources, shift, coupling, phonon, even):
    for offset, below, above in sources:
        for mode in range(coupling.shape[0]):
            step = shift[mode, offset]
            blocks = [
                jnp.where(step > 0, load(below, even, part), load(above, even, part))
                for part in range(2)
            ]
            found = mode_terms(mode, offset, blocks, coupling, phonon)
            pair[1 - step, 0] += found[0]
            pair[1 - step, 1] += found[1]


class Operands:
    def __init__(self):
        self.arrays = []

    def add(self, array):
        for n, other in enumerate(self.arrays):
            if other is array:
                return n
        self.arrays.append(array)
        return len(self.arrays) - 1

    def place(self, place):
        return (self.add(place[0]), self.add(place[1]), place[2])

    def slots(self, slots, energies):
        used = {slot for energy in energies for slot in (energy - SMAX, energy)}
        return {slot: self.place(slots[slot]) for slot in slots if slot in used}


def at_refs(refs, place):
    return (refs[place[0]], refs[place[1]], place[2])


def estimate(coupling, energies):
    modes, size, _ = coupling.shape
    flops = 128 * energies * modes * size**3
    return pl.CostEstimate(flops=flops, bytes_accessed=1 << 24, transcendentals=0)


def sums_call(energies, sources, args, like, dtype, raw=None):
    _, parts, size, _ = like.shape
    count = len(energies)
    operands = Operands()
    layout = [(offset, operands.slots(slots, energies)) for offset, slots in sources]
    source = operands.add(like) if raw is not None else None

    def kernel(shift, coupling, phonon, *refs):
        out = refs[-1]
        even = even_group()

        def sums():
            for at, energy in enumerate(energies):
                for n, (offset, slots) in enumerate(layout):
                    slots = {slot: at_refs(refs, place) for slot, place in slots.items()}
                    real, imag = terms(energy, offset, shift, coupling, phonon, slots, even)
                    if n > 0:
                        real, imag = real + out[at, 0], imag + out[at, 1]
                    out[at, 0] = real.astype(out.dtype)
                    out[at, 1] = imag.astype(out.dtype)

        if raw is None:
            sums()
        else:
            first, on_even = raw
            sends_raw = even if on_even else jnp.logical_not(even)

            @pl.when(sends_raw)
            def _():
                out[...] = refs[source][first : first + count]

            @pl.when(jnp.logical_not(sends_raw))
            def _():
                sums()

    return pl.pallas_call(
        kernel,
        out_shape=jax.ShapeDtypeStruct((count, parts, size, size), dtype),
        in_specs=[SMEM] + [VMEM] * (2 + len(operands.arrays)),
        out_specs=VMEM,
        compiler_params=pltpu.CompilerParams(vmem_limit_bytes=LIMIT),
        cost_estimate=estimate(args[1], count * len(sources)),
    )(*args, *operands.arrays)


def early_call(energies, offset, args, like):
    shift, coupling, phonon = args
    _, parts, size, _ = like.shape
    count, first = len(energies), energies[0] - SMAX

    def kernel(shift_hbm, coupling_hbm, phonon_hbm, own_hbm, out, *scratch):
        shift, coupling, phonon, own, sems = scratch
        pairs = [(own_hbm.at[pl.ds(first, count + SMAX)], own), (shift_hbm, shift)]
        pairs += [(coupling_hbm, coupling), (phonon_hbm.at[offset], phonon.at[offset])]
        copies = [pltpu.make_async_copy(*pair, sems.at[n]) for n, pair in enumerate(pairs)]
        even = even_group()
        copies[0].start()

        @pl.when(even)
        def _():
            copies[0].wait()
            out[...] = own[:count]

        @pl.when(jnp.logical_not(even))
        def _():
            for copy in copies[1:]:
                copy.start()
            for copy in copies:
                copy.wait()
            slots = {first + n: (own, own, n) for n in range(count + SMAX)}
            for at, energy in enumerate(energies):
                real, imag = terms(energy, offset, shift, coupling, phonon, slots, even)
                out[at, 0] = real.astype(out.dtype)
                out[at, 1] = imag.astype(out.dtype)

    return pl.pallas_call(
        kernel,
        out_shape=jax.ShapeDtypeStruct((count, parts, size, size), like.dtype),
        in_specs=[HBM] * 4,
        out_specs=VMEM,
        scratch_shapes=[
            pltpu.SMEM(shift.shape, shift.dtype),
            pltpu.VMEM(coupling.shape, coupling.dtype),
            pltpu.VMEM(phonon.shape, phonon.dtype),
            pltpu.VMEM((count + SMAX, parts, size, size), like.dtype),
            pltpu.SemaphoreType.DMA((4,)),
        ],
        compiler_params=pltpu.CompilerParams(vmem_limit_bytes=60 * 1024 * 1024),
        cost_estimate=estimate(coupling, count),
    )(shift, coupling, phonon, like)


def pair_call(pair, sources, args, add):
    operands = Operands()
    layout = [(offset, *[operands.place(place) for place in places]) for offset, *places in sources]

    def kernel(shift, coupling, phonon, pair_ref, *refs):
        out = refs[-1]
        out[...] = pair_ref[...]
        found = [(offset, *[at_refs(refs, p) for p in places]) for offset, *places in layout]
        add(out, found, shift, coupling, phonon, even_group())

    return pl.pallas_call(
        kernel,
        out_shape=jax.ShapeDtypeStruct(pair.shape, pair.dtype),
        in_specs=[SMEM] + [VMEM] * (len(args) + len(operands.arrays)),
        out_specs=VMEM,
        compiler_params=pltpu.CompilerParams(vmem_limit_bytes=LIMIT),
        cost_estimate=estimate(args[1], 1),
    )(*args, pair, *operands.arrays)


def add_call(energy, pair, pieces, out):
    _, parts, size, _ = out.shape
    arrays = [place[0] for place in pieces]

    def kernel(pair_ref, *refs):
        result = pair_ref[energy]
        for (_, _, at), ref in zip(pieces, refs):
            result = result + ref[at].astype(jnp.float32)
        refs[-1][0] = result.astype(out.dtype)

    return pl.pallas_call(
        kernel,
        grid=(1,),
        out_shape=jax.ShapeDtypeStruct(out.shape, out.dtype),
        in_specs=[VMEM] * (1 + len(arrays)) + [pl.BlockSpec(memory_space=pl.ANY)],
        out_specs=pl.BlockSpec((1, parts, size, size), lambda i: (i + energy, 0, 0, 0)),
        input_output_aliases={1 + len(arrays): 0},
        compiler_params=pltpu.CompilerParams(vmem_limit_bytes=LIMIT),
        cost_estimate=pl.CostEstimate(flops=1 << 33, bytes_accessed=1 << 24, transcendentals=0),
    )(pair, *arrays, out)


def finish_call(energies, whole, total, sources, pieces, args, out=None):
    _, parts, size, _ = whole
    operands = Operands()
    base = operands.add(total)
    layout = [(offset, operands.slots(slots, energies)) for offset, slots in sources]
    added = {energy: [operands.place(p) for p in pieces[energy]] for energy in energies}

    def kernel(*refs):
        shift, coupling, phonon = refs[: len(args)] if args else (None,) * 3
        refs = refs[len(args) :]
        even = even_group()
        for at, energy in enumerate(energies):

            @pl.when(pl.program_id(0) == at)
            def _():
                results = [refs[base][at, part] for part in range(2)]
                for offset, slots in layout:
                    slots = {slot: at_refs(refs, place) for slot, place in slots.items()}
                    found = terms(energy, offset, shift, coupling, phonon, slots, even)
                    results = [result + term for result, term in zip(results, found)]
                for part in range(2):
                    for place in added[energy]:
                        piece = load(at_refs(refs, place), even, part)
                        results[part] = results[part] + piece.astype(jnp.float32)
                    refs[-1][0, part] = results[part].astype(jnp.bfloat16)

    arrays = [*args, *operands.arrays]
    specs = [SMEM] * min(len(args), 1) + [VMEM] * (len(arrays) - min(len(args), 1))
    aliases = {}
    if out is not None:
        aliases = {len(arrays): 0}
        arrays.append(out)
        specs.append(pl.BlockSpec(memory_space=pl.ANY))
    first = energies[0]
    return pl.pallas_call(
        kernel,
        grid=(len(energies),),
        out_shape=jax.ShapeDtypeStruct(whole, jnp.bfloat16),
        in_specs=specs,
        out_specs=pl.BlockSpec((1, parts, size, size), lambda i: (i + first, 0, 0, 0)),
        input_output_aliases=aliases,
        compiler_params=pltpu.CompilerParams(vmem_limit_bytes=LIMIT),
        cost_estimate=pl.CostEstimate(flops=1 << 33, bytes_accessed=1 << 24, transcendentals=0),
    )(*arrays)


def body(green, coupling, phonon, shift):
    own = green[0, 0]
    whole = own.shape
    last = whole[0] - 1
    offsets = phonon.shape[0]
    radius = (offsets - 1) // 2
    ups = range(1, radius + 1)
    args = (shift.T, coupling, phonon)
    high = tuple(range(2, last + 1))

    def own_slots(block, below=None):
        slots = {energy: (block, block, energy) for energy in range(last + 1)}
        if below is not None:
            slots[-1] = (below, below, 0)
        return slots

    def send(energies, raw, *results, below=None, early=False):
        block = after(own, *results)
        made, arrived = {}, {}
        for q in ups:
            sources = [(radius - q, own_slots(block, below))]
            if early:
                made[q] = early_call(energies, radius - q, args, block)
            else:
                made[q] = sums_call(energies, sources, args, block, jnp.bfloat16, raw)
            ways = (-q, -q) if raw is None else (q, -q) if raw[1] else (-q, q)
            arrived[q] = passed_round(made[q], *ways)
        return list(made.values()), arrived

    own_top = own[last:]
    tops = {q: passed_round(own_top, q, q) for q in ups}
    made, high_1 = send(high, (1, True), own_top, early=True)
    made, high_2 = send(high, (1, False), *made)
    below = passed_along(after(own_top, *made), "energy", 1)
    block = after(own, *made)
    own_high = sums_call(high, [(radius, own_slots(block))], args, own, jnp.float32)
    pair = sums_call((0, 1), [(radius, own_slots(block, below))], args, own, jnp.float32)
    low = after(own, *made, *tops.values())[:1]
    lows = {q: passed_round(low, q, q) for q in ups}
    belows = {q: passed_along(after(tops[q], low), "energy", 1) for q in ups}
    made, second = send((1,), None, *made, low, *high_1.values())
    made, first = send((0,), None, *made, *high_2.values(), below=below)

    sources = []
    pieces = {energy: [] for energy in range(last + 1)}
    for q in ups:
        slots = {slot: (high_1[q], high_2[q], slot - 1) for slot in range(1, last)}
        slots[last] = (tops[q], tops[q], 0)
        slots[-1] = (belows[q], belows[q], 0)
        sources.append((radius + q, slots))
        for energy in high:
            pieces[energy].append((high_2[q], high_1[q], energy - 2))
        pieces[1].append((second[q], second[q], 0))
        pieces[0].append((first[q], first[q], 0))
    out = finish_call(high, whole, own_high, sources, pieces, args)
    edges = [(offset, slots[-1], slots[1]) for offset, slots in sources]
    pair = pair_call(pair, edges, args, add_edges)
    lowest = [(offset, (lows[q], lows[q], 0)) for q, (offset, _) in zip(ups, sources)]
    pair = pair_call(pair, lowest, args, add_low)
    for energy in (1, 0):
        out = add_call(energy, pair, pieces[energy], out)
    return out[None, None]


def solution(mesh):
    placed = (P("mom", "energy", None, None, None, None), P(), P(), P())
    return jax.shard_map(
        body,
        mesh=mesh,
        in_specs=placed,
        out_specs=P("mom", "energy", None, None, None, None),
        check_vma=False,
    )
```

```python
import jax
import jax.numpy as jnp
from jax import lax
from jax.experimental import pallas as pl
from jax.experimental.pallas import tpu as pltpu
from jax.sharding import PartitionSpec as P

SMAX = 1
HBM = pl.BlockSpec(memory_space=pltpu.HBM)
VMEM = pl.BlockSpec(memory_space=pltpu.VMEM)
SMEM = pl.BlockSpec(memory_space=pltpu.SMEM)
LIMIT = 32 * 1024 * 1024


def passed_along(x, axis, by):
    length = lax.axis_size(axis)
    pairs = [(i, i + by) for i in range(length) if 0 <= i + by < length]
    return lax.ppermute(x, axis, pairs)


def passed_round(x, even_by, odd_by):
    groups, points = lax.axis_size("energy"), lax.axis_size("mom")
    pairs = []
    for group in range(groups):
        by = even_by if group % 2 == 0 else odd_by
        for point in range(points):
            pairs.append((group * points + point, group * points + (point + by) % points))
    return lax.ppermute(x, ("energy", "mom"), pairs)


def after(x, *results):
    return lax.optimization_barrier((x, *results))[0]


def even_group():
    return lax.rem(lax.axis_index("energy"), 2) == 0


def products(blocks, coupling):
    lefts = [
        jnp.dot(coupling, block, preferred_element_type=jnp.float32).astype(jnp.bfloat16)
        for block in blocks
    ]
    return [jnp.dot(left, coupling, preferred_element_type=jnp.float32) for left in lefts]


def load(place, even, part, back=0):
    first, second, at = place
    if first is second:
        return first[at - back, part]
    return jnp.where(even, first[at - back, part], second[at - back, part])


def terms(energy, offset, shift, coupling, phonon, slots, even):
    modes = coupling.shape[0]
    low, high = slots[energy - SMAX], slots[energy]
    sums = None
    for mode in range(modes):
        step = shift[mode, offset]
        if low[0] is high[0] and low[1] is high[1]:
            blocks = [load(high, even, part, step) for part in range(2)]
        else:
            blocks = [
                jnp.where(step > 0, load(low, even, part), load(high, even, part))
                for part in range(2)
            ]
        found = mode_terms(mode, offset, blocks, coupling, phonon)
        sums = found if sums is None else [x + y for x, y in zip(sums, found)]
    return sums


def mode_terms(mode, offset, blocks, coupling, phonon):
    size = coupling.shape[1]
    first, second = products(blocks, coupling[mode])
    real = phonon[offset, pl.ds(2 * mode * size, size), :].astype(jnp.float32)
    imag = phonon[offset, pl.ds((2 * mode + 1) * size, size), :].astype(jnp.float32)
    return [first * real - second * imag, first * imag + second * real]


def add_low(pair, sources, shift, coupling, phonon, even):
    for offset, place in sources:
        for mode in range(coupling.shape[0]):
            blocks = [load(place, even, part) for part in range(2)]
            found = mode_terms(mode, offset, blocks, coupling, phonon)
            step = shift[mode, offset]
            pair[step, 0] += found[0]
            pair[step, 1] += found[1]


def add_edges(pair, sources, shift, coupling, phonon, even):
    for offset, below, above in sources:
        for mode in range(coupling.shape[0]):
            step = shift[mode, offset]
            blocks = [
                jnp.where(step > 0, load(below, even, part), load(above, even, part))
                for part in range(2)
            ]
            found = mode_terms(mode, offset, blocks, coupling, phonon)
            pair[1 - step, 0] += found[0]
            pair[1 - step, 1] += found[1]


class Operands:
    def __init__(self):
        self.arrays = []

    def add(self, array):
        for n, other in enumerate(self.arrays):
            if other is array:
                return n
        self.arrays.append(array)
        return len(self.arrays) - 1

    def place(self, place):
        return (self.add(place[0]), self.add(place[1]), place[2])

    def slots(self, slots, energies):
        used = {slot for energy in energies for slot in (energy - SMAX, energy)}
        return {slot: self.place(slots[slot]) for slot in slots if slot in used}


def at_refs(refs, place):
    return (refs[place[0]], refs[place[1]], place[2])


def estimate(coupling, energies):
    modes, size, _ = coupling.shape
    flops = 128 * energies * modes * size**3
    return pl.CostEstimate(flops=flops, bytes_accessed=1 << 24, transcendentals=0)


def sums_call(energies, sources, args, like, dtype, raw=None):
    _, parts, size, _ = like.shape
    count = len(energies)
    operands = Operands()
    layout = [(offset, operands.slots(slots, energies)) for offset, slots in sources]
    source = operands.add(like) if raw is not None else None

    def kernel(shift, coupling, phonon, *refs):
        out = refs[-1]
        even = even_group()

        def sums():
            for at, energy in enumerate(energies):
                for n, (offset, slots) in enumerate(layout):
                    slots = {slot: at_refs(refs, place) for slot, place in slots.items()}
                    real, imag = terms(energy, offset, shift, coupling, phonon, slots, even)
                    if n > 0:
                        real, imag = real + out[at, 0], imag + out[at, 1]
                    out[at, 0] = real.astype(out.dtype)
                    out[at, 1] = imag.astype(out.dtype)

        if raw is None:
            sums()
        else:
            first, on_even = raw
            sends_raw = even if on_even else jnp.logical_not(even)

            @pl.when(sends_raw)
            def _():
                out[...] = refs[source][first : first + count]

            @pl.when(jnp.logical_not(sends_raw))
            def _():
                sums()

    return pl.pallas_call(
        kernel,
        out_shape=jax.ShapeDtypeStruct((count, parts, size, size), dtype),
        in_specs=[SMEM] + [VMEM] * (2 + len(operands.arrays)),
        out_specs=VMEM,
        compiler_params=pltpu.CompilerParams(vmem_limit_bytes=LIMIT),
        cost_estimate=estimate(args[1], count * len(sources)),
    )(*args, *operands.arrays)


def early_call(energies, offset, args, like):
    shift, coupling, phonon = args
    _, parts, size, _ = like.shape
    count, first = len(energies), energies[0] - SMAX

    def kernel(shift_hbm, coupling_hbm, phonon_hbm, own_hbm, out, *scratch):
        shift, coupling, phonon, own, sems = scratch
        pairs = [(own_hbm.at[pl.ds(first, count + SMAX)], own), (shift_hbm, shift)]
        pairs += [(coupling_hbm, coupling), (phonon_hbm.at[offset], phonon.at[offset])]
        copies = [pltpu.make_async_copy(*pair, sems.at[n]) for n, pair in enumerate(pairs)]
        even = even_group()
        copies[0].start()

        @pl.when(even)
        def _():
            copies[0].wait()
            out[...] = own[:count]

        @pl.when(jnp.logical_not(even))
        def _():
            for copy in copies[1:]:
                copy.start()
            for copy in copies:
                copy.wait()
            slots = {first + n: (own, own, n) for n in range(count + SMAX)}
            for at, energy in enumerate(energies):
                real, imag = terms(energy, offset, shift, coupling, phonon, slots, even)
                out[at, 0] = real.astype(out.dtype)
                out[at, 1] = imag.astype(out.dtype)

    return pl.pallas_call(
        kernel,
        out_shape=jax.ShapeDtypeStruct((count, parts, size, size), like.dtype),
        in_specs=[HBM] * 4,
        out_specs=VMEM,
        scratch_shapes=[
            pltpu.SMEM(shift.shape, shift.dtype),
            pltpu.VMEM(coupling.shape, coupling.dtype),
            pltpu.VMEM(phonon.shape, phonon.dtype),
            pltpu.VMEM((count + SMAX, parts, size, size), like.dtype),
            pltpu.SemaphoreType.DMA((4,)),
        ],
        compiler_params=pltpu.CompilerParams(vmem_limit_bytes=60 * 1024 * 1024),
        cost_estimate=estimate(coupling, count),
    )(shift, coupling, phonon, like)


def pair_call(pair, sources, args, add):
    operands = Operands()
    layout = [(offset, *[operands.place(place) for place in places]) for offset, *places in sources]

    def kernel(shift, coupling, phonon, pair_ref, *refs):
        out = refs[-1]
        out[...] = pair_ref[...]
        found = [(offset, *[at_refs(refs, p) for p in places]) for offset, *places in layout]
        add(out, found, shift, coupling, phonon, even_group())

    return pl.pallas_call(
        kernel,
        out_shape=jax.ShapeDtypeStruct(pair.shape, pair.dtype),
        in_specs=[SMEM] + [VMEM] * (len(args) + len(operands.arrays)),
        out_specs=VMEM,
        compiler_params=pltpu.CompilerParams(vmem_limit_bytes=LIMIT),
        cost_estimate=estimate(args[1], 1),
    )(*args, pair, *operands.arrays)


def add_call(energy, pair, pieces, out):
    _, parts, size, _ = out.shape
    arrays = [place[0] for place in pieces]

    def kernel(pair_ref, *refs):
        result = pair_ref[energy]
        for (_, _, at), ref in zip(pieces, refs):
            result = result + ref[at].astype(jnp.float32)
        refs[-1][0] = result.astype(out.dtype)

    return pl.pallas_call(
        kernel,
        grid=(1,),
        out_shape=jax.ShapeDtypeStruct(out.shape, out.dtype),
        in_specs=[VMEM] * (1 + len(arrays)) + [pl.BlockSpec(memory_space=pl.ANY)],
        out_specs=pl.BlockSpec((1, parts, size, size), lambda i: (i + energy, 0, 0, 0)),
        input_output_aliases={1 + len(arrays): 0},
        compiler_params=pltpu.CompilerParams(vmem_limit_bytes=LIMIT),
        cost_estimate=pl.CostEstimate(flops=1 << 33, bytes_accessed=1 << 24, transcendentals=0),
    )(pair, *arrays, out)


def top_call(own, limit):
    last = own.shape[0] - 1

    def kernel(own_ref, out_ref, sem):
        copy = pltpu.make_async_copy(own_ref.at[pl.ds(last, 1)], out_ref, sem)
        copy.start()
        copy.wait()

    return pl.pallas_call(
        kernel,
        out_shape=jax.ShapeDtypeStruct((1,) + own.shape[1:], own.dtype),
        in_specs=[HBM],
        out_specs=VMEM,
        scratch_shapes=[pltpu.SemaphoreType.DMA],
        compiler_params=pltpu.CompilerParams(vmem_limit_bytes=limit),
        cost_estimate=pl.CostEstimate(flops=0, bytes_accessed=1 << 20, transcendentals=0),
    )(own)


def finish_call(energies, whole, total, sources, pieces, args, out=None):
    _, parts, size, _ = whole
    operands = Operands()
    base = operands.add(total)
    layout = [(offset, operands.slots(slots, energies)) for offset, slots in sources]
    added = {energy: [operands.place(p) for p in pieces[energy]] for energy in energies}

    def kernel(*refs):
        shift, coupling, phonon = refs[: len(args)] if args else (None,) * 3
        refs = refs[len(args) :]
        even = even_group()
        for at, energy in enumerate(energies):

            @pl.when(pl.program_id(0) == at)
            def _():
                results = [refs[base][at, part] for part in range(2)]
                for offset, slots in layout:
                    slots = {slot: at_refs(refs, place) for slot, place in slots.items()}
                    found = terms(energy, offset, shift, coupling, phonon, slots, even)
                    results = [result + term for result, term in zip(results, found)]
                for part in range(2):
                    for place in added[energy]:
                        piece = load(at_refs(refs, place), even, part)
                        results[part] = results[part] + piece.astype(jnp.float32)
                    refs[-1][0, part] = results[part].astype(jnp.bfloat16)

    arrays = [*args, *operands.arrays]
    specs = [SMEM] * min(len(args), 1) + [VMEM] * (len(arrays) - min(len(args), 1))
    aliases = {}
    if out is not None:
        aliases = {len(arrays): 0}
        arrays.append(out)
        specs.append(pl.BlockSpec(memory_space=pl.ANY))
    first = energies[0]
    return pl.pallas_call(
        kernel,
        grid=(len(energies),),
        out_shape=jax.ShapeDtypeStruct(whole, jnp.bfloat16),
        in_specs=specs,
        out_specs=pl.BlockSpec((1, parts, size, size), lambda i: (i + first, 0, 0, 0)),
        input_output_aliases=aliases,
        compiler_params=pltpu.CompilerParams(vmem_limit_bytes=LIMIT),
        cost_estimate=pl.CostEstimate(flops=1 << 33, bytes_accessed=1 << 24, transcendentals=0),
    )(*arrays)


def body(green, coupling, phonon, shift):
    own = green[0, 0]
    whole = own.shape
    last = whole[0] - 1
    offsets = phonon.shape[0]
    radius = (offsets - 1) // 2
    ups = range(1, radius + 1)
    args = (shift.T, coupling, phonon)
    high = tuple(range(2, last + 1))

    def own_slots(block, below=None):
        slots = {energy: (block, block, energy) for energy in range(last + 1)}
        if below is not None:
            slots[-1] = (below, below, 0)
        return slots

    def send(energies, raw, *results, below=None, early=False):
        block = after(own, *results)
        made, arrived = {}, {}
        for q in ups:
            sources = [(radius - q, own_slots(block, below))]
            if early:
                made[q] = early_call(energies, radius - q, args, block)
            else:
                made[q] = sums_call(energies, sources, args, block, jnp.bfloat16, raw)
            ways = (-q, -q) if raw is None else (q, -q) if raw[1] else (-q, q)
            arrived[q] = passed_round(made[q], *ways)
        return list(made.values()), arrived

    own_top = top_call(own, 53 * 1024 * 1024)
    tops = {q: passed_round(own_top, q, q) for q in ups}
    made, high_1 = send(high, (1, True), own_top, early=True)
    made, high_2 = send(high, (1, False), *made)
    below = passed_along(after(own_top, *made), "energy", 1)
    block = after(own, *made)
    own_high = sums_call(high, [(radius, own_slots(block))], args, own, jnp.float32)
    pair = sums_call((0, 1), [(radius, own_slots(block, below))], args, own, jnp.float32)
    low = after(own, *made, *tops.values())[:1]
    lows = {q: passed_round(low, q, q) for q in ups}
    belows = {q: passed_along(after(tops[q], low), "energy", 1) for q in ups}
    made, second = send((1,), None, *made, low, *high_1.values())
    made, first = send((0,), None, *made, *high_2.values(), below=below)

    sources = []
    pieces = {energy: [] for energy in range(last + 1)}
    for q in ups:
        slots = {slot: (high_1[q], high_2[q], slot - 1) for slot in range(1, last)}
        slots[last] = (tops[q], tops[q], 0)
        slots[-1] = (belows[q], belows[q], 0)
        sources.append((radius + q, slots))
        for energy in high:
            pieces[energy].append((high_2[q], high_1[q], energy - 2))
        pieces[1].append((second[q], second[q], 0))
        pieces[0].append((first[q], first[q], 0))
    out = finish_call(high, whole, own_high, sources, pieces, args)
    edges = [(offset, slots[-1], slots[1]) for offset, slots in sources]
    pair = pair_call(pair, edges, args, add_edges)
    lowest = [(offset, (lows[q], lows[q], 0)) for q, (offset, _) in zip(ups, sources)]
    pair = pair_call(pair, lowest, args, add_low)
    for energy in (1, 0):
        out = add_call(energy, pair, pieces[energy], out)
    return out[None, None]


def solution(mesh):
    placed = (P("mom", "energy", None, None, None, None), P(), P(), P())
    return jax.shard_map(
        body,
        mesh=mesh,
        in_specs=placed,
        out_specs=P("mom", "energy", None, None, None, None),
        check_vma=False,
    )
```
